32 devices in a mesh: lat: 2 (over x), lon: 16 (over z, y, core).
Axes of the slice: x: 2, y: 2, z: 4, core: 2. Of those that a mesh axis runs over, the one named last changes fastest.
Arguments:
- tracer: float32 [4, 512, 2048], P(None, 'lat', 'lon'), may hold values from -6 to 6
- wind_east: float32 [4, 512, 2048], P(None, 'lat', 'lon'), may hold values from -4 to 4
- wind_north: float32 [4, 512, 2048], P(None, 'lat', 'lon'), may hold values from -4 to 4
- kappa: float32 [4, 512, 2048], P(None, 'lat', 'lon'), may hold values from 0.25 to 4
- cutoff: int32 [128], replicated, may hold values from 64 to 511
- partner: int32 [2048], replicated, may hold values from 0 to 2047, as said below
Outputs:
- filtered: float32 [4, 512, 2048], P(None, 'lat', 'lon')
- balanced: float32 [4, 512, 2048], P(None, 'lat', 'lon')
The draws below stay inside these ranges and needn't reach their ends.
Inputs may be any that keep to these rules, and one draw needn't show every extreme that they name: partner[j] = (j + 1024 + s_j) mod 2048 with each column's own shift s_j of 0 to 127; some column has s_j = 127.
All inputs are finite; a program needn't handle non-finite values.
Results may differ from the reference program's by a relative error of at most 0.00005.
Values sent between devices are 32-bit elements; how exact they have to be, the bound alone decides.
A program may use at most 64 MiB of HBM per device.

```python
import math
import jax
import jax.numpy as jnp

CLON = 128
LEV = 4
POLE = 64
KMAX = 512
SWEEPS = 4
NLON = 2048
NLAT = 512


def draw_partner(key, part):
    shifts = jax.random.randint(jax.random.fold_in(key, 7), (NLON,), 0, CLON, dtype=jnp.int32)
    shifts = shifts.at[NLON // 2 - 1].set(0)
    shifts = shifts.at[NLON // 2].set(0)
    shifts = shifts.at[1].set(CLON - 1)
    columns = jnp.arange(NLON, dtype=jnp.int32)
    return ((columns + NLON // 2 + shifts) % NLON).astype(jnp.int32)


def draw_cutoff(key, part):
    lowest = KMAX // 8
    values = jax.random.randint(jax.random.fold_in(key, 1), (2 * POLE,), lowest, KMAX, dtype=jnp.int32)
    first = jax.random.randint(jax.random.fold_in(key, 2), (), 0, 2 * POLE, dtype=jnp.int32)
    offset = jax.random.randint(jax.random.fold_in(key, 3), (), 1, 2 * POLE, dtype=jnp.int32)
    second = (first + offset) % (2 * POLE)
    values = values.at[first].set(KMAX - 1)
    values = values.at[second].set(lowest)
    return values.astype(jnp.int32)


def block_scale(rng, extent, pieces, least, high):
    factor_of, own = 1.0, jax.random.fold_in(rng, 6)
    for axis_at, shards_of in pieces:
        draws = jnp.exp(jax.random.uniform(jax.random.fold_in(own, axis_at), (shards_of,), jnp.float32, least / len(pieces), high / len(pieces)))
        factor_of = factor_of * jnp.repeat(draws, extent[axis_at] // shards_of).reshape([-1 if axis == axis_at else 1 for axis in range(len(extent))])
    return factor_of


def centred(key, shape, width, reach, shards=(), held_as=jnp.bfloat16):
    result = width * jax.random.normal(key, shape, jnp.float32)
    if shards:
        result = result * block_scale(key, shape, shards, -0.22, 0.18)
    return jnp.clip(result, -reach, reach).astype(held_as)


def setup_inputs(seed: int = 0) -> dict:
    key_list = jax.random.split(jax.random.key(seed), 7)
    tracer = centred(key_list[0], (LEV, NLAT, NLON), 1.0, 6.0, ((1, 2), (2, 16)), jnp.float32)
    wind_east = centred(key_list[1], (LEV, NLAT, NLON), 1.0, 4.0, ((1, 2), (2, 16)), jnp.float32)
    wind_north = centred(key_list[2], (LEV, NLAT, NLON), 1.0, 4.0, ((1, 2), (2, 16)), jnp.float32)
    kappa = jnp.clip(jnp.exp(math.log(4.0) - 2.7725887 * jax.random.uniform(key_list[3], (LEV, NLAT, NLON), jnp.float32) ** block_scale(key_list[3], (LEV, NLAT, NLON), ((1, 2), (2, 16)), -0.2, 0.2)), 0.25, 4.0)
    cutoff = draw_cutoff(jax.random.fold_in(key_list[6], 71), 0)
    partner = draw_partner(jax.random.fold_in(key_list[6], 71), 0)
    return {"tracer": tracer, "wind_east": wind_east, "wind_north": wind_north, "kappa": kappa, "cutoff": cutoff, "partner": partner}


COURANT = 0.4


def neighbours(field, partner):
    beyond_north = jnp.take(field[:, 0, :], partner, axis=1)
    beyond_south = jnp.take(field[:, -1, :], partner, axis=1)
    upper = jnp.concatenate([beyond_north[:, None, :], field[:, :-1, :]], axis=1)
    lower = jnp.concatenate([field[:, 1:, :], beyond_south[:, None, :]], axis=1)
    western = jnp.roll(field, 1, axis=2)
    eastern = jnp.roll(field, -1, axis=2)
    return western, eastern, upper, lower


def lowpass(rows, limits):
    spectrum = jnp.fft.rfft(rows, axis=-1)
    waves = jnp.arange(spectrum.shape[-1], dtype=jnp.int32)
    keep = waves[None, None, :] <= limits[None, :, None]
    spectrum = jnp.where(keep, spectrum, 0.0)
    return jnp.fft.irfft(spectrum, n=rows.shape[-1], axis=-1).astype(rows.dtype)


def reference(tracer, wind_east, wind_north, kappa, cutoff, partner):
    western, eastern, upper, lower = neighbours(tracer, partner)
    advected = tracer - COURANT * 0.5 * (wind_east * (eastern - western) + wind_north * (lower - upper))
    north_rows = lowpass(advected[:, :POLE, :], cutoff[:POLE])
    south_rows = lowpass(advected[:, NLAT - POLE:, :], cutoff[POLE:])
    filtered = jnp.concatenate([north_rows, advected[:, POLE:NLAT - POLE, :], south_rows], axis=1)
    balanced = filtered
    for sweep_index in range(SWEEPS):
        western, eastern, upper, lower = neighbours(balanced, partner)
        balanced = (filtered + kappa * (western + eastern + upper + lower)) / (1.0 + 4.0 * kappa)
    return filtered, balanced
```

```python
import functools
import math

import jax
import jax.numpy as jnp
import numpy as np
from jax import lax
from jax.experimental import pallas as pl
from jax.experimental.pallas import tpu as pltpu
from jax.sharding import PartitionSpec as P

KMAX = 512
SWEEPS = 4
COURANT = 0.4
HIGHEST = lax.Precision.HIGHEST


def tables(sectors, width):
    total = sectors * width
    half = sectors // 2
    m = np.arange(width)
    theta = 2.0 * np.pi * (np.outer(np.arange(half + 1), m) % total) / total
    kept = 2 * KMAX // sectors
    k2 = np.arange(kept) - kept // 2
    phase = 2.0 * np.pi * (np.outer(m, k2) % width) / width
    c, s = np.cos(phase), np.sin(phase)
    forward = np.block([[c, -s], [s, c]])
    inverse = np.block([[c.T, s.T], [-s.T, c.T]]) / total
    return [a.astype(np.float32) for a in (np.cos(theta), np.sin(theta), forward, inverse)]


def weighted(terms):
    total = None
    for factor, value in terms:
        if abs(factor) < 1e-12:
            continue
        part = value if abs(factor - 1.0) < 1e-12 else value * np.float32(factor)
        total = part if total is None else total + part
    return total


def taken(x, at_lane):
    return jnp.take_along_axis(x, at_lane, axis=1, mode="promise_in_bounds")


def kernel(
    sectors, bands,
    tracer_h, wind_east_h, wind_north_h, kappa_h, cutoff_h, partner_h, tw_cos_h, tw_sin_h, fwd_h, inv_h,
    filtered, balanced,
    tracer, wind_east, wind_north, kappa, cutoff, partner, tw_cos, tw_sin, fwd, inv, load_s,
    col_send, col_recv, edge_send, edge_recv, stage, spread, send_b, recv_b, coupling, scaled, ping, pong,
    halo_ss, halo_rs, a_ss, a_rs, b_ss, b_rs,
):
    lev, rows, width = tracer.shape
    pole = cutoff.shape[1] // 2
    share = lev * pole // sectors
    slices = sectors // lev
    half = sectors // 2
    groups = lev * rows // 8
    per = rows // 8
    lat = lax.axis_index("lat")
    lon = lax.axis_index("lon")

    def sector(offset):
        return lax.rem(lon + (offset % sectors), sectors)

    def band(offset):
        return lax.rem(lat + (offset % bands), bands)

    held = (tracer_h, partner_h, wind_east_h, wind_north_h, kappa_h, cutoff_h, tw_cos_h, tw_sin_h, fwd_h, inv_h)
    near = (tracer, partner, wind_east, wind_north, kappa, cutoff, tw_cos, tw_sin, fwd, inv)
    loads = [pltpu.make_async_copy(h, v, load_s.at[i]) for i, (h, v) in enumerate(zip(held, near))]
    for load in loads:
        load.start()

    barrier = pltpu.get_barrier_semaphore()
    for t in range(1, sectors):
        pl.semaphore_signal(barrier, inc=1, device_id=(lat, sector(t)), device_id_type=pl.DeviceIdType.MESH)
    beside = (1,) if bands == 2 else (1, -1)
    for t in beside:
        pl.semaphore_signal(barrier, inc=1, device_id=(band(t), lon), device_id_type=pl.DeviceIdType.MESH)
    pl.semaphore_wait(barrier, sectors - 1 + len(beside))

    loads[0].wait()
    loads[1].wait()
    lane2 = lax.broadcasted_iota(jnp.int32, (rows, width), 1)
    row2 = lax.broadcasted_iota(jnp.int32, (rows, width), 0)
    diagonal = lax.broadcasted_iota(jnp.int32, (groups, 8, width), 0) == lax.broadcasted_iota(
        jnp.int32, (groups, 8, width), 2
    )
    reach = partner[pl.ds(lon, 1), :] - sector(half) * width
    reach = jnp.where(reach < 0, reach + sectors * width, reach)
    beyond = jnp.broadcast_to(reach >= width, (2 * lev, width))
    at_lane = jnp.broadcast_to(jnp.where(reach >= width, reach - width, reach), (2 * lev, width))
    lane8 = lax.broadcasted_iota(jnp.int32, (8, width), 1)
    row8 = lax.broadcasted_iota(jnp.int32, (8, width), 0)
    inner = lax.rem(lane8, per)
    level_of = lax.broadcasted_iota(jnp.int32, (lev, width), 0) * per
    place = lax.broadcasted_iota(jnp.int32, (lev, width), 1)
    head, tail = place == level_of, place == level_of + per - 1

    def column(field, at):
        whole = field[...].reshape(groups, 8, width)
        return jnp.sum(jnp.where(diagonal, whole[:, :, at : at + 1], 0.0), axis=0)

    def border(field, depth):
        return jnp.concatenate(
            [field[l, depth : depth + 1, :] for l in range(lev)]
            + [field[l, rows - 1 - depth : rows - depth, :] for l in range(lev)],
            axis=0,
        )

    def post(turn, edge, first_column, last_column):
        edge_send[turn] = edge
        col_send[turn, 0] = last_column
        col_send[turn, 1] = first_column
        plan = [
            (edge_send.at[turn], edge_recv.at[turn, 0], (lat, sector(-half))),
            (edge_send.at[turn], edge_recv.at[turn, 1], (lat, sector(-half - 1))),
            (edge_send.at[turn], edge_recv.at[turn, 2], (band(1), lon)),
            (col_send.at[turn, 0], col_recv.at[turn, 0], (lat, sector(1))),
            (col_send.at[turn, 1], col_recv.at[turn, 1], (lat, sector(-1))),
        ]
        if bands != 2:
            plan.append((edge_send.at[turn], edge_recv.at[turn, 3], (band(-1), lon)))
        copies = []
        for i, (src, dst, device) in enumerate(plan):
            copy = pltpu.make_async_remote_copy(
                src_ref=src, dst_ref=dst, send_sem=halo_ss.at[turn, i], recv_sem=halo_rs.at[turn, i],
                device_id=device, device_id_type=pl.DeviceIdType.MESH,
            )
            copy.start()
            copies.append(copy)
        return copies

    def outer(turn):
        across = jnp.where(beyond, taken(edge_recv[turn, 1], at_lane), taken(edge_recv[turn, 0], at_lane))
        top = jnp.where(lat == 0, across[:lev], edge_recv[turn, 2, lev:])
        bottom = jnp.where(lat == bands - 1, across[lev:], edge_recv[turn, 2 if bands == 2 else 3, :lev])
        return top, bottom

    def sides(turn, top, bottom):
        west = jnp.sum(jnp.where(diagonal, col_recv[turn, 0][None], 0.0), axis=2, keepdims=True)
        east = jnp.sum(jnp.where(diagonal, col_recv[turn, 1][None], 0.0), axis=2, keepdims=True)
        return top, bottom, west, east

    def along(packed, top, bottom, at):
        above = jnp.sum(jnp.where(head, top[:, at : at + 1], 0.0), axis=0, keepdims=True)
        below = jnp.sum(jnp.where(tail, bottom[:, at : at + 1], 0.0), axis=0, keepdims=True)
        up, down = pltpu.roll(packed, 1, 0), pltpu.roll(packed, 7, 0)
        up = jnp.where(row8 == 0, jnp.where(inner == 0, above, pltpu.roll(up, 1, 1)), up)
        down = jnp.where(row8 == 7, jnp.where(inner == per - 1, below, pltpu.roll(down, width - 1, 1)), down)
        return up + down

    def ends(packed):
        return jnp.concatenate(
            [
                jnp.sum(jnp.where(head, packed[0:1], 0.0), axis=1, keepdims=True),
                jnp.sum(jnp.where(tail, packed[7:8], 0.0), axis=1, keepdims=True),
            ],
            axis=0,
        )

    def around(field, l, edges):
        top, bottom, west, east = edges
        x = field[l]
        w = jnp.broadcast_to(west[per * l : per * (l + 1)], (per, 8, width)).reshape(rows, width)
        e = jnp.broadcast_to(east[per * l : per * (l + 1)], (per, 8, width)).reshape(rows, width)
        return (
            jnp.where(lane2 == 0, w, pltpu.roll(x, 1, 1)),
            jnp.where(lane2 == width - 1, e, pltpu.roll(x, width - 1, 1)),
            jnp.where(row2 == 0, top[l : l + 1], pltpu.roll(x, 1, 0)),
            jnp.where(row2 == rows - 1, bottom[l : l + 1], pltpu.roll(x, rows - 1, 0)),
        )

    copies = post(0, border(tracer, 0), column(tracer, 0), column(tracer, width - 1))
    for load in loads[2:]:
        load.wait()
    for l in range(lev):
        inverse = 1.0 / (1.0 + 4.0 * kappa[l])
        scaled[l] = inverse
        coupling[l] = kappa[l] * inverse
    last = lat == bands - 1
    base = pl.multiple_of(jnp.where(last, rows - pole, 0), 8)
    before = jnp.where(last, rows - pole - 1, 0)
    after = jnp.where(last, rows - 1, pole)
    offset = jnp.where(last, (rows - pole) // 8, 0)
    shape = (pole // 8, 8, width)
    lane_p = lax.broadcasted_iota(jnp.int32, (pole, width), 1)
    row_p = lax.broadcasted_iota(jnp.int32, (pole, width), 0)
    for copy in copies:
        copy.wait()
    top, bottom = outer(0)

    def spoke(packed, l):
        mine = lax.broadcasted_iota(jnp.int32, shape, 0) + (per * l + offset) == lax.broadcasted_iota(
            jnp.int32, shape, 2
        )
        value = jnp.sum(jnp.where(mine, packed[None], 0.0), axis=2, keepdims=True)
        return jnp.broadcast_to(value, shape).reshape(pole, width)

    def to_share(l, q):
        device = l * slices + q
        return pltpu.make_async_remote_copy(
            src_ref=stage.at[l, pl.ds(q * share, share), :], dst_ref=spread.at[lon],
            send_sem=a_ss.at[device], recv_sem=a_rs.at[lon],
            device_id=(lat, device), device_id_type=pl.DeviceIdType.MESH,
        )

    for l in range(lev):
        x = tracer[l, pl.ds(base, pole), :]
        w = jnp.where(lane_p == 0, spoke(col_recv[0, 0], l), pltpu.roll(x, 1, 1))
        e = jnp.where(lane_p == width - 1, spoke(col_recv[0, 1], l), pltpu.roll(x, width - 1, 1))
        above = jnp.where(last, tracer[l, pl.ds(before, 1), :], top[l : l + 1])
        below = jnp.where(last, bottom[l : l + 1], tracer[l, pl.ds(after, 1), :])
        u = jnp.where(row_p == 0, above, pltpu.roll(x, 1, 0))
        d = jnp.where(row_p == pole - 1, below, pltpu.roll(x, pole - 1, 0))
        stage[l] = x - COURANT * 0.5 * (
            wind_east[l, pl.ds(base, pole), :] * (e - w) + wind_north[l, pl.ds(base, pole), :] * (d - u)
        )
        for q in range(slices):
            @pl.when(lon != l * slices + q)
            def _(l=l, q=q):
                to_share(l, q).start()

            @pl.when(lon == l * slices + q)
            def _(l=l, q=q):
                spread[l * slices + q] = stage[l, q * share : (q + 1) * share, :]

    edges = sides(0, top, bottom)
    for l in range(lev):
        w, e, u, d = around(tracer, l, edges)
        filtered[l] = tracer[l] - COURANT * 0.5 * (wind_east[l] * (e - w) + wind_north[l] * (d - u))
    fixed = [(border(a, 0), column(a, 0), column(a, width - 1)) for a in (scaled, coupling)]

    first = jnp.where(lat == bands - 1, pole, 0) + lax.rem(lon, slices) * share
    spot = lax.broadcasted_iota(jnp.int32, (share, 2 * pole), 0) + first
    limit = jnp.sum(
        jnp.where(
            lax.broadcasted_iota(jnp.int32, (share, 2 * pole), 1) == spot,
            cutoff[...].astype(jnp.float32), 0.0,
        ),
        axis=1, keepdims=True,
    )
    kept = 2 * KMAX // sectors
    slot = lax.broadcasted_iota(jnp.int32, (share, 2 * kept), 1)
    wave = sectors * (jnp.where(slot < kept, slot, slot - kept) - kept // 2)
    for device in range(sectors):
        @pl.when(lon != device)
        def _(device=device):
            pltpu.make_async_remote_copy(
                src_ref=stage.at[device // slices, pl.ds(device % slices * share, share), :],
                dst_ref=spread.at[device], send_sem=a_ss.at[device], recv_sem=a_rs.at[device],
                device_id=(lat, device), device_id_type=pl.DeviceIdType.MESH,
            ).wait()

    def circle(d, k):
        angle = 2.0 * math.pi * ((d * k) % sectors) / sectors
        return math.cos(angle), math.sin(angle)

    even = [spread[0]] + [spread[d] + spread[sectors - d] for d in range(1, half)] + [spread[half]]
    odd = [None] + [spread[d] - spread[sectors - d] for d in range(1, half)]
    blocks = []
    for k in range(half + 1):
        c, s = tw_cos[k : k + 1, :], tw_sin[k : k + 1, :]
        re = weighted([(circle(d, k)[0], even[d]) for d in range(half + 1)])
        im = weighted([(-circle(d, k)[1], odd[d]) for d in range(1, half)])
        if im is None:
            blocks.append(jnp.concatenate([re * c, -(re * s)], axis=1))
        else:
            blocks.append(jnp.concatenate([re * c + im * s, im * c - re * s], axis=1))
    spectrum = jnp.dot(
        jnp.concatenate(blocks, axis=0), fwd[...], precision=HIGHEST, preferred_element_type=jnp.float32
    )
    keep = jnp.concatenate(
        [jnp.where(jnp.abs(wave + k).astype(jnp.float32) <= limit, 1.0, 0.0) for k in range(half + 1)], axis=0
    )
    back = jnp.dot(
        jnp.where(keep > 0.0, spectrum, 0.0), inv[...], precision=HIGHEST, preferred_element_type=jnp.float32
    )
    real, imag = [], []
    for k in range(half + 1):
        c, s = tw_cos[k : k + 1, :], tw_sin[k : k + 1, :]
        zr = back[k * share : (k + 1) * share, :width]
        zi = back[k * share : (k + 1) * share, width:]
        twice = 1.0 if k in (0, half) else 2.0
        real.append((zr * c - zi * s) * twice)
        imag.append((zr * s + zi * c) * twice)
    for d in range(half + 1):
        p = weighted([(circle(d, k)[0], real[k]) for k in range(half + 1)])
        q = weighted([(circle(d, k)[1], imag[k]) for k in range(1, half)])
        if q is None:
            send_b[d] = p
        else:
            send_b[d] = p - q
            send_b[sectors - d] = p + q

    copies = []
    for t in range(1, sectors):
        copy = pltpu.make_async_remote_copy(
            src_ref=send_b.at[sector(t)], dst_ref=recv_b.at[lon],
            send_sem=b_ss.at[t], recv_sem=b_rs.at[t],
            device_id=(lat, sector(t)), device_id_type=pl.DeviceIdType.MESH,
        )
        copy.start()
        copies.append(copy)
    recv_b[lon] = send_b[lon]
    plain = border(filtered, 0), column(filtered, 0), column(filtered, width - 1)
    polar = (lat == 0) | last
    for copy in copies:
        copy.wait()

    cells = recv_b[...].reshape(lev * pole // 8, 8, width)
    order = lax.broadcasted_iota(jnp.int32, cells.shape, 0)
    order = lax.div(order, pole // 8) * per + offset + lax.rem(order, pole // 8)
    mine = order == lax.broadcasted_iota(jnp.int32, cells.shape, 2)
    step = lax.rem(lane8, per) - offset
    fresh = (step >= 0) & (step < pole // 8) & polar

    def renewed(old, at):
        return jnp.where(fresh, jnp.sum(jnp.where(mine, cells[:, :, at : at + 1], 0.0), axis=0), old)

    rim = jnp.concatenate(
        [recv_b[l * slices, 0:1, :] for l in range(lev)]
        + [recv_b[l * slices + slices - 1, share - 1 : share, :] for l in range(lev)],
        axis=0,
    )
    edge = jnp.where(((row8 < lev) & (lat == 0)) | ((row8 >= lev) & last), rim, plain[0])
    first_column, last_column = renewed(plain[1], 0), renewed(plain[2], width - 1)
    copies = post(1, edge, first_column, last_column)
    fixed[0] = tuple(a * b for a, b in zip(fixed[0], (edge, first_column, last_column)))

    def restore(start):
        for l in range(lev):
            for q in range(slices):
                filtered[l, start + q * share : start + (q + 1) * share, :] = recv_b[l * slices + q]

    @pl.when(lat == 0)
    def _():
        restore(0)

    @pl.when(lat == bands - 1)
    def _():
        restore(rows - pole)

    for l in range(lev):
        scaled[l] = filtered[l] * scaled[l]
    chain = [filtered, ping, pong, ping, balanced]
    for sweep in range(SWEEPS):
        turn, source, target = 1 + sweep, chain[sweep], chain[sweep + 1]
        if sweep < SWEEPS - 1:
            second, second_first, second_last = border(source, 1), column(source, 1), column(source, width - 2)
        for copy in copies:
            copy.wait()
        top, bottom = outer(turn)
        if sweep < SWEEPS - 1:
            west, east = col_recv[turn, 0], col_recv[turn, 1]
            around_edge = (
                jnp.where(lane8 == 0, ends(west), pltpu.roll(edge, 1, 1))
                + jnp.where(lane8 == width - 1, ends(east), pltpu.roll(edge, width - 1, 1))
                + jnp.concatenate([top, bottom], axis=0)
                + second
            )
            around_first = west + second_first + along(first_column, top, bottom, 0)
            around_last = east + second_last + along(last_column, top, bottom, width - 1)
            edge, first_column, last_column = [
                a + b * c for a, b, c in zip(*fixed, (around_edge, around_first, around_last))
            ]
            copies = post(turn + 1, edge, first_column, last_column)
        edges = sides(turn, top, bottom)
        for l in range(lev):
            w, e, u, d = around(source, l, edges)
            target[l] = scaled[l] + coupling[l] * (w + e + u + d)


def solution(mesh):
    sectors, bands = mesh.shape["lon"], mesh.shape["lat"]

    def per_device(tracer, wind_east, wind_north, kappa, cutoff, partner):
        lev, rows, width = tracer.shape
        share = lev * (cutoff.shape[0] // 2) // sectors
        turns = SWEEPS + 1
        block = pltpu.VMEM((lev, rows, width), jnp.float32)
        vmem = pl.BlockSpec(memory_space=pltpu.VMEM)
        small = (cutoff.reshape(1, -1), partner.reshape(sectors, width), *tables(sectors, width))
        return pl.pallas_call(
            functools.partial(kernel, sectors, bands),
            out_shape=[jax.ShapeDtypeStruct(tracer.shape, jnp.float32)] * 2,
            in_specs=[pl.BlockSpec(memory_space=pltpu.HBM)] * 10,
            out_specs=[vmem] * 2,
            scratch_shapes=[
                block, block, block, block,
                *[pltpu.VMEM(a.shape, a.dtype) for a in small],
                pltpu.SemaphoreType.DMA((10,)),
                pltpu.VMEM((turns, 2, 8, width), jnp.float32),
                pltpu.VMEM((turns, 2, 8, width), jnp.float32),
                pltpu.VMEM((turns, 2 * lev, width), jnp.float32),
                pltpu.VMEM((turns, 4, 2 * lev, width), jnp.float32),
                pltpu.VMEM((lev, cutoff.shape[0] // 2, width), jnp.float32),
                pltpu.VMEM((sectors, share, width), jnp.float32),
                pltpu.VMEM((sectors, share, width), jnp.float32),
                pltpu.VMEM((sectors, share, width), jnp.float32),
                block, block, block, block,
                pltpu.SemaphoreType.DMA((turns, 6)),
                pltpu.SemaphoreType.DMA((turns, 6)),
                pltpu.SemaphoreType.DMA((sectors,)),
                pltpu.SemaphoreType.DMA((sectors,)),
                pltpu.SemaphoreType.DMA((sectors,)),
                pltpu.SemaphoreType.DMA((sectors,)),
            ],
            compiler_params=pltpu.CompilerParams(
                collective_id=0, has_side_effects=True, vmem_limit_bytes=32 * 1024 * 1024
            ),
        )(
            *[pltpu.with_memory_space_constraint(jnp.asarray(a), pltpu.HBM) for a in (tracer, wind_east, wind_north, kappa, *small)]
        )

    spec = P(None, "lat", "lon")
    return jax.shard_map(
        per_device, mesh=mesh, in_specs=(spec, spec, spec, spec, P(), P()), out_specs=(spec, spec),
        check_vma=False,
    )
```

```python
import functools
import math

import jax
import jax.numpy as jnp
import numpy as np
from jax import lax
from jax.experimental import pallas as pl
from jax.experimental.pallas import tpu as pltpu
from jax.sharding import PartitionSpec as P

KMAX = 512
SWEEPS = 4
COURANT = 0.4
HIGHEST = lax.Precision.HIGHEST


def tables(sectors, width):
    total = sectors * width
    half = sectors // 2
    m = np.arange(width)
    theta = 2.0 * np.pi * (np.outer(np.arange(half + 1), m) % total) / total
    kept = 2 * KMAX // sectors
    k2 = np.arange(kept) - kept // 2
    phase = 2.0 * np.pi * (np.outer(m, k2) % width) / width
    c, s = np.cos(phase), np.sin(phase)
    forward = np.block([[c, -s], [s, c]])
    inverse = np.block([[c.T, s.T], [-s.T, c.T]]) / total
    return [a.astype(np.float32) for a in (np.cos(theta), np.sin(theta), forward, inverse)]


def weighted(terms):
    total = None
    for factor, value in terms:
        if abs(factor) < 1e-12:
            continue
        part = value if abs(factor - 1.0) < 1e-12 else value * np.float32(factor)
        total = part if total is None else total + part
    return total


PAD = 16
DEEP = 24
MESH = pl.DeviceIdType.MESH


def taken(x, at_lane):
    return jnp.take_along_axis(x, at_lane, axis=1, mode="promise_in_bounds")


def kernel(
    sectors, bands,
    tracer_h, wind_east_h, wind_north_h, kappa_h, cutoff_h, partner_h, tw_cos_h, tw_sin_h, fwd_h, inv_h,
    filtered, balanced,
    tr, we, wn, ka, cutoff, partner, tw_cos, tw_sin, fwd, inv, load_s,
    send_a, recv_a, pole_send, pole_recv, send_d, recv_d, cross_send, cross_recv, beyond_fix, strip,
    rim_send, rim_recv, adv_send, adv_recv, kcorner_send, kcorner_recv, corner_send, corner_recv,
    field, ping, pong, invert, coupling, scaled,
    side_tiles, side, side_kappa, side_scaled, side_coupling, side_cross,
    a_ss, a_rs, d_ss, d_rs, b_ss, b_rs, c_ss, c_rs, x_ss, x_rs,
):
    lev, rows, width = we.shape
    pole = cutoff.shape[1] // 2
    share = lev * pole // sectors
    slices = sectors // lev
    half = sectors // 2
    groups = rows // 8
    lat = lax.axis_index("lat")
    lon = lax.axis_index("lon")
    last = lat == bands - 1
    north = lat == 0
    polar = north | last

    def sector(offset):
        return lax.rem(lon + (offset % sectors), sectors)

    def band(offset):
        return lax.rem(lat + (offset % bands), bands)

    barrier = pltpu.get_barrier_semaphore()
    for t in range(1, sectors):
        pl.semaphore_signal(barrier, inc=1, device_id=(lat, sector(t)), device_id_type=MESH)
    beside = (1,) if bands == 2 else (1, -1)
    for t in beside:
        pl.semaphore_signal(barrier, inc=1, device_id=(band(t), lon), device_id_type=MESH)

    body = pl.ds(PAD, rows)
    held = (tracer_h, wind_east_h, wind_north_h, kappa_h, partner_h, cutoff_h, tw_cos_h, tw_sin_h, fwd_h, inv_h)
    near = (tr.at[:, body, :], we, wn, ka.at[:, body, :], partner, cutoff, tw_cos, tw_sin, fwd, inv)
    loads = [pltpu.make_async_copy(h, v, load_s.at[i]) for i, (h, v) in enumerate(zip(held, near))]
    for load in loads:
        load.start()

    lane = lax.broadcasted_iota(jnp.int32, (8, width), 1)
    row8 = lax.broadcasted_iota(jnp.int32, (8, width), 0)
    zero = jnp.zeros((8, width), jnp.float32)

    def roll(x, by):
        by = by % width
        return x if by == 0 else pltpu.roll(x, by, 1)

    def swapped(v0, v1):
        low = lane < width // 2
        v0, v1 = jnp.where(low, v0, roll(v1, width // 2)), jnp.where(low, roll(v0, width // 2), v1)
        out = []
        for v in (v0, v1):
            for b in (2, 1, 0):
                step, hop = 1 << b, 8 << b
                upper = (lane & hop) != 0
                same = ((row8 >> b) & 1) == ((lane >> (3 + b)) & 1)
                v = jnp.where(
                    same, v,
                    jnp.where(upper, pltpu.roll(roll(v, hop), 8 - step, 0), pltpu.roll(roll(v, -hop), step, 0)),
                )
            out.append(v)
        return out

    base = pl.multiple_of(jnp.where(last, rows - pole, 0), 8)
    tip = jnp.where(last, rows - 1, 0)
    tip_tile = pl.multiple_of(jnp.where(last, rows - 8, 0), 8)
    tip_slice = jnp.where(last, slices - 1, 0)
    keeper = lax.rem(lon, slices) == tip_slice

    @pl.when(north)
    def _():
        for l in range(lev):
            tr[l, PAD - 8 : PAD, :] = zero

    @pl.when(last)
    def _():
        for l in range(lev):
            tr[l, PAD + rows : PAD + rows + 8, :] = zero

    for load in loads[:3]:
        load.wait()
    lane_p = lax.broadcasted_iota(jnp.int32, (pole, width), 1)
    row_p = lax.broadcasted_iota(jnp.int32, (pole, width), 0)
    before = jnp.where(last, rows - pole - 1, 0)
    after = jnp.where(last, rows - 1, pole)
    eight = lane & 7
    packs = [zero, zero]
    for l in range(lev):
        x = tr[l, pl.ds(base + PAD, pole), :]
        east_wind = we[l, pl.ds(base, pole), :]
        w = jnp.where(lane_p == 0, 0.0, pltpu.roll(x, 1, 1))
        e = jnp.where(lane_p == width - 1, 0.0, pltpu.roll(x, width - 1, 1))
        above = jnp.where(last, tr[l, pl.ds(PAD + before, 1), :], 0.0)
        below = jnp.where(last, 0.0, tr[l, pl.ds(PAD + after, 1), :])
        u = jnp.where(row_p == 0, above, pltpu.roll(x, 1, 0))
        d = jnp.where(row_p == pole - 1, below, pltpu.roll(x, pole - 1, 0))
        stage = x - COURANT * 0.5 * (east_wind * (e - w) + wn[l, pl.ds(base, pole), :] * (d - u))
        for q in range(slices):
            k = l * slices + q
            send_a[k * DEEP : k * DEEP + share, :] = stage[q * share : (q + 1) * share]
            for h in range(2):
                at = q * share + 8 * h
                t = jnp.where(
                    (eight == 3) | (eight == 4), roll(x[at : at + 8], 4 + 8 * k), roll(east_wind[at : at + 8], 6 + 8 * k)
                )
                packs[h] = jnp.where((lane >> 3) == k, t, packs[h])
    for h, v in enumerate(swapped(*packs)):
        for k in range(8):
            send_a[(8 * h + k) * DEEP + share : (8 * h + k) * DEEP + share + 1, :] = v[k : k + 1]

    pl.semaphore_wait(barrier, sectors - 1 + len(beside))

    def across(src, dst, stride, count, ss, rs):
        copies = []
        for t in range(1, sectors):
            copies.append(
                pltpu.make_async_remote_copy(
                    src_ref=src.at[pl.ds(pl.multiple_of(sector(t) * stride, 8), count), :],
                    dst_ref=dst.at[pl.ds(pl.multiple_of(lon * stride, 8), count), :],
                    send_sem=ss.at[t], recv_sem=rs.at[t], device_id=(lat, sector(t)), device_id_type=MESH,
                )
            )
        return copies

    a_copies = across(send_a, recv_a, DEEP, share + 1, a_ss, a_rs)
    for copy in a_copies:
        copy.start()

    loads[3].wait()
    for l in range(lev):
        pole_send[16 * l : 16 * l + 8, :] = ka[l, pl.ds(tip_tile + PAD, 8), :]
        pole_send[16 * l + 8 : 16 * l + 9, :] = tr[l, pl.ds(tip + PAD, 1), :]
        pole_send[16 * l + 9 : 16 * l + 10, :] = wn[l, pl.ds(tip, 1), :]

    def pole_copy(l):
        return pltpu.make_async_remote_copy(
            src_ref=pole_send.at[pl.ds(16 * l, 10), :], dst_ref=pole_recv.at[pl.ds(pl.multiple_of(16 * lon, 8), 10), :],
            send_sem=b_ss.at[l], recv_sem=b_rs.at[lon],
            device_id=(lat, l * slices + tip_slice), device_id_type=MESH,
        )

    for l in range(lev):
        @pl.when(lon != l * slices + tip_slice)
        def _(l=l):
            pole_copy(l).start()

        @pl.when(lon == l * slices + tip_slice)
        def _(l=l):
            pole_recv[pl.ds(pl.multiple_of(16 * lon, 8), 8), :] = pole_send[16 * l : 16 * l + 8, :]
            pole_recv[pl.ds(pl.multiple_of(16 * lon, 8) + 8, 2), :] = pole_send[16 * l + 8 : 16 * l + 10, :]

    four = lane >> 2

    def packed(tiles):
        first, second = zero, zero
        for g, x in enumerate(tiles):
            z = roll(x, 4 * g + 4)
            first = jnp.where(four == g, z, first)
            second = jnp.where(four == (g + 1) % groups, z, second)
        return first, second

    def pack_rims(l, carry):
        at = pl.multiple_of(8 * l, 8)
        for i, source in enumerate((tr, ka)):
            first, second = packed([source[l, PAD + 8 * g : PAD + 8 * g + 8, :] for g in range(groups)])
            rim_send[0, pl.ds(at + 8 * lev * i, 8), :] = first
            rim_send[1, pl.ds(at + 8 * lev * i, 8), :] = second
        return carry

    lax.fori_loop(0, lev, pack_rims, 0)

    def sideways(src, dst, i):
        return [
            pltpu.make_async_remote_copy(
                src_ref=src.at[j], dst_ref=dst.at[j], send_sem=x_ss.at[i + j], recv_sem=x_rs.at[i + j],
                device_id=(lat, sector(1 - 2 * j)), device_id_type=MESH,
            )
            for j in range(2)
        ]

    class Polewards:
        def __init__(self, step, src, dst, i):
            self.copy = lambda: pltpu.make_async_remote_copy(
                src_ref=src, dst_ref=dst, send_sem=x_ss.at[i], recv_sem=x_rs.at[i],
                device_id=(band(step), lon), device_id_type=MESH,
            )
            self.sends = lat < bands - 1 if step == 1 else lat > 0
            self.takes = lat > 0 if step == 1 else lat < bands - 1

        def start(self):
            @pl.when(self.sends)
            def _():
                self.copy().start()

        def wait_recv(self):
            @pl.when(self.takes)
            def _():
                self.copy().wait_recv()

        def wait_send(self):
            @pl.when(self.sends)
            def _():
                self.copy().wait_send()

    def over_rows(ref, i):
        return [
            Polewards(1, ref.at[:, pl.ds(PAD + rows - 8, 8), :], ref.at[:, pl.ds(PAD - 8, 8), :], i),
            Polewards(-1, ref.at[:, pl.ds(PAD, 8), :], ref.at[:, pl.ds(PAD + rows, 8), :], i + 1),
        ]

    x0 = sideways(rim_send, rim_recv, 0) + over_rows(tr, 2) + over_rows(ka, 4)
    for copy in x0:
        copy.start()
    for load in loads[4:]:
        load.wait()

    start = lax.broadcasted_iota(jnp.int32, (sectors, width), 0) + half
    reach = partner[...] - jnp.where(start >= sectors, start - sectors, start) * width
    reach = jnp.where(reach < 0, reach + sectors * width, reach)
    farther = reach >= width
    at_lane = jnp.where(farther, reach - width, reach)

    def crossed(points):
        return jnp.where(
            farther, taken(pltpu.roll(points, sectors - half - 1, 0), at_lane), taken(pltpu.roll(points, half, 0), at_lane)
        )

    for copy in x0:
        copy.wait_recv()

    def renew(l, carry):
        at = pl.multiple_of(8 * l, 8)
        rim = jnp.where(
            (lane & 3) == 3, rim_recv[0, pl.ds(at, 8), :], roll(rim_recv[1, pl.ds(at, 8), :], -2)
        )
        tiles = []
        for g in range(groups):
            at = PAD + 8 * g
            x = tr[l, at : at + 8, :]
            h = roll(rim, -(4 * g + 3))
            w = jnp.where(lane == 0, h, roll(x, 1))
            e = jnp.where(lane == width - 1, h, roll(x, -1))
            turn = wn[l, 8 * g : 8 * g + 8, :] * (tr[l, at + 1 : at + 9, :] - tr[l, at - 1 : at + 7, :])
            value = x - COURANT * 0.5 * (we[l, 8 * g : 8 * g + 8, :] * (e - w) + turn)
            field[l, at : at + 8, :] = value
            filtered[l, 8 * g : 8 * g + 8, :] = value
            k = ka[l, at : at + 8, :]
            inverse = 1.0 / (1.0 + 4.0 * k)
            invert[l, at : at + 8, :] = inverse
            coupling[l, at : at + 8, :] = k * inverse
            scaled[l, at : at + 8, :] = value * inverse
            tiles.append(value)
        first, second = packed(tiles)
        at = pl.multiple_of(8 * l, 8)
        adv_send[0, pl.ds(at, 8), :] = first
        adv_send[1, pl.ds(at, 8), :] = second
        for at in (PAD - 8, PAD + rows):
            k = ka[l, at : at + 8, :]
            inverse = 1.0 / (1.0 + 4.0 * k)
            invert[l, at : at + 8, :] = inverse
            coupling[l, at : at + 8, :] = k * inverse
        return carry

    lax.fori_loop(0, lev, renew, 0)

    def sided(send, recv, at, put):
        for kk in range(4):
            mine = (four & 3) == kk
            near_west = jnp.where(mine, recv[0, at : at + 8, :], send[1, at : at + 8, :])
            near_east = jnp.where(mine, send[0, at : at + 8, :], recv[1, at : at + 8, :])
            put(kk, jnp.where((lane & 15) < 8, roll(near_west, -4 * kk), roll(near_east, 8 - 4 * kk)))

    for l in range(lev):
        def put(kk, tile, l=l):
            side_kappa[l, 12 + 8 * kk : 20 + 8 * kk, :] = tile
            if kk == 3:
                kcorner_send[0, 8 * l : 8 * l + 8, :] = tile
            if kk == 0:
                kcorner_send[1, 8 * l : 8 * l + 8, :] = tile

        sided(rim_send, rim_recv, 8 * (lev + l), put)

    def corners(send, recv, i):
        return [Polewards(1, send.at[0], recv.at[0], i), Polewards(-1, send.at[1], recv.at[1], i + 1)]

    x1 = sideways(adv_send, adv_recv, 6) + over_rows(field, 8) + corners(kcorner_send, kcorner_recv, 10)
    for copy in x1:
        copy.start()

    beyond_fix[...] = jnp.zeros_like(beyond_fix)

    @pl.when(keeper)
    def _():
        for d in range(sectors):
            @pl.when(lon != d)
            def _(d=d):
                pltpu.make_async_remote_copy(
                    src_ref=pole_send.at[pl.ds(0, 10), :], dst_ref=pole_recv.at[pl.ds(16 * d, 10), :],
                    send_sem=b_ss.at[0], recv_sem=b_rs.at[d], device_id=(lat, sector(1)), device_id_type=MESH,
                ).wait_recv()
        tips = jnp.concatenate([pole_recv[16 * d + 8 : 16 * d + 9, :] for d in range(sectors)], axis=0)
        winds = jnp.concatenate([pole_recv[16 * d + 9 : 16 * d + 10, :] for d in range(sectors)], axis=0)
        turned = COURANT * 0.5 * winds * crossed(tips)
        beyond_fix[...] = jnp.where(last, -turned, turned)

    first = jnp.where(last, pole, 0) + lax.rem(lon, slices) * share
    spot = lax.broadcasted_iota(jnp.int32, (share, 2 * pole), 0) + first
    limit = jnp.sum(
        jnp.where(
            lax.broadcasted_iota(jnp.int32, (share, 2 * pole), 1) == spot,
            cutoff[...].astype(jnp.float32), 0.0,
        ),
        axis=1, keepdims=True,
    )
    kept = 2 * KMAX // sectors
    slot = lax.broadcasted_iota(jnp.int32, (share, 2 * kept), 1)
    wave = sectors * (jnp.where(slot < kept, slot, slot - kept) - kept // 2)
    own = pl.multiple_of(lon * DEEP, 8)
    recv_a[pl.ds(own, share), :] = send_a[pl.ds(own, share), :]
    recv_a[pl.ds(own + share, 1), :] = send_a[pl.ds(own + share, 1), :]
    for copy in a_copies:
        copy.wait_recv()

    def rows_of(ref):
        return [
            jnp.concatenate(
                [ref[(8 * h + k) * DEEP + share : (8 * h + k) * DEEP + share + 1, :] for k in range(8)], axis=0
            )
            for h in range(2)
        ]

    fixes = []
    for v in swapped(*rows_of(recv_a)):
        fixes.append(COURANT * 0.5 * v * jnp.where(eight == 6, roll(v, 11), -roll(v, -7)))
    at_tip = [(row8 == 0) & north & keeper, (row8 == 7) & last & keeper]
    ends = (lane == 0) | (lane == width - 1)
    spread = []
    for d in range(sectors):
        parts = []
        for h in range(2):
            x = recv_a[d * DEEP + 8 * h : d * DEEP + 8 * h + 8, :]
            x = x + jnp.where(ends, roll(fixes[h], -(8 * d + 6)), 0.0)
            parts.append(x + jnp.where(at_tip[h], beyond_fix[d : d + 1, :], 0.0))
        spread.append(jnp.concatenate(parts, axis=0))

    def circle(d, k):
        angle = 2.0 * math.pi * ((d * k) % sectors) / sectors
        return math.cos(angle), math.sin(angle)

    even = [spread[0]] + [spread[d] + spread[sectors - d] for d in range(1, half)] + [spread[half]]
    odd = [None] + [spread[d] - spread[sectors - d] for d in range(1, half)]
    blocks = []
    for k in range(half + 1):
        c, s = tw_cos[k : k + 1, :], tw_sin[k : k + 1, :]
        re = weighted([(circle(d, k)[0], even[d]) for d in range(half + 1)])
        im = weighted([(-circle(d, k)[1], odd[d]) for d in range(1, half)])
        if im is None:
            blocks.append(jnp.concatenate([re * c, -(re * s)], axis=1))
        else:
            blocks.append(jnp.concatenate([re * c + im * s, im * c - re * s], axis=1))
    spectrum = jnp.dot(
        jnp.concatenate(blocks, axis=0), fwd[...], precision=HIGHEST, preferred_element_type=jnp.float32
    )
    keep = jnp.concatenate(
        [jnp.where(jnp.abs(wave + k).astype(jnp.float32) <= limit, 1.0, 0.0) for k in range(half + 1)], axis=0
    )
    back = jnp.dot(
        jnp.where(keep > 0.0, spectrum, 0.0), inv[...], precision=HIGHEST, preferred_element_type=jnp.float32
    )
    real, imag = [], []
    for k in range(half + 1):
        c, s = tw_cos[k : k + 1, :], tw_sin[k : k + 1, :]
        zr = back[k * share : (k + 1) * share, :width]
        zi = back[k * share : (k + 1) * share, width:]
        twice = 1.0 if k in (0, half) else 2.0
        real.append((zr * c - zi * s) * twice)
        imag.append((zr * s + zi * c) * twice)
    smooth = [None] * sectors
    for d in range(half + 1):
        p = weighted([(circle(d, k)[0], real[k]) for k in range(half + 1)])
        q = weighted([(circle(d, k)[1], imag[k]) for k in range(1, half)])
        if q is None:
            smooth[d] = p
        else:
            smooth[d], smooth[sectors - d] = p - q, p + q
    edges = [zero, zero]
    for d in range(sectors):
        send_d[d * DEEP : d * DEEP + share, :] = smooth[d]
        for h in range(2):
            edges[h] = jnp.where((lane >> 3) == d, roll(smooth[d][8 * h : 8 * h + 8], 8 * d + 4), edges[h])
    edges = [jnp.where(eight < 4, roll(v, 8), roll(v, -8)) for v in edges]
    for h, v in enumerate(swapped(*edges)):
        for k in range(8):
            send_d[(8 * h + k) * DEEP + share : (8 * h + k) * DEEP + share + 1, :] = v[k : k + 1]

    d_copies = across(send_d, recv_d, DEEP, share + 1, d_ss, d_rs)
    for copy in d_copies:
        copy.start()
    recv_d[pl.ds(own, share), :] = send_d[pl.ds(own, share), :]
    recv_d[pl.ds(own + share, 1), :] = send_d[pl.ds(own + share, 1), :]

    me = lax.div(lon, slices)

    def cross_copy(d):
        return pltpu.make_async_remote_copy(
            src_ref=cross_send.at[pl.ds(8 * d, 5), :], dst_ref=cross_recv.at[pl.ds(pl.multiple_of(8 * me, 8), 5), :],
            send_sem=c_ss.at[d], recv_sem=c_rs.at[me], device_id=(lat, d), device_id_type=MESH,
        )

    @pl.when(keeper)
    def _():
        now, inverse, pull = [], [], []
        for d in range(sectors):
            top, low = d * DEEP, d * DEEP + 8
            now.append(jnp.where(last, send_d[low : low + 8, :], send_d[top : top + 8, :]))
            k = pole_recv[16 * d : 16 * d + 8, :]
            inverse.append(1.0 / (1.0 + 4.0 * k))
            pull.append(k * inverse[d])
        source = [a * b for a, b in zip(now, inverse)]
        ends = jnp.zeros((sectors, width), jnp.float32)
        wide = lax.broadcasted_iota(jnp.int32, (sectors, width), 1)
        for t in range(SWEEPS):
            tips = jnp.concatenate([jnp.where(last, x[7:8], x[0:1]) for x in now], axis=0)
            over = crossed(tips)
            for d in range(sectors):
                cross_send[8 * d + t : 8 * d + t + 1, :] = over[d : d + 1]
            z = roll(over, 8 * t + 4)
            z = jnp.where((wide & 7) < 4, pltpu.roll(z, 1, 0), pltpu.roll(z, sectors - 1, 0))
            ends = jnp.where((wide >> 3) == t, z, ends)
            if t < SWEEPS - 1:
                right, left = [roll(x, 1) for x in now], [roll(x, -1) for x in now]
                later = []
                for d in range(sectors):
                    w = jnp.where(lane == 0, right[d - 1], right[d])
                    e = jnp.where(lane == width - 1, left[(d + 1) % sectors], left[d])
                    u = jnp.where((row8 == 0) & jnp.logical_not(last), over[d : d + 1], pltpu.roll(now[d], 1, 0))
                    b = jnp.where((row8 == 7) & last, over[d : d + 1], pltpu.roll(now[d], 7, 0))
                    later.append(source[d] + pull[d] * (w + e + u + b))
                now = later
        for d in range(sectors):
            cross_send[8 * d + 4 : 8 * d + 5, :] = ends[d : d + 1]
        for d in range(sectors):
            @pl.when(lon != d)
            def _(d=d):
                cross_copy(d).start()
        cross_recv[pl.ds(pl.multiple_of(8 * me, 8), 5), :] = cross_send[pl.ds(pl.multiple_of(8 * lon, 8), 5), :]

    for copy in x1:
        copy.wait_recv()
    for l in range(lev):
        def put(kk, tile, l=l):
            side_tiles[32 * l + 8 * kk : 32 * l + 8 * kk + 8, :] = tile
            if kk == 3:
                corner_send[0, 8 * l : 8 * l + 8, :] = tile
            if kk == 0:
                corner_send[1, 8 * l : 8 * l + 8, :] = tile

        sided(adv_send, adv_recv, 8 * l, put)
    x2 = corners(corner_send, corner_recv, 12)
    for copy in x2:
        copy.start()

    def capped(first_tile, last_tile, recv, l):
        top = roll(jnp.where(lane < width - 16, last_tile, recv[0, 8 * l : 8 * l + 8, :]), 16)
        bottom = roll(jnp.where(lane >= 16, first_tile, recv[1, 8 * l : 8 * l + 8, :]), -16)
        return top, bottom

    for l in range(lev):
        top, bottom = capped(kcorner_send[1, 8 * l : 8 * l + 8, :], kcorner_send[0, 8 * l : 8 * l + 8, :], kcorner_recv, l)
        side_kappa[l, 4:12, :] = top
        side_kappa[l, 44:52, :] = bottom
        for j in range(5):
            at = 8 + 8 * j
            k = side_kappa[l, at : at + 8, :]
            inverse = 1.0 / (1.0 + 4.0 * k)
            side_kappa[l, at : at + 8, :] = inverse
            side_coupling[l, at : at + 8, :] = k * inverse
        for at in (PAD - 8, PAD + rows):
            scaled[l, at : at + 8, :] = field[l, at : at + 8, :] * invert[l, at : at + 8, :]
    for copy in x2:
        copy.wait_recv()

    for copy in d_copies:
        copy.wait_recv()
    for l in range(lev):
        @pl.when(lon != l * slices + tip_slice)
        def _(l=l):
            pltpu.make_async_remote_copy(
                src_ref=cross_send.at[pl.ds(0, 5), :], dst_ref=cross_recv.at[pl.ds(8 * l, 5), :],
                send_sem=c_ss.at[0], recv_sem=c_rs.at[l], device_id=(lat, sector(1)), device_id_type=MESH,
            ).wait_recv()

    @pl.when(polar)
    def _():
        for k in range(sectors):
            l, q = k // slices, k % slices
            x = recv_d[k * DEEP : k * DEEP + share, :]
            at = base + PAD + q * share
            field[l, pl.ds(at, share), :] = x
            scaled[l, pl.ds(at, share), :] = x * invert[l, pl.ds(at, share), :]
            filtered[l, pl.ds(base + q * share, share), :] = x

    def set_cross(target, t):
        @pl.when(north)
        def _():
            for l in range(lev):
                target[l, PAD - 1 : PAD, :] = cross_recv[8 * l + t : 8 * l + t + 1, :]

        @pl.when(last)
        def _():
            for l in range(lev):
                target[l, PAD + rows : PAD + rows + 1, :] = cross_recv[8 * l + t : 8 * l + t + 1, :]

    set_cross(field, 0)

    halo = jnp.concatenate([cross_recv[8 * l + 4 : 8 * l + 5, :] for l in range(lev)] * 2, axis=0)
    for t in range(SWEEPS):
        plain = jnp.concatenate([cross_recv[8 * l + t : 8 * l + t + 1, :] for l in range(lev)] * 2, axis=0)
        z = jnp.where(
            lane < 8,
            jnp.where(lane < 4, roll(halo, -8 * t), roll(plain, 4)),
            jnp.where(lane < 12, roll(plain, 12), roll(halo, 8 - 8 * t)),
        )
        side_cross[t] = jnp.where(last, roll(z, -16), z)

    outside = [jnp.where(last, roll(v, 96), v) for v in swapped(*rows_of(recv_d))]
    from_cap = jnp.where(last, lane - (width - 32), lane)
    inside_cap = polar & (from_cap >= 0) & (from_cap < 32)
    top_spot = north & (row8 == 7) & (lane < 16)
    bottom_spot = last & (row8 == 0) & (lane >= width - 16)
    for l in range(lev):
        tiles = []
        for kk in range(4):
            z = zero
            for g in range(2):
                k, h = l * slices + 2 * g + kk // 2, kk % 2
                x = recv_d[k * DEEP + 8 * h : k * DEEP + 8 * h + 8, :]
                part = lane - 16 * g
                inner = jnp.where(part < 8, roll(x, 16 * g + 4), roll(x, 16 * g + 12))
                inner = jnp.where(last, roll(inner, 96), inner)
                z_outer = outside[h]
                here = from_cap - 16 * g
                outer = jnp.where(here < 8, roll(z_outer, 16 * g - 8 * k), roll(z_outer, 16 * g + 8 - 8 * k))
                value = jnp.where((here >= 4) & (here < 12), inner, outer)
                z = jnp.where((here >= 0) & (here < 16), value, z)
            tile = jnp.where(inside_cap, z, side_tiles[32 * l + 8 * kk : 32 * l + 8 * kk + 8, :])
            side[0, l, 12 + 8 * kk : 20 + 8 * kk, :] = tile
            tiles.append(tile)
        top, bottom = capped(tiles[0], tiles[3], corner_recv, l)
        side[0, l, 4:12, :] = jnp.where(top_spot, side_cross[0, l : l + 1, :], top)
        side[0, l, 44:52, :] = jnp.where(bottom_spot, side_cross[0, l : l + 1, :], bottom)

    for t in range(SWEEPS - 1):
        for l in range(lev):
            for j in range(5):
                at = 8 + 8 * j
                x = side[t, l, at : at + 8, :]
                total = roll(x, 1) + roll(x, -1) + side[t, l, at - 1 : at + 7, :] + side[t, l, at + 1 : at + 9, :]
                if t == 0:
                    source = x * side_kappa[l, at : at + 8, :]
                    side_scaled[l, at : at + 8, :] = source
                else:
                    source = side_scaled[l, at : at + 8, :]
                x = source + side_coupling[l, at : at + 8, :] * total
                if j == 0:
                    x = jnp.where(north & (row8 == 3) & (lane < 16), side_cross[t + 1, l : l + 1, :], x)
                if j == 4:
                    x = jnp.where(last & (row8 == 4) & (lane >= width - 16), side_cross[t + 1, l : l + 1, :], x)
                side[t + 1, l, at : at + 8, :] = x

    chain = [field, ping, pong, ping, balanced]
    for sweep in range(SWEEPS):
        source, target = chain[sweep], chain[sweep + 1]
        final = sweep == SWEEPS - 1

        def relax(l, carry, sweep=sweep, source=source, target=target, final=final):
            for kk in range(4) if final else range(-1, 5):
                h = side[sweep, l, 12 + 8 * kk : 20 + 8 * kk, :]
                h = jnp.where((lane & 15) == 3, h, roll(h, -10))
                for g in range(groups // 4) if 0 <= kk < 4 else ((0,) if kk < 0 else (groups // 4 - 1,)):
                    at = PAD + 32 * g + 8 * kk
                    edge = roll(h, -(16 * g + 3))
                    x = source[l, at : at + 8, :]
                    w = jnp.where(lane == 0, edge, roll(x, 1))
                    e = jnp.where(lane == width - 1, edge, roll(x, -1))
                    total = (w + e) + (source[l, at - 1 : at + 7, :] + source[l, at + 1 : at + 9, :])
                    value = scaled[l, at : at + 8, :] + coupling[l, at : at + 8, :] * total
                    put = at - PAD if final else at
                    target[l, put : put + 8, :] = value
            return carry

        lax.fori_loop(0, lev, relax, 0)
        if not final:
            set_cross(target, sweep + 1)

    for copy in a_copies + x0 + x1 + d_copies + x2:
        copy.wait_send()
    for l in range(lev):
        @pl.when(lon != l * slices + tip_slice)
        def _(l=l):
            pole_copy(l).wait_send()

    @pl.when(keeper)
    def _():
        for d in range(sectors):
            @pl.when(lon != d)
            def _(d=d):
                cross_copy(d).wait_send()


def solution(mesh):
    sectors, bands = mesh.shape["lon"], mesh.shape["lat"]

    def per_device(tracer, wind_east, wind_north, kappa, cutoff, partner):
        lev, rows, width = tracer.shape
        f32 = jnp.float32
        block = pltpu.VMEM((lev, rows, width), f32)
        tall = pltpu.VMEM((lev, rows + 2 * PAD, width), f32)
        strips = pltpu.VMEM((sectors * DEEP, width), f32)
        pair = pltpu.VMEM((2, lev * 8, width), f32)
        narrow = pltpu.VMEM((lev, 56, width), f32)
        vmem = pl.BlockSpec(memory_space=pltpu.VMEM)
        small = (cutoff.reshape(1, -1), partner.reshape(sectors, width), *tables(sectors, width))
        dma = pltpu.SemaphoreType.DMA
        return pl.pallas_call(
            functools.partial(kernel, sectors, bands),
            out_shape=[jax.ShapeDtypeStruct(tracer.shape, f32)] * 2,
            in_specs=[pl.BlockSpec(memory_space=pltpu.HBM)] * 10,
            out_specs=[vmem] * 2,
            scratch_shapes=[
                tall, block, block, tall,
                pltpu.VMEM((1, cutoff.shape[0]), jnp.int32), pltpu.VMEM((sectors, width), jnp.int32),
                *[pltpu.VMEM(a.shape, a.dtype) for a in small[2:]],
                dma((10,)),
                strips, strips,
                pltpu.VMEM((16 * lev, width), f32), pltpu.VMEM((16 * sectors, width), f32),
                strips, strips,
                pltpu.VMEM((8 * sectors, width), f32), pltpu.VMEM((8 * lev, width), f32),
                pltpu.VMEM((sectors, width), f32), pltpu.VMEM((8 * sectors, width), f32),
                pltpu.VMEM((2, 2 * lev * 8, width), f32), pltpu.VMEM((2, 2 * lev * 8, width), f32),
                pair, pair, pair, pair, pair, pair,
                tall, tall, tall, tall, tall, tall,
                pltpu.VMEM((lev * 32, width), f32), pltpu.VMEM((SWEEPS, lev, 56, width), f32),
                narrow, narrow, narrow, pltpu.VMEM((SWEEPS, 8, width), f32),
                *[dma((sectors,))] * 4,
                dma((lev,)), dma((sectors,)), dma((sectors,)), dma((lev,)), dma((14,)), dma((14,)),
            ],
            compiler_params=pltpu.CompilerParams(
                collective_id=0, has_side_effects=True, vmem_limit_bytes=32 * 1024 * 1024
            ),
        )(
            *[pltpu.with_memory_space_constraint(jnp.asarray(a), pltpu.HBM) for a in (tracer, wind_east, wind_north, kappa, *small)]
        )

    spec = P(None, "lat", "lon")
    return jax.shard_map(
        per_device, mesh=mesh, in_specs=(spec, spec, spec, spec, P(), P()), out_specs=(spec, spec),
        check_vma=False,
    )
```

```python
import functools
import math

import jax
import jax.numpy as jnp
import numpy as np
from jax import lax
from jax.experimental import pallas as pl
from jax.experimental.pallas import tpu as pltpu
from jax.sharding import PartitionSpec as P

KMAX = 512
SWEEPS = 4
COURANT = 0.4
HIGHEST = lax.Precision.HIGHEST


def tables(sectors, width):
    total = sectors * width
    half = sectors // 2
    m = np.arange(width)
    theta = 2.0 * np.pi * (np.outer(np.arange(half + 1), m) % total) / total
    kept = 2 * KMAX // sectors
    k2 = np.arange(kept) - kept // 2
    phase = 2.0 * np.pi * (np.outer(m, k2) % width) / width
    c, s = np.cos(phase), np.sin(phase)
    forward = np.block([[c, -s], [s, c]])
    inverse = np.block([[c.T, s.T], [-s.T, c.T]]) / total
    return [a.astype(np.float32) for a in (np.cos(theta), np.sin(theta), forward, inverse)]


def weighted(terms):
    total = None
    for factor, value in terms:
        if abs(factor) < 1e-12:
            continue
        part = value if abs(factor - 1.0) < 1e-12 else value * np.float32(factor)
        total = part if total is None else total + part
    return total


PAD = 16
DEEP = 24
MESH = pl.DeviceIdType.MESH


def taken(x, at_lane):
    return jnp.take_along_axis(x, at_lane, axis=1, mode="promise_in_bounds")


def kernel(
    sectors, bands,
    tracer_h, wind_east_h, wind_north_h, kappa_h, cutoff_h, partner_h, tw_cos_h, tw_sin_h, fwd_h, inv_h,
    field, scaled, coupling, side, side_scaled, side_coupling, side_cross,
    tr, we, wn, ka, cutoff, partner, tw_cos, tw_sin, fwd, inv, load_s,
    send_a, recv_a, pole_send, pole_recv, send_d, recv_d, cross_send, cross_recv, beyond_fix,
    rim_send, rim_recv, kap_send, kap_recv, kap_diag, adv_send, adv_recv, adv_diag, corner, invert, side_tiles, side_invert,
    a_ss, a_rs, d_ss, d_rs, b_ss, b_rs, c_ss, c_rs, x_ss, x_rs,
):
    lev, rows, width = we.shape
    pole = cutoff.shape[1] // 2
    share = lev * pole // sectors
    slices = sectors // lev
    half = sectors // 2
    groups = rows // 8
    lat = lax.axis_index("lat")
    lon = lax.axis_index("lon")
    last = lat == bands - 1
    north = lat == 0
    polar = north | last

    def sector(offset):
        return lax.rem(lon + (offset % sectors), sectors)

    def band(offset):
        return lax.rem(lat + (offset % bands), bands)

    barrier = pltpu.get_barrier_semaphore()
    for t in range(1, sectors):
        pl.semaphore_signal(barrier, inc=1, device_id=(lat, sector(t)), device_id_type=MESH)
    beside = (1,) if bands == 2 else (1, -1)
    for t in beside:
        for i in (-1, 0, 1):
            pl.semaphore_signal(barrier, inc=1, device_id=(band(t), sector(i)), device_id_type=MESH)

    body = pl.ds(PAD, rows)
    held = (tracer_h, wind_east_h, wind_north_h, kappa_h, partner_h, cutoff_h, tw_cos_h, tw_sin_h, fwd_h, inv_h)
    near = (tr.at[:, body, :], we, wn, ka.at[:, body, :], partner, cutoff, tw_cos, tw_sin, fwd, inv)
    loads = [pltpu.make_async_copy(h, v, load_s.at[i]) for i, (h, v) in enumerate(zip(held, near))]
    for load in loads:
        load.start()

    lane = lax.broadcasted_iota(jnp.int32, (8, width), 1)
    row8 = lax.broadcasted_iota(jnp.int32, (8, width), 0)
    zero = jnp.zeros((8, width), jnp.float32)

    def roll(x, by):
        by = by % width
        return x if by == 0 else pltpu.roll(x, by, 1)

    def swapped(v0, v1):
        low = lane < width // 2
        v0, v1 = jnp.where(low, v0, roll(v1, width // 2)), jnp.where(low, roll(v0, width // 2), v1)
        out = []
        for v in (v0, v1):
            for b in (2, 1, 0):
                step, hop = 1 << b, 8 << b
                upper = (lane & hop) != 0
                same = ((row8 >> b) & 1) == ((lane >> (3 + b)) & 1)
                v = jnp.where(
                    same, v,
                    jnp.where(upper, pltpu.roll(roll(v, hop), 8 - step, 0), pltpu.roll(roll(v, -hop), step, 0)),
                )
            out.append(v)
        return out

    base = pl.multiple_of(jnp.where(last, rows - pole, 0), 8)
    tip = jnp.where(last, rows - 1, 0)
    tip_tile = pl.multiple_of(jnp.where(last, rows - 8, 0), 8)
    tip_slice = jnp.where(last, slices - 1, 0)
    keeper = lax.rem(lon, slices) == tip_slice

    @pl.when(north)
    def _():
        for l in range(lev):
            tr[l, PAD - 8 : PAD, :] = zero

    @pl.when(last)
    def _():
        for l in range(lev):
            tr[l, PAD + rows : PAD + rows + 8, :] = zero

    for load in loads[:3]:
        load.wait()
    lane_p = lax.broadcasted_iota(jnp.int32, (pole, width), 1)
    row_p = lax.broadcasted_iota(jnp.int32, (pole, width), 0)
    before = jnp.where(last, rows - pole - 1, 0)
    after = jnp.where(last, rows - 1, pole)
    eight = lane & 7
    packs = [zero, zero]
    for l in range(lev):
        x = tr[l, pl.ds(base + PAD, pole), :]
        east_wind = we[l, pl.ds(base, pole), :]
        w = jnp.where(lane_p == 0, 0.0, pltpu.roll(x, 1, 1))
        e = jnp.where(lane_p == width - 1, 0.0, pltpu.roll(x, width - 1, 1))
        above = jnp.where(last, tr[l, pl.ds(PAD + before, 1), :], 0.0)
        below = jnp.where(last, 0.0, tr[l, pl.ds(PAD + after, 1), :])
        u = jnp.where(row_p == 0, above, pltpu.roll(x, 1, 0))
        d = jnp.where(row_p == pole - 1, below, pltpu.roll(x, pole - 1, 0))
        stage = x - COURANT * 0.5 * (east_wind * (e - w) + wn[l, pl.ds(base, pole), :] * (d - u))
        for q in range(slices):
            k = l * slices + q
            send_a[k * DEEP : k * DEEP + share, :] = stage[q * share : (q + 1) * share]
            for h in range(2):
                at = q * share + 8 * h
                t = jnp.where(
                    (eight == 3) | (eight == 4), roll(x[at : at + 8], 4 + 8 * k), roll(east_wind[at : at + 8], 6 + 8 * k)
                )
                packs[h] = jnp.where((lane >> 3) == k, t, packs[h])
    for h, v in enumerate(swapped(*packs)):
        for k in range(8):
            send_a[(8 * h + k) * DEEP + share : (8 * h + k) * DEEP + share + 1, :] = v[k : k + 1]

    pl.semaphore_wait(barrier, sectors - 1 + 3 * len(beside))

    def across(src, dst, stride, count, ss, rs):
        copies = []
        for t in range(1, sectors):
            copies.append(
                pltpu.make_async_remote_copy(
                    src_ref=src.at[pl.ds(pl.multiple_of(sector(t) * stride, 8), count), :],
                    dst_ref=dst.at[pl.ds(pl.multiple_of(lon * stride, 8), count), :],
                    send_sem=ss.at[t], recv_sem=rs.at[t], device_id=(lat, sector(t)), device_id_type=MESH,
                )
            )
        return copies

    a_copies = across(send_a, recv_a, DEEP, share + 1, a_ss, a_rs)
    for copy in a_copies:
        copy.start()

    four = lane >> 2

    def packed(tiles):
        first, second = zero, zero
        for g, x in enumerate(tiles):
            z = roll(x, 4 * g + 4)
            first = jnp.where(four == g, z, first)
            second = jnp.where(four == (g + 1) % groups, z, second)
        return first, second

    def pack_rims(source, target):
        def one(l, carry):
            at = pl.multiple_of(8 * l, 8)
            first, second = packed([source[l, PAD + 8 * g : PAD + 8 * g + 8, :] for g in range(groups)])
            target[0, pl.ds(at, 8), :] = first
            target[1, pl.ds(at, 8), :] = second
            return carry

        lax.fori_loop(0, lev, one, 0)

    def sideways(src, dst, i):
        return [
            pltpu.make_async_remote_copy(
                src_ref=src.at[j], dst_ref=dst.at[j], send_sem=x_ss.at[i + j], recv_sem=x_rs.at[i + j],
                device_id=(lat, sector(1 - 2 * j)), device_id_type=MESH,
            )
            for j in range(2)
        ]

    class Polewards:
        def __init__(self, step, src, dst, i, aside=0):
            self.copy = lambda: pltpu.make_async_remote_copy(
                src_ref=src, dst_ref=dst, send_sem=x_ss.at[i], recv_sem=x_rs.at[i],
                device_id=(band(step), sector(aside)), device_id_type=MESH,
            )
            self.sends = lat < bands - 1 if step == 1 else lat > 0
            self.takes = lat > 0 if step == 1 else lat < bands - 1

        def start(self):
            @pl.when(self.sends)
            def _():
                self.copy().start()

        def wait_recv(self):
            @pl.when(self.takes)
            def _():
                self.copy().wait_recv()

        def wait_send(self):
            @pl.when(self.sends)
            def _():
                self.copy().wait_send()

    def over_rows(ref, i):
        return [
            Polewards(1, ref.at[:, pl.ds(PAD + rows - 8, 8), :], ref.at[:, pl.ds(PAD - 8, 8), :], i),
            Polewards(-1, ref.at[:, pl.ds(PAD, 8), :], ref.at[:, pl.ds(PAD + rows, 8), :], i + 1),
        ]

    def diagonal(src, dst, i):
        return [
            Polewards(step, src.at[j], dst.at[2 * s + j], i + 2 * s + j, 1 - 2 * j)
            for s, step in enumerate((1, -1))
            for j in range(2)
        ]

    pack_rims(tr, rim_send)
    x0 = sideways(rim_send, rim_recv, 0) + over_rows(tr, 2)
    for copy in x0:
        copy.start()

    loads[3].wait()
    for l in range(lev):
        pole_send[16 * l : 16 * l + 8, :] = ka[l, pl.ds(tip_tile + PAD, 8), :]
        pole_send[16 * l + 8 : 16 * l + 9, :] = tr[l, pl.ds(tip + PAD, 1), :]
        pole_send[16 * l + 9 : 16 * l + 10, :] = wn[l, pl.ds(tip, 1), :]

    def pole_copy(l):
        return pltpu.make_async_remote_copy(
            src_ref=pole_send.at[pl.ds(16 * l, 10), :], dst_ref=pole_recv.at[pl.ds(pl.multiple_of(16 * lon, 8), 10), :],
            send_sem=b_ss.at[l], recv_sem=b_rs.at[lon],
            device_id=(lat, l * slices + tip_slice), device_id_type=MESH,
        )

    for l in range(lev):
        @pl.when(lon != l * slices + tip_slice)
        def _(l=l):
            pole_copy(l).start()

        @pl.when(lon == l * slices + tip_slice)
        def _(l=l):
            pole_recv[pl.ds(pl.multiple_of(16 * lon, 8), 8), :] = pole_send[16 * l : 16 * l + 8, :]
            pole_recv[pl.ds(pl.multiple_of(16 * lon, 8) + 8, 2), :] = pole_send[16 * l + 8 : 16 * l + 10, :]

    pack_rims(ka, kap_send)
    xk = sideways(kap_send, kap_recv, 4) + over_rows(ka, 6) + diagonal(kap_send, kap_diag, 8)
    for copy in xk:
        copy.start()
    for load in loads[4:]:
        load.wait()

    start = lax.broadcasted_iota(jnp.int32, (sectors, width), 0) + half
    reach = partner[...] - jnp.where(start >= sectors, start - sectors, start) * width
    reach = jnp.where(reach < 0, reach + sectors * width, reach)
    farther = reach >= width
    at_lane = jnp.where(farther, reach - width, reach)

    def crossed(points):
        return jnp.where(
            farther, taken(pltpu.roll(points, sectors - half - 1, 0), at_lane), taken(pltpu.roll(points, half, 0), at_lane)
        )

    for copy in x0:
        copy.wait_recv()

    def renew(l, carry):
        at = pl.multiple_of(8 * l, 8)
        rim = jnp.where(
            (lane & 3) == 3, rim_recv[0, pl.ds(at, 8), :], roll(rim_recv[1, pl.ds(at, 8), :], -2)
        )
        tiles = []
        for g in range(groups):
            at = PAD + 8 * g
            x = tr[l, at : at + 8, :]
            h = roll(rim, -(4 * g + 3))
            w = jnp.where(lane == 0, h, roll(x, 1))
            e = jnp.where(lane == width - 1, h, roll(x, -1))
            turn = wn[l, 8 * g : 8 * g + 8, :] * (tr[l, at + 1 : at + 9, :] - tr[l, at - 1 : at + 7, :])
            value = x - COURANT * 0.5 * (we[l, 8 * g : 8 * g + 8, :] * (e - w) + turn)
            field[l, at : at + 8, :] = value
            k = ka[l, at : at + 8, :]
            inverse = 1.0 / (1.0 + 4.0 * k)
            invert[l, at : at + 8, :] = inverse
            coupling[l, at : at + 8, :] = k * inverse
            scaled[l, at : at + 8, :] = value * inverse
            tiles.append(value)
        first, second = packed(tiles)
        at = pl.multiple_of(8 * l, 8)
        adv_send[0, pl.ds(at, 8), :] = first
        adv_send[1, pl.ds(at, 8), :] = second
        return carry

    lax.fori_loop(0, lev, renew, 0)

    def sided(send, recv, at, put):
        for kk in range(4):
            mine = (four & 3) == kk
            near_west = jnp.where(mine, recv[0, at : at + 8, :], send[1, at : at + 8, :])
            near_east = jnp.where(mine, send[0, at : at + 8, :], recv[1, at : at + 8, :])
            put(kk, jnp.where((lane & 15) < 8, roll(near_west, -4 * kk), roll(near_east, 8 - 4 * kk)))

    x1 = sideways(adv_send, adv_recv, 12) + over_rows(field, 14) + diagonal(adv_send, adv_diag, 16)
    for copy in x1:
        copy.start()

    beyond_fix[...] = jnp.zeros_like(beyond_fix)

    @pl.when(keeper)
    def _():
        for d in range(sectors):
            @pl.when(lon != d)
            def _(d=d):
                pltpu.make_async_remote_copy(
                    src_ref=pole_send.at[pl.ds(0, 10), :], dst_ref=pole_recv.at[pl.ds(16 * d, 10), :],
                    send_sem=b_ss.at[0], recv_sem=b_rs.at[d], device_id=(lat, sector(1)), device_id_type=MESH,
                ).wait_recv()
        tips = jnp.concatenate([pole_recv[16 * d + 8 : 16 * d + 9, :] for d in range(sectors)], axis=0)
        winds = jnp.concatenate([pole_recv[16 * d + 9 : 16 * d + 10, :] for d in range(sectors)], axis=0)
        turned = COURANT * 0.5 * winds * crossed(tips)
        beyond_fix[...] = jnp.where(last, -turned, turned)

    first = jnp.where(last, pole, 0) + lax.rem(lon, slices) * share
    spot = lax.broadcasted_iota(jnp.int32, (share, 2 * pole), 0) + first
    limit = jnp.sum(
        jnp.where(
            lax.broadcasted_iota(jnp.int32, (share, 2 * pole), 1) == spot,
            cutoff[...].astype(jnp.float32), 0.0,
        ),
        axis=1, keepdims=True,
    )
    kept = 2 * KMAX // sectors
    slot = lax.broadcasted_iota(jnp.int32, (share, 2 * kept), 1)
    wave = sectors * (jnp.where(slot < kept, slot, slot - kept) - kept // 2)
    own = pl.multiple_of(lon * DEEP, 8)
    recv_a[pl.ds(own, share), :] = send_a[pl.ds(own, share), :]
    recv_a[pl.ds(own + share, 1), :] = send_a[pl.ds(own + share, 1), :]
    for copy in a_copies:
        copy.wait_recv()

    def rows_of(ref, at):
        return [
            jnp.concatenate(
                [ref[(8 * h + k) * DEEP + at : (8 * h + k) * DEEP + at + 1, :] for k in range(8)], axis=0
            )
            for h in range(2)
        ]

    fixes = []
    for v in swapped(*rows_of(recv_a, share)):
        fixes.append(COURANT * 0.5 * v * jnp.where(eight == 6, roll(v, 11), -roll(v, -7)))
    at_tip = [(row8 == 0) & north & keeper, (row8 == 7) & last & keeper]
    ends = (lane == 0) | (lane == width - 1)
    spread = []
    for d in range(sectors):
        parts = []
        for h in range(2):
            x = recv_a[d * DEEP + 8 * h : d * DEEP + 8 * h + 8, :]
            x = x + jnp.where(ends, roll(fixes[h], -(8 * d + 6)), 0.0)
            parts.append(x + jnp.where(at_tip[h], beyond_fix[d : d + 1, :], 0.0))
        spread.append(jnp.concatenate(parts, axis=0))

    def circle(d, k):
        angle = 2.0 * math.pi * ((d * k) % sectors) / sectors
        return math.cos(angle), math.sin(angle)

    even = [spread[0]] + [spread[d] + spread[sectors - d] for d in range(1, half)] + [spread[half]]
    odd = [None] + [spread[d] - spread[sectors - d] for d in range(1, half)]
    blocks = []
    for k in range(half + 1):
        c, s = tw_cos[k : k + 1, :], tw_sin[k : k + 1, :]
        re = weighted([(circle(d, k)[0], even[d]) for d in range(half + 1)])
        im = weighted([(-circle(d, k)[1], odd[d]) for d in range(1, half)])
        if im is None:
            blocks.append(jnp.concatenate([re * c, -(re * s)], axis=1))
        else:
            blocks.append(jnp.concatenate([re * c + im * s, im * c - re * s], axis=1))
    spectrum = jnp.dot(
        jnp.concatenate(blocks, axis=0), fwd[...], precision=HIGHEST, preferred_element_type=jnp.float32
    )
    keep = jnp.concatenate(
        [jnp.where(jnp.abs(wave + k).astype(jnp.float32) <= limit, 1.0, 0.0) for k in range(half + 1)], axis=0
    )
    back = jnp.dot(
        jnp.where(keep > 0.0, spectrum, 0.0), inv[...], precision=HIGHEST, preferred_element_type=jnp.float32
    )
    real, imag = [], []
    for k in range(half + 1):
        c, s = tw_cos[k : k + 1, :], tw_sin[k : k + 1, :]
        zr = back[k * share : (k + 1) * share, :width]
        zi = back[k * share : (k + 1) * share, width:]
        twice = 1.0 if k in (0, half) else 2.0
        real.append((zr * c - zi * s) * twice)
        imag.append((zr * s + zi * c) * twice)
    smooth = [None] * sectors
    for d in range(half + 1):
        p = weighted([(circle(d, k)[0], real[k]) for k in range(half + 1)])
        q = weighted([(circle(d, k)[1], imag[k]) for k in range(1, half)])
        if q is None:
            smooth[d] = p
        else:
            smooth[d], smooth[sectors - d] = p - q, p + q
    edges = [zero, zero]
    for d in range(sectors):
        send_d[d * DEEP : d * DEEP + share, :] = smooth[d]
        for h in range(2):
            edges[h] = jnp.where((lane >> 3) == d, roll(smooth[d][8 * h : 8 * h + 8], 8 * d + 4), edges[h])
    beyond = [jnp.where(eight < 4, roll(v, 8), roll(v, -8)) for v in edges]
    for i in range(2):
        west, east = (beyond, edges) if i == 0 else (edges, beyond)
        for h, v in enumerate(swapped(*[jnp.where(eight < 4, w, e) for w, e in zip(west, east)])):
            for k in range(8):
                at = (8 * h + k) * DEEP + share + i
                send_d[at : at + 1, :] = v[k : k + 1]

    d_copies = across(send_d, recv_d, DEEP, share + 2, d_ss, d_rs)
    for copy in d_copies:
        copy.start()
    recv_d[pl.ds(own, share), :] = send_d[pl.ds(own, share), :]
    recv_d[pl.ds(own + share, 2), :] = send_d[pl.ds(own + share, 2), :]

    me = lax.div(lon, slices)

    def cross_copy(d):
        return pltpu.make_async_remote_copy(
            src_ref=cross_send.at[pl.ds(8 * d, 5), :], dst_ref=cross_recv.at[pl.ds(pl.multiple_of(8 * me, 8), 5), :],
            send_sem=c_ss.at[d], recv_sem=c_rs.at[me], device_id=(lat, d), device_id_type=MESH,
        )

    @pl.when(keeper)
    def _():
        now, inverse, pull = [], [], []
        for d in range(sectors):
            top, low = d * DEEP, d * DEEP + 8
            now.append(jnp.where(last, send_d[low : low + 8, :], send_d[top : top + 8, :]))
            k = pole_recv[16 * d : 16 * d + 8, :]
            inverse.append(1.0 / (1.0 + 4.0 * k))
            pull.append(k * inverse[d])
        source = [a * b for a, b in zip(now, inverse)]
        ends = jnp.zeros((sectors, width), jnp.float32)
        wide = lax.broadcasted_iota(jnp.int32, (sectors, width), 1)
        for t in range(SWEEPS):
            tips = jnp.concatenate([jnp.where(last, x[7:8], x[0:1]) for x in now], axis=0)
            over = crossed(tips)
            for d in range(sectors):
                cross_send[8 * d + t : 8 * d + t + 1, :] = over[d : d + 1]
            z = roll(over, 8 * t + 4)
            z = jnp.where((wide & 7) < 4, pltpu.roll(z, 1, 0), pltpu.roll(z, sectors - 1, 0))
            ends = jnp.where((wide >> 3) == t, z, ends)
            if t < SWEEPS - 1:
                right, left = [roll(x, 1) for x in now], [roll(x, -1) for x in now]
                later = []
                for d in range(sectors):
                    w = jnp.where(lane == 0, right[d - 1], right[d])
                    e = jnp.where(lane == width - 1, left[(d + 1) % sectors], left[d])
                    u = jnp.where((row8 == 0) & jnp.logical_not(last), over[d : d + 1], pltpu.roll(now[d], 1, 0))
                    b = jnp.where((row8 == 7) & last, over[d : d + 1], pltpu.roll(now[d], 7, 0))
                    later.append(source[d] + pull[d] * (w + e + u + b))
                now = later
        for d in range(sectors):
            cross_send[8 * d + 4 : 8 * d + 5, :] = ends[d : d + 1]
        for d in range(sectors):
            @pl.when(lon != d)
            def _(d=d):
                cross_copy(d).start()
        cross_recv[pl.ds(pl.multiple_of(8 * me, 8), 5), :] = cross_send[pl.ds(pl.multiple_of(8 * lon, 8), 5), :]

    for copy in xk:
        copy.wait_recv()

    def corners(ref, diag, l):
        top, bottom = ref[l, PAD - 8 : PAD, :], ref[l, PAD + rows : PAD + rows + 8, :]
        nw, ne, sw, se = [diag[i, 8 * l : 8 * l + 8, :] for i in range(4)]
        first = jnp.where(
            lane < 8, roll(jnp.where(lane >= width - 4, nw, top), 4), roll(jnp.where(lane < 4, ne, top), 12)
        )
        second = jnp.where(
            lane < width - 8,
            jnp.where(lane < width - 12, roll(sw, -16), roll(bottom, -12)),
            jnp.where(lane < width - 4, roll(bottom, -4), roll(se, -8)),
        )
        return first, second

    def capped(first_tile, last_tile, first, second):
        return jnp.where(lane < 16, first, roll(last_tile, 16)), jnp.where(lane >= width - 16, second, roll(first_tile, -16))

    for l in range(lev):
        tiles = []

        def put(kk, tile, l=l, tiles=tiles):
            side_invert[l, 12 + 8 * kk : 20 + 8 * kk, :] = tile
            tiles.append(tile)

        sided(kap_send, kap_recv, 8 * l, put)
        top, bottom = capped(tiles[0], tiles[3], *corners(ka, kap_diag, l))
        side_invert[l, 4:12, :] = top
        side_invert[l, 44:52, :] = bottom
        for j in range(5):
            at = 8 + 8 * j
            k = side_invert[l, at : at + 8, :]
            inverse = 1.0 / (1.0 + 4.0 * k)
            side_invert[l, at : at + 8, :] = inverse
            side_coupling[l, at : at + 8, :] = k * inverse
    for copy in x1:
        copy.wait_recv()
    for l in range(lev):
        for at in (PAD - 8, PAD + rows):
            k = ka[l, at : at + 8, :]
            inverse = 1.0 / (1.0 + 4.0 * k)
            coupling[l, at : at + 8, :] = k * inverse
            scaled[l, at : at + 8, :] = field[l, at : at + 8, :] * inverse

        def put(kk, tile, l=l):
            side_tiles[32 * l + 8 * kk : 32 * l + 8 * kk + 8, :] = tile

        sided(adv_send, adv_recv, 8 * l, put)
        corner[0, 8 * l : 8 * l + 8, :], corner[1, 8 * l : 8 * l + 8, :] = corners(field, adv_diag, l)

    for copy in d_copies:
        copy.wait_recv()
    for l in range(lev):
        @pl.when(lon != l * slices + tip_slice)
        def _(l=l):
            pltpu.make_async_remote_copy(
                src_ref=cross_send.at[pl.ds(0, 5), :], dst_ref=cross_recv.at[pl.ds(8 * l, 5), :],
                send_sem=c_ss.at[0], recv_sem=c_rs.at[l], device_id=(lat, sector(1)), device_id_type=MESH,
            ).wait_recv()

    @pl.when(polar)
    def _():
        for k in range(sectors):
            l, q = k // slices, k % slices
            x = recv_d[k * DEEP : k * DEEP + share, :]
            at = base + PAD + q * share
            field[l, pl.ds(at, share), :] = x
            scaled[l, pl.ds(at, share), :] = x * invert[l, pl.ds(at, share), :]

    @pl.when(north)
    def _():
        for l in range(lev):
            field[l, PAD - 1 : PAD, :] = cross_recv[8 * l : 8 * l + 1, :]

    @pl.when(last)
    def _():
        for l in range(lev):
            field[l, PAD + rows : PAD + rows + 1, :] = cross_recv[8 * l : 8 * l + 1, :]

    halo = jnp.concatenate([cross_recv[8 * l + 4 : 8 * l + 5, :] for l in range(lev)] * 2, axis=0)
    for t in range(SWEEPS):
        plain = jnp.concatenate([cross_recv[8 * l + t : 8 * l + t + 1, :] for l in range(lev)] * 2, axis=0)
        z = jnp.where(
            lane < 8,
            jnp.where(lane < 4, roll(halo, -8 * t), roll(plain, 4)),
            jnp.where(lane < 12, roll(plain, 12), roll(halo, 8 - 8 * t)),
        )
        side_cross[t, :8, :] = jnp.where(last, roll(z, -16), z)
        side_cross[t, 8:, :] = plain

    strips = [
        [jnp.where(last, roll(v, -32), v) for v in swapped(*rows_of(recv_d, share + i))] for i in range(2)
    ]
    from_cap = jnp.where(last, lane - (width - 32), lane)
    inside_cap = polar & (from_cap >= 0) & (from_cap < 32)
    top_spot = north & (row8 == 7) & (lane < 16)
    bottom_spot = last & (row8 == 0) & (lane >= width - 16)
    for l in range(lev):
        tiles = []
        for kk in range(4):
            h, by = kk % 2, -32 * l - 8 * (kk // 2)
            z = jnp.where((lane & 15) < 8, roll(strips[0][h], by), roll(strips[1][h], by + 8))
            tile = jnp.where(inside_cap, z, side_tiles[32 * l + 8 * kk : 32 * l + 8 * kk + 8, :])
            side[l, 12 + 8 * kk : 20 + 8 * kk, :] = tile
            tiles.append(tile)
        at = 8 * l
        top, bottom = capped(tiles[0], tiles[3], corner[0, at : at + 8, :], corner[1, at : at + 8, :])
        side[l, 4:12, :] = jnp.where(top_spot, side_cross[0, l : l + 1, :], top)
        side[l, 44:52, :] = jnp.where(bottom_spot, side_cross[0, l : l + 1, :], bottom)
        for j in range(5):
            at = 8 + 8 * j
            side_scaled[l, at : at + 8, :] = side[l, at : at + 8, :] * side_invert[l, at : at + 8, :]

    for copy in a_copies + x0 + xk + x1 + d_copies:
        copy.wait_send()
    for l in range(lev):
        @pl.when(lon != l * slices + tip_slice)
        def _(l=l):
            pole_copy(l).wait_send()

    @pl.when(keeper)
    def _():
        for d in range(sectors):
            @pl.when(lon != d)
            def _(d=d):
                cross_copy(d).wait_send()


def relax(
    bands, field, scaled, coupling, side0, side_scaled, side_coupling, side_cross, filtered, balanced, stack, side, sems
):
    lev, rows, width = filtered.shape
    groups = rows // 8
    bf16, f32 = jnp.bfloat16, jnp.float32
    lat = lax.axis_index("lat")
    north, last = lat == 0, lat == bands - 1
    out = pltpu.make_async_copy(field.at[:, pl.ds(PAD, rows), :], filtered, sems.at[0])
    out.start()
    lane = lax.broadcasted_iota(jnp.int32, (8, width), 1)
    row8 = lax.broadcasted_iota(jnp.int32, (8, width), 0)
    at16 = lane & 15
    one = lax.broadcasted_iota(jnp.int32, (width, width), 0)
    two = lax.broadcasted_iota(jnp.int32, (width, width), 1)
    shift = jnp.where((one - two == 1) | (two - one == 1), 1.0, 0.0).astype(bf16)
    spot = one & 15
    from_west = (two == 0) & ((spot == 3) | (spot == 4))
    from_east = (two == width - 1) & ((spot == 12) | (spot == 13))
    weights = jnp.concatenate([shift, shift, jnp.where(from_west | from_east, 1.0, 0.0).astype(bf16)], axis=0)

    def roll(x, by):
        return pltpu.roll(x, by % width, 1)

    def parts(x):
        high = x.astype(bf16)
        return high, (x - high.astype(f32)).astype(bf16)

    def level(source, target, beside, l):
        ends = {}
        for kk in range(-1, 5):
            high, low = parts(beside(l, 12 + 8 * kk))
            ends[kk] = jnp.where(
                (at16 == 3) | (at16 == 12), high.astype(f32),
                jnp.where((at16 == 4) | (at16 == 13), roll(low.astype(f32), 1), 0.0),
            )
        order = [(0, -1)] + [(i // 4, i % 4) for i in range(groups)] + [(groups // 4 - 1, 4)]
        high, low = parts(source(l, PAD - 8, rows + 16))
        edge = jnp.concatenate([jnp.where((lane >> 4) == g, ends[kk], 0.0) for g, kk in order], axis=0).astype(bf16)
        total = jnp.dot(jnp.concatenate([high, low, edge], axis=1), weights, preferred_element_type=f32)
        for i in range(groups + 2):
            at = PAD - 8 + 8 * i
            value = total[8 * i : 8 * i + 8] + (source(l, at - 1, 8) + source(l, at + 1, 8))
            target(l, at, scaled[l, at : at + 8, :] + coupling[l, at : at + 8, :] * value)

    for l in range(lev):
        stack[0, l, PAD - 16 : PAD + rows + 16, :] = field[l]
        side[0, l] = side0[l]

    def sweep(t, carry):
        def source(l, at, count):
            return stack[t, l, at : at + count, :]

        def target(l, at, value):
            stack[t + 1, l, at : at + 8, :] = value

        def beside(l, at):
            return side[t, l, at : at + 8, :]

        for l in range(lev):
            level(source, target, beside, l)
            for j in range(5):
                at = 8 + 8 * j
                x = beside(l, at)
                total = roll(x, 1) + roll(x, -1) + beside(l, at - 1) + beside(l, at + 1)
                x = side_scaled[l, at : at + 8, :] + side_coupling[l, at : at + 8, :] * total
                cross = side_cross[t + 1, pl.ds(l, 1), :]
                if j == 0:
                    x = jnp.where(north & (row8 == 3) & (lane < 16), cross, x)
                if j == 4:
                    x = jnp.where(last & (row8 == 4) & (lane >= width - 16), cross, x)
                side[t + 1, l, at : at + 8, :] = x
        for l in range(lev):
            cross = side_cross[t + 1, pl.ds(8 + l, 1), :]
            for here, at in ((north, PAD - 1), (last, PAD + rows)):
                stack[t + 1, l, at : at + 1, :] = jnp.where(here, cross, stack[t + 1, l, at : at + 1, :])
        return carry

    lax.fori_loop(0, SWEEPS - 1, sweep, 0)
    copies = [out]
    for l in range(lev):
        level(
            lambda l, at, count: stack[SWEEPS - 1, l, at : at + count, :],
            lambda l, at, value: stack.__setitem__((SWEEPS, l, slice(at, at + 8), slice(None)), value),
            lambda l, at: side[SWEEPS - 1, l, at : at + 8, :],
            l,
        )
        copy = pltpu.make_async_copy(stack.at[SWEEPS, l, pl.ds(PAD, rows), :], balanced.at[l], sems.at[1 + l])
        copy.start()
        copies.append(copy)
    for copy in copies:
        copy.wait()


def solution(mesh):
    sectors, bands = mesh.shape["lon"], mesh.shape["lat"]

    def per_device(tracer, wind_east, wind_north, kappa, cutoff, partner):
        lev, rows, width = tracer.shape
        f32 = jnp.float32
        high = rows + 2 * PAD

        def array(*shape):
            return pltpu.VMEM(shape, f32)

        block, tall = array(lev, rows, width), array(lev, high, width)
        strips = array(sectors * DEEP, width)
        pair, four = array(2, lev * 8, width), array(4, lev * 8, width)
        narrow = array(lev, 56, width)
        vmem = pl.BlockSpec(memory_space=pltpu.VMEM)
        hbm = pl.BlockSpec(memory_space=pltpu.HBM)
        small = (cutoff.reshape(1, -1), partner.reshape(sectors, width), *tables(sectors, width))
        dma = pltpu.SemaphoreType.DMA
        made = [(lev, high, width)] * 3 + [(lev, 56, width)] * 3 + [(SWEEPS, 16, width)]
        limit = 24 * 1024 * 1024
        held = pl.pallas_call(
            functools.partial(kernel, sectors, bands),
            out_shape=[jax.ShapeDtypeStruct(shape, f32) for shape in made],
            in_specs=[hbm] * 10,
            out_specs=[vmem] * len(made),
            scratch_shapes=[
                tall, block, block, tall,
                *[pltpu.VMEM(a.shape, a.dtype) for a in small],
                dma((10,)),
                strips, strips, array(16 * lev, width), array(16 * sectors, width), strips, strips,
                array(8 * sectors, width), array(8 * lev, width), array(sectors, width),
                pair, pair, pair, pair, four, pair, pair, four, pair, tall, array(lev * 32, width), narrow,
                *[dma((sectors,))] * 4,
                dma((lev,)), dma((sectors,)), dma((sectors,)), dma((lev,)), dma((20,)), dma((20,)),
            ],
            compiler_params=pltpu.CompilerParams(collective_id=0, has_side_effects=True, vmem_limit_bytes=limit),
        )(
            *[pltpu.with_memory_space_constraint(jnp.asarray(a), pltpu.HBM) for a in (tracer, wind_east, wind_north, kappa, *small)]
        )
        return pl.pallas_call(
            functools.partial(relax, bands),
            out_shape=[jax.ShapeDtypeStruct(tracer.shape, f32)] * 2,
            in_specs=[vmem] * len(made),
            out_specs=[hbm] * 2,
            scratch_shapes=[array(SWEEPS + 1, lev, high, width), array(SWEEPS, lev, 56, width), dma((1 + lev,))],
            compiler_params=pltpu.CompilerParams(vmem_limit_bytes=limit),
        )(*[pltpu.with_memory_space_constraint(a, pltpu.VMEM) for a in held])

    spec = P(None, "lat", "lon")
    return jax.shard_map(
        per_device, mesh=mesh, in_specs=(spec, spec, spec, spec, P(), P()), out_specs=(spec, spec),
        check_vma=False,
    )
```

```python
import functools
import math

import jax
import jax.numpy as jnp
import numpy as np
from jax import lax
from jax.experimental import pallas as pl
from jax.experimental.pallas import tpu as pltpu
from jax.sharding import PartitionSpec as P

KMAX = 512
SWEEPS = 4
COURANT = 0.4
HIGHEST = lax.Precision.HIGHEST


def tables(sectors, width):
    total = sectors * width
    half = sectors // 2
    m = np.arange(width)
    theta = 2.0 * np.pi * (np.outer(np.arange(half + 1), m) % total) / total
    kept = 2 * KMAX // sectors
    k2 = np.arange(kept) - kept // 2
    phase = 2.0 * np.pi * (np.outer(m, k2) % width) / width
    c, s = np.cos(phase), np.sin(phase)
    forward = np.block([[c, -s], [s, c]])
    inverse = np.block([[c.T, s.T], [-s.T, c.T]]) / total
    return [a.astype(np.float32) for a in (np.cos(theta), np.sin(theta), forward, inverse)]


def weighted(terms):
    total = None
    for factor, value in terms:
        if abs(factor) < 1e-12:
            continue
        part = value if abs(factor - 1.0) < 1e-12 else value * np.float32(factor)
        total = part if total is None else total + part
    return total


PAD = 16
DEEP = 24
MESH = pl.DeviceIdType.MESH


def taken(x, at_lane):
    return jnp.take_along_axis(x, at_lane, axis=1, mode="promise_in_bounds")


def parts(x):
    high = x.astype(jnp.bfloat16)
    return high, (x - high.astype(jnp.float32)).astype(jnp.bfloat16)


def shift_weights(width):
    one = lax.broadcasted_iota(jnp.int32, (width, width), 0)
    two = lax.broadcasted_iota(jnp.int32, (width, width), 1)
    shift = jnp.where((one - two == 1) | (two - one == 1), 1.0, 0.0).astype(jnp.bfloat16)
    spot = one & 15
    from_west = (two == 0) & ((spot == 3) | (spot == 4))
    from_east = (two == width - 1) & ((spot == 12) | (spot == 13))
    edge = jnp.where(from_west | from_east, 1.0, 0.0).astype(jnp.bfloat16)
    return jnp.concatenate([shift, shift, edge], axis=0)


def rim(h, at16):
    high, low = parts(h)
    return jnp.where(
        (at16 == 3) | (at16 == 12), high.astype(jnp.float32),
        jnp.where((at16 == 4) | (at16 == 13), pltpu.roll(low.astype(jnp.float32), 1, 1), 0.0),
    )


def west_and_east(x, edges, weights):
    high, low = parts(x)
    rims = jnp.concatenate(edges, axis=0).astype(jnp.bfloat16)
    return jnp.dot(jnp.concatenate([high, low, rims], axis=1), weights, preferred_element_type=jnp.float32)


def kernel(
    sectors, bands,
    tracer_h, wind_east_h, wind_north_h, kappa_h, cutoff_h, partner_h, table_h,
    stack, scaled, coupling, side, side_scaled, side_coupling, side_cross,
    tr, we, wn, ka, cutoff, partner, table, load_s,
    send_a, recv_a, pole_send, pole_recv, send_d, recv_d, beyond_fix,
    rim_send, rim_recv, kap_send, kap_recv, kap_diag, adv_send, adv_recv, adv_diag, corner, invert, side_tiles, side_invert, early, early_scaled,
    a_s, a_r, b_s, b_r, d_s, d_r, x_s, x_r, k_s, k_r, f_s, f_r,
):
    lev, rows, width = we.shape
    field = stack.at[0]
    pole = cutoff.shape[1] // 2
    share = lev * pole // sectors
    slices = sectors // lev
    half = sectors // 2
    groups = rows // 8
    lat = lax.axis_index("lat")
    lon = lax.axis_index("lon")
    last = lat == bands - 1
    north = lat == 0
    polar = north | last

    def sector(offset):
        return lax.rem(lon + (offset % sectors), sectors)

    def band(offset):
        return lax.rem(lat + (offset % bands), bands)

    body = pl.ds(PAD, rows)
    held = (tracer_h, wind_east_h, wind_north_h, kappa_h, partner_h, cutoff_h, table_h)
    near = (tr.at[:, body, :], we, wn, ka.at[:, body, :], partner, cutoff, table)
    loads = [pltpu.make_async_copy(h, v, load_s.at[i]) for i, (h, v) in enumerate(zip(held, near))]
    for load in loads[:3]:
        load.start()

    barrier = pltpu.get_barrier_semaphore()
    for t in range(1, sectors):
        pl.semaphore_signal(barrier, inc=1, device_id=(lat, sector(t)), device_id_type=MESH)
    beside = (1,) if bands == 2 else (1, -1)
    for t in beside:
        for i in (-1, 0, 1):
            pl.semaphore_signal(barrier, inc=1, device_id=(band(t), sector(i)), device_id_type=MESH)

    for load in loads[3:]:
        load.start()

    lane = lax.broadcasted_iota(jnp.int32, (8, width), 1)
    row8 = lax.broadcasted_iota(jnp.int32, (8, width), 0)
    zero = jnp.zeros((8, width), jnp.float32)

    def roll(x, by):
        by = by % width
        return x if by == 0 else pltpu.roll(x, by, 1)

    def swapped(v0, v1):
        low = lane < width // 2
        v0, v1 = jnp.where(low, v0, roll(v1, width // 2)), jnp.where(low, roll(v0, width // 2), v1)
        out = []
        for v in (v0, v1):
            for b in (2, 1, 0):
                step, hop = 1 << b, 8 << b
                upper = (lane & hop) != 0
                same = ((row8 >> b) & 1) == ((lane >> (3 + b)) & 1)
                v = jnp.where(
                    same, v,
                    jnp.where(upper, pltpu.roll(roll(v, hop), 8 - step, 0), pltpu.roll(roll(v, -hop), step, 0)),
                )
            out.append(v)
        return out

    base = pl.multiple_of(jnp.where(last, rows - pole, 0), 8)
    tip = jnp.where(last, rows - 1, 0)
    tip_tile = pl.multiple_of(jnp.where(last, rows - 8, 0), 8)
    tip_slice = jnp.where(last, slices - 1, 0)
    keeper = lax.rem(lon, slices) == tip_slice

    @pl.when(north)
    def _():
        for l in range(lev):
            tr[l, PAD - 8 : PAD, :] = zero

    @pl.when(last)
    def _():
        for l in range(lev):
            tr[l, PAD + rows : PAD + rows + 8, :] = zero

    for load in loads[:3]:
        load.wait()
    lane_p = lax.broadcasted_iota(jnp.int32, (pole, width), 1)
    row_p = lax.broadcasted_iota(jnp.int32, (pole, width), 0)
    before = jnp.where(last, rows - pole - 1, 0)
    after = jnp.where(last, rows - 1, pole)
    eight = lane & 7
    packs = [zero, zero]
    for l in range(lev):
        x = tr[l, pl.ds(base + PAD, pole), :]
        east_wind = we[l, pl.ds(base, pole), :]
        w = jnp.where(lane_p == 0, 0.0, pltpu.roll(x, 1, 1))
        e = jnp.where(lane_p == width - 1, 0.0, pltpu.roll(x, width - 1, 1))
        above = jnp.where(last, tr[l, pl.ds(PAD + before, 1), :], 0.0)
        below = jnp.where(last, 0.0, tr[l, pl.ds(PAD + after, 1), :])
        u = jnp.where(row_p == 0, above, pltpu.roll(x, 1, 0))
        d = jnp.where(row_p == pole - 1, below, pltpu.roll(x, pole - 1, 0))
        stage = x - COURANT * 0.5 * (east_wind * (e - w) + wn[l, pl.ds(base, pole), :] * (d - u))
        for q in range(slices):
            k = l * slices + q
            send_a[k * DEEP : k * DEEP + share, :] = stage[q * share : (q + 1) * share]
            for h in range(2):
                at = q * share + 8 * h
                t = jnp.where(
                    (eight == 3) | (eight == 4), roll(x[at : at + 8], 4 + 8 * k), roll(east_wind[at : at + 8], 6 + 8 * k)
                )
                packs[h] = jnp.where((lane >> 3) == k, t, packs[h])
    for h, v in enumerate(swapped(*packs)):
        send_a[pl.ds(8 * h * DEEP + share, 8, stride=DEEP), :] = v

    pl.semaphore_wait(barrier, sectors - 1 + 3 * len(beside))

    def across(src, dst, count, ss, rs):
        for t in range(1, sectors):
            there = sector(t)
            pltpu.make_async_remote_copy(
                src_ref=src.at[pl.ds(pl.multiple_of(there * DEEP, 8), count), :],
                dst_ref=dst.at[pl.ds(pl.multiple_of(lon * DEEP, 8), count), :],
                send_sem=ss, recv_sem=rs, device_id=(lat, there), device_id_type=MESH,
            ).start()

    def bulk(count, sem):
        whole = send_d.at[pl.ds(0, count), :]
        return pltpu.make_async_remote_copy(
            src_ref=whole, dst_ref=whole, send_sem=sem, recv_sem=sem, device_id=(lat, sector(1)), device_id_type=MESH
        )

    def split_wait(single, double, sem, send):
        for here, count in ((polar, single), (jnp.logical_not(polar), double)):
            @pl.when(here)
            def _(count=count):
                if send:
                    bulk(count, sem).wait_send()
                else:
                    bulk(count, sem).wait_recv()

    across(send_a, recv_a, share + 1, a_s, a_r)

    four = lane >> 2

    def packed(tiles):
        first, second = zero, zero
        for g, x in enumerate(tiles):
            z = roll(x, 4 * g + 4)
            first = jnp.where(four == g, z, first)
            second = jnp.where(four == (g + 1) % groups, z, second)
        return first, second

    def pack_rims(source, target):
        def one(l, carry):
            at = pl.multiple_of(8 * l, 8)
            first, second = packed([source[l, PAD + 8 * g : PAD + 8 * g + 8, :] for g in range(groups)])
            target[0, pl.ds(at, 8), :] = first
            target[1, pl.ds(at, 8), :] = second
            return carry

        lax.fori_loop(0, lev, one, 0)

    def sideways(src, dst, ss, rs):
        for j in range(2):
            pltpu.make_async_remote_copy(
                src_ref=src.at[j], dst_ref=dst.at[j], send_sem=ss, recv_sem=rs,
                device_id=(lat, sector(1 - 2 * j)), device_id_type=MESH,
            ).start()

    def poleward(ref, ss, rs, send=None, recv=None):
        for i, step in enumerate((1, -1)):
            plan = [
                (
                    ref.at[:, pl.ds(PAD + rows - 8 if step == 1 else PAD, 8), :],
                    ref.at[:, pl.ds(PAD - 8 if step == 1 else PAD + rows, 8), :], 0,
                )
            ]
            if send is not None:
                plan += [(send.at[j], recv.at[2 * i + j], 1 - 2 * j) for j in range(2)]

            @pl.when(lat < bands - 1 if step == 1 else lat > 0)
            def _(step=step, plan=plan):
                for src, dst, aside in plan:
                    pltpu.make_async_remote_copy(
                        src_ref=src, dst_ref=dst, send_sem=ss, recv_sem=rs,
                        device_id=(band(step), sector(aside)), device_id_type=MESH,
                    ).start()

    unit = 8 * lev
    pack_rims(tr, rim_send)
    sideways(rim_send, rim_recv, x_s, x_r)
    poleward(tr, x_s, x_r)

    loads[3].wait()
    for l in range(lev):
        pole_send[16 * l : 16 * l + 8, :] = ka[l, pl.ds(tip_tile + PAD, 8), :]
        pole_send[16 * l + 8 : 16 * l + 9, :] = tr[l, pl.ds(tip + PAD, 1), :]
        pole_send[16 * l + 9 : 16 * l + 10, :] = wn[l, pl.ds(tip, 1), :]

    def pole_copy(l):
        return pltpu.make_async_remote_copy(
            src_ref=pole_send.at[pl.ds(16 * l, 10), :], dst_ref=pole_recv.at[pl.ds(pl.multiple_of(16 * lon, 8), 10), :],
            send_sem=b_s, recv_sem=b_r,
            device_id=(lat, l * slices + tip_slice), device_id_type=MESH,
        )

    for l in range(lev):
        @pl.when(lon != l * slices + tip_slice)
        def _(l=l):
            pole_copy(l).start()

        @pl.when(lon == l * slices + tip_slice)
        def _(l=l):
            pole_recv[pl.ds(pl.multiple_of(16 * lon, 8), 8), :] = pole_send[16 * l : 16 * l + 8, :]
            pole_recv[pl.ds(pl.multiple_of(16 * lon, 8) + 8, 2), :] = pole_send[16 * l + 8 : 16 * l + 10, :]

    pack_rims(ka, kap_send)
    sideways(kap_send, kap_recv, k_s, k_r)
    poleward(ka, k_s, k_r, kap_send, kap_diag)
    for load in loads[4:]:
        load.wait()

    start = lax.broadcasted_iota(jnp.int32, (sectors, width), 0) + half
    reach = partner[...] - jnp.where(start >= sectors, start - sectors, start) * width
    reach = jnp.where(reach < 0, reach + sectors * width, reach)
    farther = reach >= width
    at_lane = jnp.where(farther, reach - width, reach)

    def crossed(points):
        return jnp.where(
            farther, taken(pltpu.roll(points, sectors - half - 1, 0), at_lane), taken(pltpu.roll(points, half, 0), at_lane)
        )

    split_wait(3 * unit, 4 * unit, x_r, False)

    def renew(l, carry):
        at = pl.multiple_of(8 * l, 8)
        rim = jnp.where(
            (lane & 3) == 3, rim_recv[0, pl.ds(at, 8), :], roll(rim_recv[1, pl.ds(at, 8), :], -2)
        )
        tiles = []
        for g in range(groups):
            at = PAD + 8 * g
            x = tr[l, at : at + 8, :]
            h = roll(rim, -(4 * g + 3))
            w = jnp.where(lane == 0, h, roll(x, 1))
            e = jnp.where(lane == width - 1, h, roll(x, -1))
            turn = wn[l, 8 * g : 8 * g + 8, :] * (tr[l, at + 1 : at + 9, :] - tr[l, at - 1 : at + 7, :])
            value = x - COURANT * 0.5 * (we[l, 8 * g : 8 * g + 8, :] * (e - w) + turn)
            field[l, at : at + 8, :] = value
            k = ka[l, at : at + 8, :]
            inverse = 1.0 / (1.0 + 4.0 * k)
            invert[l, at : at + 8, :] = inverse
            coupling[l, at : at + 8, :] = k * inverse
            scaled[l, at : at + 8, :] = value * inverse
            tiles.append(value)
        first, second = packed(tiles)
        at = pl.multiple_of(8 * l, 8)
        adv_send[0, pl.ds(at, 8), :] = first
        adv_send[1, pl.ds(at, 8), :] = second
        return carry

    lax.fori_loop(0, lev, renew, 0)

    def sided(send, recv, at, put):
        for kk in range(4):
            mine = (four & 3) == kk
            near_west = jnp.where(mine, recv[0, at : at + 8, :], send[1, at : at + 8, :])
            near_east = jnp.where(mine, send[0, at : at + 8, :], recv[1, at : at + 8, :])
            put(kk, jnp.where((lane & 15) < 8, roll(near_west, -4 * kk), roll(near_east, 8 - 4 * kk)))

    sideways(adv_send, adv_recv, f_s, f_r)
    poleward(field, f_s, f_r, adv_send, adv_diag)

    beyond_fix[...] = jnp.zeros_like(beyond_fix)

    @pl.when(keeper)
    def _():
        bulk(10 * (sectors - 1), b_r).wait_recv()
        tips = jnp.concatenate([pole_recv[16 * d + 8 : 16 * d + 9, :] for d in range(sectors)], axis=0)
        winds = jnp.concatenate([pole_recv[16 * d + 9 : 16 * d + 10, :] for d in range(sectors)], axis=0)
        turned = COURANT * 0.5 * winds * crossed(tips)
        beyond_fix[...] = jnp.where(last, -turned, turned)

    first = jnp.where(last, pole, 0) + lax.rem(lon, slices) * share
    spot = lax.broadcasted_iota(jnp.int32, (share, 2 * pole), 0) + first
    limit = jnp.sum(
        jnp.where(
            lax.broadcasted_iota(jnp.int32, (share, 2 * pole), 1) == spot,
            cutoff[...].astype(jnp.float32), 0.0,
        ),
        axis=1, keepdims=True,
    )
    kept = 2 * KMAX // sectors
    slot = lax.broadcasted_iota(jnp.int32, (share, 2 * kept), 1)
    wave = sectors * (jnp.where(slot < kept, slot, slot - kept) - kept // 2)
    own = pl.multiple_of(lon * DEEP, 8)
    recv_a[pl.ds(own, share), :] = send_a[pl.ds(own, share), :]
    recv_a[pl.ds(own + share, 1), :] = send_a[pl.ds(own + share, 1), :]
    bulk((share + 1) * (sectors - 1), a_r).wait_recv()
    tw_cos, tw_sin = table[0 : half + 1, :], table[16 : half + 17, :]
    fwd = table[32 : 32 + 2 * width, :]
    inv = jnp.concatenate([table[32 + 2 * width : 32 + 3 * width, :], table[32 + 3 * width : 32 + 4 * width, :]], axis=1)

    def rows_of(ref, at):
        return [ref[pl.ds(8 * h * DEEP + at, 8, stride=DEEP), :] for h in range(2)]

    fixes = []
    for v in swapped(*rows_of(recv_a, share)):
        fixes.append(COURANT * 0.5 * v * jnp.where(eight == 6, roll(v, 11), -roll(v, -7)))
    at_tip = [(row8 == 0) & north & keeper, (row8 == 7) & last & keeper]
    ends = (lane == 0) | (lane == width - 1)
    spread = []
    for d in range(sectors):
        parts = []
        for h in range(2):
            x = recv_a[d * DEEP + 8 * h : d * DEEP + 8 * h + 8, :]
            x = x + jnp.where(ends, roll(fixes[h], -(8 * d + 6)), 0.0)
            parts.append(x + jnp.where(at_tip[h], beyond_fix[d : d + 1, :], 0.0))
        spread.append(jnp.concatenate(parts, axis=0))

    def circle(d, k):
        angle = 2.0 * math.pi * ((d * k) % sectors) / sectors
        return math.cos(angle), math.sin(angle)

    even = [spread[0]] + [spread[d] + spread[sectors - d] for d in range(1, half)] + [spread[half]]
    odd = [None] + [spread[d] - spread[sectors - d] for d in range(1, half)]
    blocks = []
    for k in range(half + 1):
        c, s = tw_cos[k : k + 1, :], tw_sin[k : k + 1, :]
        re = weighted([(circle(d, k)[0], even[d]) for d in range(half + 1)])
        im = weighted([(-circle(d, k)[1], odd[d]) for d in range(1, half)])
        if im is None:
            blocks.append(jnp.concatenate([re * c, -(re * s)], axis=1))
        else:
            blocks.append(jnp.concatenate([re * c + im * s, im * c - re * s], axis=1))
    spectrum = jnp.dot(
        jnp.concatenate(blocks, axis=0), fwd, precision=HIGHEST, preferred_element_type=jnp.float32
    )
    keep = jnp.concatenate(
        [jnp.where(jnp.abs(wave + k).astype(jnp.float32) <= limit, 1.0, 0.0) for k in range(half + 1)], axis=0
    )
    back = jnp.dot(
        jnp.where(keep > 0.0, spectrum, 0.0), inv, precision=HIGHEST, preferred_element_type=jnp.float32
    )
    real, imag = [], []
    for k in range(half + 1):
        c, s = tw_cos[k : k + 1, :], tw_sin[k : k + 1, :]
        zr = back[k * share : (k + 1) * share, :width]
        zi = back[k * share : (k + 1) * share, width:]
        twice = 1.0 if k in (0, half) else 2.0
        real.append((zr * c - zi * s) * twice)
        imag.append((zr * s + zi * c) * twice)
    smooth = [None] * sectors
    for d in range(half + 1):
        p = weighted([(circle(d, k)[0], real[k]) for k in range(half + 1)])
        q = weighted([(circle(d, k)[1], imag[k]) for k in range(1, half)])
        if q is None:
            smooth[d] = p
        else:
            smooth[d], smooth[sectors - d] = p - q, p + q
    edges = [zero, zero]
    for d in range(sectors):
        send_d[d * DEEP : d * DEEP + share, :] = smooth[d]
        for h in range(2):
            edges[h] = jnp.where((lane >> 3) == d, roll(smooth[d][8 * h : 8 * h + 8], 8 * d + 4), edges[h])
    beyond = [jnp.where(eight < 4, roll(v, 8), roll(v, -8)) for v in edges]
    for i in range(2):
        west, east = (beyond, edges) if i == 0 else (edges, beyond)
        for h, v in enumerate(swapped(*[jnp.where(eight < 4, w, e) for w, e in zip(west, east)])):
            send_d[pl.ds(8 * h * DEEP + share + i, 8, stride=DEEP), :] = v

    extra = share + 2 + SWEEPS + 1

    def put_cross(t, rows16):
        for h in range(2):
            send_d[pl.ds(8 * h * DEEP + share + 2 + t, 8, stride=DEEP), :] = rows16[8 * h : 8 * h + 8]

    @pl.when(keeper)
    def _():
        now, inverse, pull = [], [], []
        for d in range(sectors):
            top, low = d * DEEP, d * DEEP + 8
            now.append(jnp.where(last, send_d[low : low + 8, :], send_d[top : top + 8, :]))
            k = pole_recv[16 * d : 16 * d + 8, :]
            inverse.append(1.0 / (1.0 + 4.0 * k))
            pull.append(k * inverse[d])
        source = [a * b for a, b in zip(now, inverse)]
        ends = jnp.zeros((sectors, width), jnp.float32)
        wide = lax.broadcasted_iota(jnp.int32, (sectors, width), 1)
        for t in range(SWEEPS):
            tips = jnp.concatenate([jnp.where(last, x[7:8], x[0:1]) for x in now], axis=0)
            over = crossed(tips)
            put_cross(t, over)
            z = roll(over, 8 * t + 4)
            z = jnp.where((wide & 7) < 4, pltpu.roll(z, 1, 0), pltpu.roll(z, sectors - 1, 0))
            ends = jnp.where((wide >> 3) == t, z, ends)
            if t < SWEEPS - 1:
                right, left = [roll(x, 1) for x in now], [roll(x, -1) for x in now]
                later = []
                for d in range(sectors):
                    w = jnp.where(lane == 0, right[d - 1], right[d])
                    e = jnp.where(lane == width - 1, left[(d + 1) % sectors], left[d])
                    u = jnp.where((row8 == 0) & jnp.logical_not(last), over[d : d + 1], pltpu.roll(now[d], 1, 0))
                    b = jnp.where((row8 == 7) & last, over[d : d + 1], pltpu.roll(now[d], 7, 0))
                    later.append(source[d] + pull[d] * (w + e + u + b))
                now = later
        put_cross(SWEEPS, ends)
        across(send_d, recv_d, extra, d_s, d_r)

    @pl.when(jnp.logical_not(keeper))
    def _():
        across(send_d, recv_d, share + 2, d_s, d_r)

    recv_d[pl.ds(own, share), :] = send_d[pl.ds(own, share), :]
    recv_d[pl.ds(own + share, 2), :] = send_d[pl.ds(own + share, 2), :]

    @pl.when(keeper)
    def _():
        recv_d[pl.ds(own + share + 2, SWEEPS + 1), :] = send_d[pl.ds(own + share + 2, SWEEPS + 1), :]

    split_wait(5 * unit, 8 * unit, k_r, False)

    def corners(ref, diag, l):
        top, bottom = ref[l, PAD - 8 : PAD, :], ref[l, PAD + rows : PAD + rows + 8, :]
        nw, ne, sw, se = [diag[i, 8 * l : 8 * l + 8, :] for i in range(4)]
        first = jnp.where(
            lane < 8, roll(jnp.where(lane >= width - 4, nw, top), 4), roll(jnp.where(lane < 4, ne, top), 12)
        )
        second = jnp.where(
            lane < width - 8,
            jnp.where(lane < width - 12, roll(sw, -16), roll(bottom, -12)),
            jnp.where(lane < width - 4, roll(bottom, -4), roll(se, -8)),
        )
        return first, second

    def capped(first_tile, last_tile, first, second):
        return jnp.where(lane < 16, first, roll(last_tile, 16)), jnp.where(lane >= width - 16, second, roll(first_tile, -16))

    for l in range(lev):
        tiles = []

        def put(kk, tile, l=l, tiles=tiles):
            side_invert[l, 12 + 8 * kk : 20 + 8 * kk, :] = tile
            tiles.append(tile)

        sided(kap_send, kap_recv, 8 * l, put)
        top, bottom = capped(tiles[0], tiles[3], *corners(ka, kap_diag, l))
        side_invert[l, 4:12, :] = top
        side_invert[l, 44:52, :] = bottom
        for j in range(5):
            at = 8 + 8 * j
            k = side_invert[l, at : at + 8, :]
            inverse = 1.0 / (1.0 + 4.0 * k)
            side_invert[l, at : at + 8, :] = inverse
            side_coupling[l, at : at + 8, :] = k * inverse
    split_wait(5 * unit, 8 * unit, f_r, False)
    for l in range(lev):
        for at in (PAD - 8, PAD + rows):
            k = ka[l, at : at + 8, :]
            inverse = 1.0 / (1.0 + 4.0 * k)
            coupling[l, at : at + 8, :] = k * inverse
            scaled[l, at : at + 8, :] = field[l, at : at + 8, :] * inverse

        def put(kk, tile, l=l):
            side_tiles[32 * l + 8 * kk : 32 * l + 8 * kk + 8, :] = tile

        sided(adv_send, adv_recv, 8 * l, put)
        corner[0, 8 * l : 8 * l + 8, :], corner[1, 8 * l : 8 * l + 8, :] = corners(field, adv_diag, l)
        at = 32 * l
        early[0, l, 12:44, :] = side_tiles[at : at + 32, :]
        early[0, l, 4:12, :], early[0, l, 44:52, :] = capped(
            side_tiles[at : at + 8, :], side_tiles[at + 24 : at + 32, :],
            corner[0, 8 * l : 8 * l + 8, :], corner[1, 8 * l : 8 * l + 8, :],
        )
        early_scaled[l, 8:48, :] = early[0, l, 8:48, :] * side_invert[l, 8:48, :]

    weights = shift_weights(width)
    order = [(0, -1)] + [(i // 4, i % 4) for i in range(groups)] + [(groups // 4 - 1, 4)]
    at16 = lane & 15

    def sweep_early(t, carry):
        for l in range(lev):
            ends = {kk: rim(early[t, l, 12 + 8 * kk : 20 + 8 * kk, :], at16) for kk in range(-1, 5)}
            total = west_and_east(
                stack[t, l, PAD - 8 : PAD + rows + 8, :],
                [jnp.where((lane >> 4) == g, ends[kk], 0.0) for g, kk in order], weights,
            )
            for i in range(groups + 2):
                at = PAD - 8 + 8 * i
                value = total[8 * i : 8 * i + 8] + (stack[t, l, at - 1 : at + 7, :] + stack[t, l, at + 1 : at + 9, :])
                stack[t + 1, l, at : at + 8, :] = scaled[l, at : at + 8, :] + coupling[l, at : at + 8, :] * value
            for j in range(5):
                at = 8 + 8 * j
                x = early[t, l, at : at + 8, :]
                value = roll(x, 1) + roll(x, -1) + early[t, l, at - 1 : at + 7, :] + early[t, l, at + 1 : at + 9, :]
                early[t + 1, l, at : at + 8, :] = (
                    early_scaled[l, at : at + 8, :] + side_coupling[l, at : at + 8, :] * value
                )
        return carry

    lax.fori_loop(0, SWEEPS, sweep_early, 0)

    plain_rows, more = (share + 2) * (sectors - 1), SWEEPS + 1
    d_waits = ((keeper, plain_rows + more * (lev - 1)), (jnp.logical_not(keeper), plain_rows + more * lev))
    for here, count in d_waits:
        @pl.when(here)
        def _(count=count):
            bulk(count, d_r).wait_recv()

    def cross(l, t):
        return recv_d[pl.ds((l * slices + tip_slice) * DEEP + share + 2 + t, 1), :]

    @pl.when(polar)
    def _():
        for k in range(sectors):
            l, q = k // slices, k % slices
            x = recv_d[k * DEEP : k * DEEP + share, :]
            at = base + PAD + q * share
            field[l, pl.ds(at, share), :] = x
            scaled[l, pl.ds(at, share), :] = x * invert[l, pl.ds(at, share), :]

    @pl.when(north)
    def _():
        for l in range(lev):
            field[l, PAD - 1 : PAD, :] = cross(l, 0)

    @pl.when(last)
    def _():
        for l in range(lev):
            field[l, PAD + rows : PAD + rows + 1, :] = cross(l, 0)

    halo = jnp.concatenate([cross(l, SWEEPS) for l in range(lev)] * 2, axis=0)
    for t in range(SWEEPS):
        plain = jnp.concatenate([cross(l, t) for l in range(lev)] * 2, axis=0)
        z = jnp.where(
            lane < 8,
            jnp.where(lane < 4, roll(halo, -8 * t), roll(plain, 4)),
            jnp.where(lane < 12, roll(plain, 12), roll(halo, 8 - 8 * t)),
        )
        side_cross[t, :8, :] = jnp.where(last, roll(z, -16), z)
        side_cross[t, 8:, :] = plain

    strips = [
        [jnp.where(last, roll(v, -32), v) for v in swapped(*rows_of(recv_d, share + i))] for i in range(2)
    ]
    from_cap = jnp.where(last, lane - (width - 32), lane)
    inside_cap = polar & (from_cap >= 0) & (from_cap < 32)
    top_spot = north & (row8 == 7) & (lane < 16)
    bottom_spot = last & (row8 == 0) & (lane >= width - 16)
    for l in range(lev):
        tiles = []
        for kk in range(4):
            h, by = kk % 2, -32 * l - 8 * (kk // 2)
            z = jnp.where((lane & 15) < 8, roll(strips[0][h], by), roll(strips[1][h], by + 8))
            tile = jnp.where(inside_cap, z, side_tiles[32 * l + 8 * kk : 32 * l + 8 * kk + 8, :])
            side[l, 12 + 8 * kk : 20 + 8 * kk, :] = tile
            tiles.append(tile)
        at = 8 * l
        top, bottom = capped(tiles[0], tiles[3], corner[0, at : at + 8, :], corner[1, at : at + 8, :])
        side[l, 4:12, :] = jnp.where(top_spot, side_cross[0, l : l + 1, :], top)
        side[l, 44:52, :] = jnp.where(bottom_spot, side_cross[0, l : l + 1, :], bottom)
        for j in range(5):
            at = 8 + 8 * j
            side_scaled[l, at : at + 8, :] = side[l, at : at + 8, :] * side_invert[l, at : at + 8, :]

    bulk((share + 1) * (sectors - 1), a_s).wait_send()
    split_wait(3 * unit, 4 * unit, x_s, True)
    split_wait(5 * unit, 8 * unit, k_s, True)
    split_wait(5 * unit, 8 * unit, f_s, True)
    for here, pole_rows, rows_out in (
        (keeper, 10 * (lev - 1), extra * (sectors - 1)), (jnp.logical_not(keeper), 10 * lev, plain_rows)
    ):
        @pl.when(here)
        def _(pole_rows=pole_rows, rows_out=rows_out):
            bulk(pole_rows, b_s).wait_send()
            bulk(rows_out, d_s).wait_send()


def relax(
    bands, stack, scaled, coupling, side0, side_scaled, side_coupling, side_cross, filtered, balanced, local, side, sems
):
    lev, rows, width = filtered.shape
    near = local.shape[2] - 2 * PAD
    tiles = near // 8 + 2
    lat = lax.axis_index("lat")
    north, last = lat == 0, lat == bands - 1
    base = pl.multiple_of(jnp.where(last, rows - near, 0), 8)
    rest = pl.multiple_of(jnp.where(last, 0, near), 8)
    copies = [
        pltpu.make_async_copy(stack.at[0, :, pl.ds(PAD, rows), :], filtered, sems.at[0]),
        pltpu.make_async_copy(
            stack.at[SWEEPS, :, pl.ds(rest + PAD, rows - near), :], balanced.at[:, pl.ds(rest, rows - near), :], sems.at[1]
        ),
    ]
    for copy in copies:
        copy.start()
    lane = lax.broadcasted_iota(jnp.int32, (8, width), 1)
    row8 = lax.broadcasted_iota(jnp.int32, (8, width), 0)
    at16 = lane & 15
    group = (lane >> 4) - jnp.where(last, (rows - near) // 32, 0)
    weights = shift_weights(width)
    for l in range(lev):
        local[0, l, PAD - 8 : PAD + near + 8, :] = stack[0, l, pl.ds(base + PAD - 8, near + 16), :]
    for t in range(SWEEPS):
        beside = side0 if t == 0 else side.at[t - 1]
        edges = []
        for l in range(lev):
            ends = {kk: rim(beside[l, 12 + 8 * kk : 20 + 8 * kk, :], at16) for kk in range(-1, 5)}
            edges.append(jnp.where(lane < 16, ends[-1], 0.0))
            for i in range(near // 8):
                edges.append(jnp.where(group == i // 4, ends[i % 4], 0.0))
            edges.append(jnp.where(lane >= width - 16, ends[4], 0.0))
        whole = jnp.concatenate([local[t, l, PAD - 8 : PAD + near + 8, :] for l in range(lev)], axis=0)
        total = west_and_east(whole, edges, weights)
        for l in range(lev):
            for i in range(tiles):
                at = PAD - 8 + 8 * i
                start = 8 * (tiles * l + i)
                value = total[start : start + 8] + (local[t, l, at - 1 : at + 7, :] + local[t, l, at + 1 : at + 9, :])
                there = pl.ds(base + at, 8)
                value = scaled[l, there, :] + coupling[l, there, :] * value
                if t < SWEEPS - 1 and i in (0, tiles - 1):
                    cross = side_cross[t + 1, 8 + l : 9 + l, :]
                    if i == 0:
                        at_end = rows - near + PAD - 8
                        value = jnp.where(north & (row8 == 7), cross, value)
                        value = jnp.where(last, stack[t + 1, l, at_end : at_end + 8, :], value)
                    else:
                        at_end = near + PAD
                        value = jnp.where(
                            last, jnp.where(row8 == 0, cross, value), stack[t + 1, l, at_end : at_end + 8, :]
                        )
                local[t + 1, l, at : at + 8, :] = value
        if t == SWEEPS - 1:
            break
        for l in range(lev):
            for j in range(5):
                at = 8 + 8 * j
                x = beside[l, at : at + 8, :]
                value = pltpu.roll(x, 1, 1) + pltpu.roll(x, width - 1, 1)
                value = value + (beside[l, at - 1 : at + 7, :] + beside[l, at + 1 : at + 9, :])
                x = side_scaled[l, at : at + 8, :] + side_coupling[l, at : at + 8, :] * value
                cross = side_cross[t + 1, l : l + 1, :]
                if j == 0:
                    x = jnp.where(north & (row8 == 3) & (lane < 16), cross, x)
                if j == 4:
                    x = jnp.where(last & (row8 == 4) & (lane >= width - 16), cross, x)
                side[t, l, at : at + 8, :] = x
    copy = pltpu.make_async_copy(
        local.at[SWEEPS, :, pl.ds(PAD, near), :], balanced.at[:, pl.ds(base, near), :], sems.at[2]
    )
    copy.start()
    for copy in (*copies, copy):
        copy.wait()


def solution(mesh):
    sectors, bands = mesh.shape["lon"], mesh.shape["lat"]

    def per_device(tracer, wind_east, wind_north, kappa, cutoff, partner):
        lev, rows, width = tracer.shape
        f32 = jnp.float32
        high = rows + 2 * PAD

        def array(*shape):
            return pltpu.VMEM(shape, f32)

        block, tall = array(lev, rows, width), array(lev, high, width)
        strips = array(sectors * DEEP, width)
        pair, four = array(2, lev * 8, width), array(4, lev * 8, width)
        narrow = array(lev, 56, width)
        vmem = pl.BlockSpec(memory_space=pltpu.VMEM)
        hbm = pl.BlockSpec(memory_space=pltpu.HBM)
        tw_cos, tw_sin, fwd, inv = tables(sectors, width)
        blank = np.zeros((16 - tw_cos.shape[0], width), np.float32)
        table = np.concatenate([tw_cos, blank, tw_sin, blank, fwd, inv[:, :width], inv[:, width:]], axis=0)
        small = (cutoff.reshape(1, -1), partner.reshape(sectors, width), table)
        dma = pltpu.SemaphoreType.DMA
        made = [(SWEEPS + 1, lev, high, width)] + [(lev, high, width)] * 2 + [(lev, 56, width)] * 3 + [(SWEEPS, 16, width)]
        limit = 24 * 1024 * 1024
        near = cutoff.shape[0] // 2 + 32
        held = pl.pallas_call(
            functools.partial(kernel, sectors, bands),
            out_shape=[jax.ShapeDtypeStruct(shape, f32) for shape in made],
            in_specs=[hbm] * 7,
            out_specs=[vmem] * len(made),
            scratch_shapes=[
                tall, block, block, tall,
                *[pltpu.VMEM(a.shape, a.dtype) for a in small],
                dma((7,)),
                strips, strips, array(16 * lev, width), array(16 * sectors, width), strips, strips,
                array(sectors, width),
                pair, pair, pair, pair, four, pair, pair, four, pair, tall, array(lev * 32, width), narrow, array(SWEEPS + 1, lev, 56, width), narrow,
                *[dma] * 12,
            ],
            compiler_params=pltpu.CompilerParams(collective_id=0, has_side_effects=True, vmem_limit_bytes=limit),
        )(
            *[pltpu.with_memory_space_constraint(jnp.asarray(a), pltpu.HBM) for a in (tracer, wind_east, wind_north, kappa, *small)]
        )
        return pl.pallas_call(
            functools.partial(relax, bands),
            out_shape=[jax.ShapeDtypeStruct(tracer.shape, f32)] * 2,
            in_specs=[vmem] * len(made),
            out_specs=[hbm] * 2,
            scratch_shapes=[array(SWEEPS + 1, lev, near + 2 * PAD, width), array(SWEEPS - 1, lev, 56, width), dma((3,))],
            compiler_params=pltpu.CompilerParams(vmem_limit_bytes=limit),
        )(*[pltpu.with_memory_space_constraint(a, pltpu.VMEM) for a in held])

    spec = P(None, "lat", "lon")
    return jax.shard_map(
        per_device, mesh=mesh, in_specs=(spec, spec, spec, spec, P(), P()), out_specs=(spec, spec),
        check_vma=False,
    )
```

```python
import functools
import math

import jax
import jax.numpy as jnp
import numpy as np
from jax import lax
from jax.experimental import pallas as pl
from jax.experimental.pallas import tpu as pltpu
from jax.sharding import PartitionSpec as P

KMAX = 512
SWEEPS = 4
COURANT = 0.4
HIGHEST = lax.Precision.HIGHEST


def tables(sectors, width):
    total = sectors * width
    half = sectors // 2
    m = np.arange(width)
    theta = 2.0 * np.pi * (np.outer(np.arange(half + 1), m) % total) / total
    kept = 2 * KMAX // sectors
    k2 = np.arange(kept) - kept // 2
    phase = 2.0 * np.pi * (np.outer(m, k2) % width) / width
    c, s = np.cos(phase), np.sin(phase)
    forward = np.block([[c, -s], [s, c]])
    inverse = np.block([[c.T, s.T], [-s.T, c.T]]) / total
    return [a.astype(np.float32) for a in (np.cos(theta), np.sin(theta), forward, inverse)]


def weighted(terms):
    total = None
    for factor, value in terms:
        if abs(factor) < 1e-12:
            continue
        part = value if abs(factor - 1.0) < 1e-12 else value * np.float32(factor)
        total = part if total is None else total + part
    return total


PAD = 16
DEEP = 24
MESH = pl.DeviceIdType.MESH


def taken(x, at_lane):
    return jnp.take_along_axis(x, at_lane, axis=1, mode="promise_in_bounds")


def parts(x):
    high = x.astype(jnp.bfloat16)
    return high, (x - high.astype(jnp.float32)).astype(jnp.bfloat16)


def shift_weights(width):
    one = lax.broadcasted_iota(jnp.int32, (width, width), 0)
    two = lax.broadcasted_iota(jnp.int32, (width, width), 1)
    shift = jnp.where((one - two == 1) | (two - one == 1), 1.0, 0.0).astype(jnp.bfloat16)
    spot = one & 15
    from_west = (two == 0) & ((spot == 3) | (spot == 4))
    from_east = (two == width - 1) & ((spot == 12) | (spot == 13))
    edge = jnp.where(from_west | from_east, 1.0, 0.0).astype(jnp.bfloat16)
    return jnp.concatenate([shift, shift, edge], axis=0)


def change_weights(width):
    one = lax.broadcasted_iota(jnp.int32, (width, width), 0)
    two = lax.broadcasted_iota(jnp.int32, (width, width), 1)
    shift = (jnp.where(one - two == 1, 1.0, 0.0) - jnp.where(two - one == 1, 1.0, 0.0)).astype(jnp.bfloat16)
    edge = jnp.where((two == width - 1) & ((one & 1) == 0), 1.0, 0.0) - jnp.where((two == 0) & ((one & 1) == 1), 1.0, 0.0)
    return jnp.concatenate([shift, shift, edge.astype(jnp.bfloat16)], axis=0)


def rim(h, at16):
    high, low = parts(h)
    return jnp.where(
        (at16 == 3) | (at16 == 12), high.astype(jnp.float32),
        jnp.where((at16 == 4) | (at16 == 13), pltpu.roll(low.astype(jnp.float32), 1, 1), 0.0),
    )


def west_and_east(x, edges, weights):
    high, low = parts(x)
    rims = jnp.concatenate(edges, axis=0).astype(jnp.bfloat16)
    return jnp.dot(jnp.concatenate([high, low, rims], axis=1), weights, preferred_element_type=jnp.float32)


def kernel(
    sectors, bands,
    tracer_h, wind_east_h, wind_north_h, kappa_h, cutoff_h, partner_h, table_h,
    stack, scaled, coupling, side, side_scaled, side_coupling, side_cross,
    tr, we, wn, ka, cutoff, partner, table, load_s,
    send_a, recv_a, pole_send, pole_recv, send_d, recv_d, beyond_fix,
    rim_send, rim_recv, kap_send, kap_recv, kap_diag, adv_send, adv_recv, adv_diag, corner, invert, side_tiles, side_invert, early, early_scaled,
    a_s, a_r, b_s, b_r, d_s, d_r, x_s, x_r, k_s, k_r, f_s, f_r,
):
    lev, rows, width = we.shape
    field = stack.at[0]
    pole = cutoff.shape[1] // 2
    share = lev * pole // sectors
    slices = sectors // lev
    half = sectors // 2
    groups = rows // 8
    lat = lax.axis_index("lat")
    lon = lax.axis_index("lon")
    last = lat == bands - 1
    north = lat == 0
    polar = north | last

    def sector(offset):
        return lax.rem(lon + (offset % sectors), sectors)

    def band(offset):
        return lax.rem(lat + (offset % bands), bands)

    body = pl.ds(PAD, rows)
    held = (tracer_h, wind_east_h, wind_north_h, kappa_h, partner_h, cutoff_h, table_h)
    near = (tr.at[:, body, :], we, wn, ka.at[:, body, :], partner, cutoff, table)
    loads = [pltpu.make_async_copy(h, v, load_s.at[i]) for i, (h, v) in enumerate(zip(held, near))]
    for load in loads[:3]:
        load.start()

    barrier = pltpu.get_barrier_semaphore()
    for t in range(1, sectors):
        pl.semaphore_signal(barrier, inc=1, device_id=(lat, sector(t)), device_id_type=MESH)
    beside = (1,) if bands == 2 else (1, -1)
    for t in beside:
        for i in (-1, 0, 1):
            pl.semaphore_signal(barrier, inc=1, device_id=(band(t), sector(i)), device_id_type=MESH)

    for load in loads[3:]:
        load.start()

    lane = lax.broadcasted_iota(jnp.int32, (8, width), 1)
    row8 = lax.broadcasted_iota(jnp.int32, (8, width), 0)
    zero = jnp.zeros((8, width), jnp.float32)

    def roll(x, by):
        by = by % width
        return x if by == 0 else pltpu.roll(x, by, 1)

    def swapped(v0, v1):
        low = lane < width // 2
        v0, v1 = jnp.where(low, v0, roll(v1, width // 2)), jnp.where(low, roll(v0, width // 2), v1)
        out = []
        for v in (v0, v1):
            for b in (2, 1, 0):
                step, hop = 1 << b, 8 << b
                upper = (lane & hop) != 0
                same = ((row8 >> b) & 1) == ((lane >> (3 + b)) & 1)
                v = jnp.where(
                    same, v,
                    jnp.where(upper, pltpu.roll(roll(v, hop), 8 - step, 0), pltpu.roll(roll(v, -hop), step, 0)),
                )
            out.append(v)
        return out

    base = pl.multiple_of(jnp.where(last, rows - pole, 0), 8)
    tip = jnp.where(last, rows - 1, 0)
    tip_tile = pl.multiple_of(jnp.where(last, rows - 8, 0), 8)
    tip_slice = jnp.where(last, slices - 1, 0)
    keeper = lax.rem(lon, slices) == tip_slice

    @pl.when(north)
    def _():
        for l in range(lev):
            tr[l, PAD - 8 : PAD, :] = zero

    @pl.when(last)
    def _():
        for l in range(lev):
            tr[l, PAD + rows : PAD + rows + 8, :] = zero

    for load in loads[:3]:
        load.wait()
    lane_p = lax.broadcasted_iota(jnp.int32, (pole, width), 1)
    row_p = lax.broadcasted_iota(jnp.int32, (pole, width), 0)
    before = jnp.where(last, rows - pole - 1, 0)
    after = jnp.where(last, rows - 1, pole)
    eight = lane & 7
    packs = [zero, zero]
    for l in range(lev):
        x = tr[l, pl.ds(base + PAD, pole), :]
        east_wind = we[l, pl.ds(base, pole), :]
        w = jnp.where(lane_p == 0, 0.0, pltpu.roll(x, 1, 1))
        e = jnp.where(lane_p == width - 1, 0.0, pltpu.roll(x, width - 1, 1))
        above = jnp.where(last, tr[l, pl.ds(PAD + before, 1), :], 0.0)
        below = jnp.where(last, 0.0, tr[l, pl.ds(PAD + after, 1), :])
        u = jnp.where(row_p == 0, above, pltpu.roll(x, 1, 0))
        d = jnp.where(row_p == pole - 1, below, pltpu.roll(x, pole - 1, 0))
        stage = x - COURANT * 0.5 * (east_wind * (e - w) + wn[l, pl.ds(base, pole), :] * (d - u))
        for q in range(slices):
            k = l * slices + q
            send_a[k * DEEP : k * DEEP + share, :] = stage[q * share : (q + 1) * share]
            for h in range(2):
                at = q * share + 8 * h
                t = jnp.where(
                    (eight == 3) | (eight == 4), roll(x[at : at + 8], 4 + 8 * k), roll(east_wind[at : at + 8], 6 + 8 * k)
                )
                packs[h] = jnp.where((lane >> 3) == k, t, packs[h])
    for h, v in enumerate(swapped(*packs)):
        send_a[pl.ds(8 * h * DEEP + share, 8, stride=DEEP), :] = v

    def across(src, dst, count, ss, rs):
        for t in range(1, sectors):
            there = sector(t)
            pltpu.make_async_remote_copy(
                src_ref=src.at[pl.ds(pl.multiple_of(there * DEEP, 8), count), :],
                dst_ref=dst.at[pl.ds(pl.multiple_of(lon * DEEP, 8), count), :],
                send_sem=ss, recv_sem=rs, device_id=(lat, there), device_id_type=MESH,
            ).start()

    def bulk(count, sem):
        whole = send_d.at[pl.ds(0, count), :]
        return pltpu.make_async_remote_copy(
            src_ref=whole, dst_ref=whole, send_sem=sem, recv_sem=sem, device_id=(lat, sector(1)), device_id_type=MESH
        )

    def split_wait(single, double, sem, send):
        for here, count in ((polar, single), (jnp.logical_not(polar), double)):
            @pl.when(here)
            def _(count=count):
                if send:
                    bulk(count, sem).wait_send()
                else:
                    bulk(count, sem).wait_recv()

    four = lane >> 2

    def packed(tiles):
        first, second = zero, zero
        for g, x in enumerate(tiles):
            z = roll(x, 4 * g + 4)
            first = jnp.where(four == g, z, first)
            second = jnp.where(four == (g + 1) % groups, z, second)
        return first, second

    def pack_rims(source, target):
        def one(l, carry):
            at = pl.multiple_of(8 * l, 8)
            first, second = packed([source[l, PAD + 8 * g : PAD + 8 * g + 8, :] for g in range(groups)])
            target[0, pl.ds(at, 8), :] = first
            target[1, pl.ds(at, 8), :] = second
            return carry

        lax.fori_loop(0, lev, one, 0)

    def sideways(src, dst, ss, rs):
        for j in range(2):
            pltpu.make_async_remote_copy(
                src_ref=src.at[j], dst_ref=dst.at[j], send_sem=ss, recv_sem=rs,
                device_id=(lat, sector(1 - 2 * j)), device_id_type=MESH,
            ).start()

    def poleward(ref, ss, rs, send=None, recv=None):
        for i, step in enumerate((1, -1)):
            plan = [
                (
                    ref.at[:, pl.ds(PAD + rows - 8 if step == 1 else PAD, 8), :],
                    ref.at[:, pl.ds(PAD - 8 if step == 1 else PAD + rows, 8), :], 0,
                )
            ]
            if send is not None:
                plan += [(send.at[j], recv.at[2 * i + j], 1 - 2 * j) for j in range(2)]

            @pl.when(lat < bands - 1 if step == 1 else lat > 0)
            def _(step=step, plan=plan):
                for src, dst, aside in plan:
                    pltpu.make_async_remote_copy(
                        src_ref=src, dst_ref=dst, send_sem=ss, recv_sem=rs,
                        device_id=(band(step), sector(aside)), device_id_type=MESH,
                    ).start()

    unit = 8 * lev
    pack_rims(tr, rim_send)
    pl.semaphore_wait(barrier, sectors - 1 + 3 * len(beside))
    sideways(rim_send, rim_recv, x_s, x_r)
    poleward(tr, x_s, x_r)
    across(send_a, recv_a, share + 1, a_s, a_r)

    loads[3].wait()
    for l in range(lev):
        pole_send[16 * l : 16 * l + 8, :] = ka[l, pl.ds(tip_tile + PAD, 8), :]
        pole_send[16 * l + 8 : 16 * l + 9, :] = tr[l, pl.ds(tip + PAD, 1), :]
        pole_send[16 * l + 9 : 16 * l + 10, :] = wn[l, pl.ds(tip, 1), :]

    def pole_copy(l):
        return pltpu.make_async_remote_copy(
            src_ref=pole_send.at[pl.ds(16 * l, 10), :], dst_ref=pole_recv.at[pl.ds(pl.multiple_of(16 * lon, 8), 10), :],
            send_sem=b_s, recv_sem=b_r,
            device_id=(lat, l * slices + tip_slice), device_id_type=MESH,
        )

    for l in range(lev):
        @pl.when(lon != l * slices + tip_slice)
        def _(l=l):
            pole_copy(l).start()

        @pl.when(lon == l * slices + tip_slice)
        def _(l=l):
            pole_recv[pl.ds(pl.multiple_of(16 * lon, 8), 8), :] = pole_send[16 * l : 16 * l + 8, :]
            pole_recv[pl.ds(pl.multiple_of(16 * lon, 8) + 8, 2), :] = pole_send[16 * l + 8 : 16 * l + 10, :]

    pack_rims(ka, kap_send)
    sideways(kap_send, kap_recv, k_s, k_r)
    poleward(ka, k_s, k_r, kap_send, kap_diag)
    for load in loads[4:]:
        load.wait()

    start = lax.broadcasted_iota(jnp.int32, (sectors, width), 0) + half
    reach = partner[...] - jnp.where(start >= sectors, start - sectors, start) * width
    reach = jnp.where(reach < 0, reach + sectors * width, reach)
    farther = reach >= width
    at_lane = jnp.where(farther, reach - width, reach)

    def crossed(points):
        return jnp.where(
            farther, taken(pltpu.roll(points, sectors - half - 1, 0), at_lane), taken(pltpu.roll(points, half, 0), at_lane)
        )


    change = change_weights(width)
    split_wait(3 * unit, 4 * unit, x_r, False)
    for l in range(lev):
        edge = jnp.where((lane & 3) == 3, rim_recv[0, 8 * l : 8 * l + 8, :], roll(rim_recv[1, 8 * l : 8 * l + 8, :], -2))
        high, low = parts(edge)
        edge = jnp.where((lane & 3) >= 2, high.astype(jnp.float32), roll(low.astype(jnp.float32), -2))
        across_east = west_and_east(
            tr[l, PAD : PAD + rows, :], [jnp.where(four == g, edge, 0.0) for g in range(groups)], change
        )
        tiles = []
        for g in range(groups):
            at = PAD + 8 * g
            x = tr[l, at : at + 8, :]
            turn = wn[l, 8 * g : 8 * g + 8, :] * (tr[l, at + 1 : at + 9, :] - tr[l, at - 1 : at + 7, :])
            push = we[l, 8 * g : 8 * g + 8, :] * across_east[8 * g : 8 * g + 8]
            value = x - COURANT * 0.5 * (push + turn)
            field[l, at : at + 8, :] = value
            k = ka[l, at : at + 8, :]
            inverse = 1.0 / (1.0 + 4.0 * k)
            invert[l, at : at + 8, :] = inverse
            coupling[l, at : at + 8, :] = k * inverse
            scaled[l, at : at + 8, :] = value * inverse
            tiles.append(value)
        first, second = packed(tiles)
        adv_send[0, 8 * l : 8 * l + 8, :] = first
        adv_send[1, 8 * l : 8 * l + 8, :] = second

    def sided(send, recv, at, put):
        for kk in range(4):
            mine = (four & 3) == kk
            near_west = jnp.where(mine, recv[0, at : at + 8, :], send[1, at : at + 8, :])
            near_east = jnp.where(mine, send[0, at : at + 8, :], recv[1, at : at + 8, :])
            put(kk, jnp.where((lane & 15) < 8, roll(near_west, -4 * kk), roll(near_east, 8 - 4 * kk)))

    sideways(adv_send, adv_recv, f_s, f_r)
    poleward(field, f_s, f_r, adv_send, adv_diag)

    beyond_fix[...] = jnp.zeros_like(beyond_fix)

    @pl.when(keeper)
    def _():
        bulk(10 * (sectors - 1), b_r).wait_recv()
        tips = jnp.concatenate([pole_recv[16 * d + 8 : 16 * d + 9, :] for d in range(sectors)], axis=0)
        winds = jnp.concatenate([pole_recv[16 * d + 9 : 16 * d + 10, :] for d in range(sectors)], axis=0)
        turned = COURANT * 0.5 * winds * crossed(tips)
        beyond_fix[...] = jnp.where(last, -turned, turned)

    first = jnp.where(last, pole, 0) + lax.rem(lon, slices) * share
    spot = lax.broadcasted_iota(jnp.int32, (share, 2 * pole), 0) + first
    limit = jnp.sum(
        jnp.where(
            lax.broadcasted_iota(jnp.int32, (share, 2 * pole), 1) == spot,
            cutoff[...].astype(jnp.float32), 0.0,
        ),
        axis=1, keepdims=True,
    )
    kept = 2 * KMAX // sectors
    slot = lax.broadcasted_iota(jnp.int32, (share, 2 * kept), 1)
    wave = sectors * (jnp.where(slot < kept, slot, slot - kept) - kept // 2)
    own = pl.multiple_of(lon * DEEP, 8)
    recv_a[pl.ds(own, share), :] = send_a[pl.ds(own, share), :]
    recv_a[pl.ds(own + share, 1), :] = send_a[pl.ds(own + share, 1), :]
    bulk((share + 1) * (sectors - 1), a_r).wait_recv()
    tw_cos, tw_sin = table[0 : half + 1, :], table[16 : half + 17, :]
    fwd = table[32 : 32 + 2 * width, :]
    inv = jnp.concatenate([table[32 + 2 * width : 32 + 3 * width, :], table[32 + 3 * width : 32 + 4 * width, :]], axis=1)

    def rows_of(ref, at):
        return [ref[pl.ds(8 * h * DEEP + at, 8, stride=DEEP), :] for h in range(2)]

    fixes = []
    for v in swapped(*rows_of(recv_a, share)):
        fixes.append(COURANT * 0.5 * v * jnp.where(eight == 6, roll(v, 11), -roll(v, -7)))
    at_tip = [(row8 == 0) & north & keeper, (row8 == 7) & last & keeper]
    ends = (lane == 0) | (lane == width - 1)
    spread = []
    for d in range(sectors):
        halves = []
        for h in range(2):
            x = recv_a[d * DEEP + 8 * h : d * DEEP + 8 * h + 8, :]
            x = x + jnp.where(ends, roll(fixes[h], -(8 * d + 6)), 0.0)
            halves.append(x + jnp.where(at_tip[h], beyond_fix[d : d + 1, :], 0.0))
        spread.append(jnp.concatenate(halves, axis=0))

    def circle(d, k):
        angle = 2.0 * math.pi * ((d * k) % sectors) / sectors
        return math.cos(angle), math.sin(angle)

    even = [spread[0]] + [spread[d] + spread[sectors - d] for d in range(1, half)] + [spread[half]]
    odd = [None] + [spread[d] - spread[sectors - d] for d in range(1, half)]
    blocks = []
    for k in range(half + 1):
        c, s = tw_cos[k : k + 1, :], tw_sin[k : k + 1, :]
        re = weighted([(circle(d, k)[0], even[d]) for d in range(half + 1)])
        im = weighted([(-circle(d, k)[1], odd[d]) for d in range(1, half)])
        if im is None:
            blocks.append(jnp.concatenate([re * c, -(re * s)], axis=1))
        else:
            blocks.append(jnp.concatenate([re * c + im * s, im * c - re * s], axis=1))
    spectrum = jnp.dot(
        jnp.concatenate(blocks, axis=0), fwd, precision=HIGHEST, preferred_element_type=jnp.float32
    )
    keep = jnp.concatenate(
        [jnp.where(jnp.abs(wave + k).astype(jnp.float32) <= limit, 1.0, 0.0) for k in range(half + 1)], axis=0
    )
    back = jnp.dot(
        jnp.where(keep > 0.0, spectrum, 0.0), inv, precision=HIGHEST, preferred_element_type=jnp.float32
    )
    real, imag = [], []
    for k in range(half + 1):
        c, s = tw_cos[k : k + 1, :], tw_sin[k : k + 1, :]
        zr = back[k * share : (k + 1) * share, :width]
        zi = back[k * share : (k + 1) * share, width:]
        twice = 1.0 if k in (0, half) else 2.0
        real.append((zr * c - zi * s) * twice)
        imag.append((zr * s + zi * c) * twice)
    smooth = [None] * sectors
    for d in range(half + 1):
        p = weighted([(circle(d, k)[0], real[k]) for k in range(half + 1)])
        q = weighted([(circle(d, k)[1], imag[k]) for k in range(1, half)])
        if q is None:
            smooth[d] = p
        else:
            smooth[d], smooth[sectors - d] = p - q, p + q
    edges = [zero, zero]
    for d in range(sectors):
        send_d[d * DEEP : d * DEEP + share, :] = smooth[d]
        for h in range(2):
            edges[h] = jnp.where((lane >> 3) == d, roll(smooth[d][8 * h : 8 * h + 8], 8 * d + 4), edges[h])
    beyond = [jnp.where(eight < 4, roll(v, 8), roll(v, -8)) for v in edges]
    for i in range(2):
        west, east = (beyond, edges) if i == 0 else (edges, beyond)
        for h, v in enumerate(swapped(*[jnp.where(eight < 4, w, e) for w, e in zip(west, east)])):
            send_d[pl.ds(8 * h * DEEP + share + i, 8, stride=DEEP), :] = v

    extra = share + 2 + SWEEPS + 1

    def put_cross(t, rows16):
        for h in range(2):
            send_d[pl.ds(8 * h * DEEP + share + 2 + t, 8, stride=DEEP), :] = rows16[8 * h : 8 * h + 8]

    @pl.when(keeper)
    def _():
        now, inverse, pull = [], [], []
        for d in range(sectors):
            top, low = d * DEEP, d * DEEP + 8
            now.append(jnp.where(last, send_d[low : low + 8, :], send_d[top : top + 8, :]))
            k = pole_recv[16 * d : 16 * d + 8, :]
            inverse.append(1.0 / (1.0 + 4.0 * k))
            pull.append(k * inverse[d])
        source = [a * b for a, b in zip(now, inverse)]
        ends = jnp.zeros((sectors, width), jnp.float32)
        wide = lax.broadcasted_iota(jnp.int32, (sectors, width), 1)
        for t in range(SWEEPS):
            tips = jnp.concatenate([jnp.where(last, x[7:8], x[0:1]) for x in now], axis=0)
            over = crossed(tips)
            put_cross(t, over)
            z = roll(over, 8 * t + 4)
            z = jnp.where((wide & 7) < 4, pltpu.roll(z, 1, 0), pltpu.roll(z, sectors - 1, 0))
            ends = jnp.where((wide >> 3) == t, z, ends)
            if t < SWEEPS - 1:
                right, left = [roll(x, 1) for x in now], [roll(x, -1) for x in now]
                later = []
                for d in range(sectors):
                    w = jnp.where(lane == 0, right[d - 1], right[d])
                    e = jnp.where(lane == width - 1, left[(d + 1) % sectors], left[d])
                    u = jnp.where((row8 == 0) & jnp.logical_not(last), over[d : d + 1], pltpu.roll(now[d], 1, 0))
                    b = jnp.where((row8 == 7) & last, over[d : d + 1], pltpu.roll(now[d], 7, 0))
                    later.append(source[d] + pull[d] * (w + e + u + b))
                now = later
        put_cross(SWEEPS, ends)
        across(send_d, recv_d, extra, d_s, d_r)

    @pl.when(jnp.logical_not(keeper))
    def _():
        across(send_d, recv_d, share + 2, d_s, d_r)

    recv_d[pl.ds(own, share), :] = send_d[pl.ds(own, share), :]
    recv_d[pl.ds(own + share, 2), :] = send_d[pl.ds(own + share, 2), :]

    @pl.when(keeper)
    def _():
        recv_d[pl.ds(own + share + 2, SWEEPS + 1), :] = send_d[pl.ds(own + share + 2, SWEEPS + 1), :]

    split_wait(5 * unit, 8 * unit, k_r, False)

    def corners(ref, diag, l):
        top, bottom = ref[l, PAD - 8 : PAD, :], ref[l, PAD + rows : PAD + rows + 8, :]
        nw, ne, sw, se = [diag[i, 8 * l : 8 * l + 8, :] for i in range(4)]
        first = jnp.where(
            lane < 8, roll(jnp.where(lane >= width - 4, nw, top), 4), roll(jnp.where(lane < 4, ne, top), 12)
        )
        second = jnp.where(
            lane < width - 8,
            jnp.where(lane < width - 12, roll(sw, -16), roll(bottom, -12)),
            jnp.where(lane < width - 4, roll(bottom, -4), roll(se, -8)),
        )
        return first, second

    def capped(first_tile, last_tile, first, second):
        return jnp.where(lane < 16, first, roll(last_tile, 16)), jnp.where(lane >= width - 16, second, roll(first_tile, -16))

    for l in range(lev):
        tiles = []

        def put(kk, tile, l=l, tiles=tiles):
            side_invert[l, 12 + 8 * kk : 20 + 8 * kk, :] = tile
            tiles.append(tile)

        sided(kap_send, kap_recv, 8 * l, put)
        top, bottom = capped(tiles[0], tiles[3], *corners(ka, kap_diag, l))
        side_invert[l, 4:12, :] = top
        side_invert[l, 44:52, :] = bottom
        for j in range(5):
            at = 8 + 8 * j
            k = side_invert[l, at : at + 8, :]
            inverse = 1.0 / (1.0 + 4.0 * k)
            side_invert[l, at : at + 8, :] = inverse
            side_coupling[l, at : at + 8, :] = k * inverse
    split_wait(5 * unit, 8 * unit, f_r, False)
    for l in range(lev):
        for at in (PAD - 8, PAD + rows):
            k = ka[l, at : at + 8, :]
            inverse = 1.0 / (1.0 + 4.0 * k)
            coupling[l, at : at + 8, :] = k * inverse
            scaled[l, at : at + 8, :] = field[l, at : at + 8, :] * inverse

        def put(kk, tile, l=l):
            side_tiles[32 * l + 8 * kk : 32 * l + 8 * kk + 8, :] = tile

        sided(adv_send, adv_recv, 8 * l, put)
        corner[0, 8 * l : 8 * l + 8, :], corner[1, 8 * l : 8 * l + 8, :] = corners(field, adv_diag, l)
        at = 32 * l
        early[0, l, 12:44, :] = side_tiles[at : at + 32, :]
        early[0, l, 4:12, :], early[0, l, 44:52, :] = capped(
            side_tiles[at : at + 8, :], side_tiles[at + 24 : at + 32, :],
            corner[0, 8 * l : 8 * l + 8, :], corner[1, 8 * l : 8 * l + 8, :],
        )
        early_scaled[l, 8:48, :] = early[0, l, 8:48, :] * side_invert[l, 8:48, :]

    weights = shift_weights(width)
    order = [(0, -1)] + [(i // 4, i % 4) for i in range(groups)] + [(groups // 4 - 1, 4)]
    at16 = lane & 15

    def sweep_early(t, carry):
        for l in range(lev):
            ends = {kk: rim(early[t, l, 12 + 8 * kk : 20 + 8 * kk, :], at16) for kk in range(-1, 5)}
            total = west_and_east(
                stack[t, l, PAD - 8 : PAD + rows + 8, :],
                [jnp.where((lane >> 4) == g, ends[kk], 0.0) for g, kk in order], weights,
            )
            for i in range(groups + 2):
                at = PAD - 8 + 8 * i
                value = total[8 * i : 8 * i + 8] + (stack[t, l, at - 1 : at + 7, :] + stack[t, l, at + 1 : at + 9, :])
                stack[t + 1, l, at : at + 8, :] = scaled[l, at : at + 8, :] + coupling[l, at : at + 8, :] * value
            for j in range(5):
                at = 8 + 8 * j
                x = early[t, l, at : at + 8, :]
                value = roll(x, 1) + roll(x, -1) + early[t, l, at - 1 : at + 7, :] + early[t, l, at + 1 : at + 9, :]
                early[t + 1, l, at : at + 8, :] = (
                    early_scaled[l, at : at + 8, :] + side_coupling[l, at : at + 8, :] * value
                )
        return carry

    lax.fori_loop(0, SWEEPS, sweep_early, 0)

    plain_rows, more = (share + 2) * (sectors - 1), SWEEPS + 1
    d_waits = ((keeper, plain_rows + more * (lev - 1)), (jnp.logical_not(keeper), plain_rows + more * lev))
    for here, count in d_waits:
        @pl.when(here)
        def _(count=count):
            bulk(count, d_r).wait_recv()

    def cross(l, t):
        return recv_d[pl.ds((l * slices + tip_slice) * DEEP + share + 2 + t, 1), :]

    @pl.when(polar)
    def _():
        for k in range(sectors):
            l, q = k // slices, k % slices
            x = recv_d[k * DEEP : k * DEEP + share, :]
            at = base + PAD + q * share
            field[l, pl.ds(at, share), :] = x
            scaled[l, pl.ds(at, share), :] = x * invert[l, pl.ds(at, share), :]

    @pl.when(north)
    def _():
        for l in range(lev):
            field[l, PAD - 1 : PAD, :] = cross(l, 0)

    @pl.when(last)
    def _():
        for l in range(lev):
            field[l, PAD + rows : PAD + rows + 1, :] = cross(l, 0)

    halo = jnp.concatenate([cross(l, SWEEPS) for l in range(lev)] * 2, axis=0)
    for t in range(SWEEPS):
        plain = jnp.concatenate([cross(l, t) for l in range(lev)] * 2, axis=0)
        z = jnp.where(
            lane < 8,
            jnp.where(lane < 4, roll(halo, -8 * t), roll(plain, 4)),
            jnp.where(lane < 12, roll(plain, 12), roll(halo, 8 - 8 * t)),
        )
        side_cross[t, :8, :] = jnp.where(last, roll(z, -16), z)
        side_cross[t, 8:, :] = plain

    strips = [
        [jnp.where(last, roll(v, -32), v) for v in swapped(*rows_of(recv_d, share + i))] for i in range(2)
    ]
    from_cap = jnp.where(last, lane - (width - 32), lane)
    inside_cap = polar & (from_cap >= 0) & (from_cap < 32)
    top_spot = north & (row8 == 7) & (lane < 16)
    bottom_spot = last & (row8 == 0) & (lane >= width - 16)
    for l in range(lev):
        tiles = []
        for kk in range(4):
            h, by = kk % 2, -32 * l - 8 * (kk // 2)
            z = jnp.where((lane & 15) < 8, roll(strips[0][h], by), roll(strips[1][h], by + 8))
            tile = jnp.where(inside_cap, z, side_tiles[32 * l + 8 * kk : 32 * l + 8 * kk + 8, :])
            side[l, 12 + 8 * kk : 20 + 8 * kk, :] = tile
            tiles.append(tile)
        at = 8 * l
        top, bottom = capped(tiles[0], tiles[3], corner[0, at : at + 8, :], corner[1, at : at + 8, :])
        side[l, 4:12, :] = jnp.where(top_spot, side_cross[0, l : l + 1, :], top)
        side[l, 44:52, :] = jnp.where(bottom_spot, side_cross[0, l : l + 1, :], bottom)
        for j in range(5):
            at = 8 + 8 * j
            side_scaled[l, at : at + 8, :] = side[l, at : at + 8, :] * side_invert[l, at : at + 8, :]

    bulk((share + 1) * (sectors - 1), a_s).wait_send()
    split_wait(3 * unit, 4 * unit, x_s, True)
    split_wait(5 * unit, 8 * unit, k_s, True)
    split_wait(5 * unit, 8 * unit, f_s, True)
    for here, pole_rows, rows_out in (
        (keeper, 10 * (lev - 1), extra * (sectors - 1)), (jnp.logical_not(keeper), 10 * lev, plain_rows)
    ):
        @pl.when(here)
        def _(pole_rows=pole_rows, rows_out=rows_out):
            bulk(pole_rows, b_s).wait_send()
            bulk(rows_out, d_s).wait_send()


def relax(
    bands, stack, scaled, coupling, side0, side_scaled, side_coupling, side_cross, filtered, balanced, local, side, sems
):
    lev, rows, width = filtered.shape
    near = local.shape[2] - 2 * PAD
    tiles = near // 8 + 2
    lat = lax.axis_index("lat")
    north, last = lat == 0, lat == bands - 1
    base = pl.multiple_of(jnp.where(last, rows - near, 0), 8)
    rest = pl.multiple_of(jnp.where(last, 0, near), 8)
    copies = [
        pltpu.make_async_copy(stack.at[0, :, pl.ds(PAD, rows), :], filtered, sems.at[0]),
        pltpu.make_async_copy(
            stack.at[SWEEPS, :, pl.ds(rest + PAD, rows - near), :], balanced.at[:, pl.ds(rest, rows - near), :], sems.at[1]
        ),
    ]
    for copy in copies:
        copy.start()
    lane = lax.broadcasted_iota(jnp.int32, (8, width), 1)
    row8 = lax.broadcasted_iota(jnp.int32, (8, width), 0)
    at16 = lane & 15
    group = (lane >> 4) - jnp.where(last, (rows - near) // 32, 0)
    weights = shift_weights(width)
    for l in range(lev):
        local[0, l, PAD - 8 : PAD + near + 8, :] = stack[0, l, pl.ds(base + PAD - 8, near + 16), :]
    for t in range(SWEEPS):
        beside = side0 if t == 0 else side.at[t - 1]
        edges = []
        for l in range(lev):
            ends = {kk: rim(beside[l, 12 + 8 * kk : 20 + 8 * kk, :], at16) for kk in range(-1, 5)}
            edges.append(jnp.where(lane < 16, ends[-1], 0.0))
            for i in range(near // 8):
                edges.append(jnp.where(group == i // 4, ends[i % 4], 0.0))
            edges.append(jnp.where(lane >= width - 16, ends[4], 0.0))
        whole = jnp.concatenate([local[t, l, PAD - 8 : PAD + near + 8, :] for l in range(lev)], axis=0)
        total = west_and_east(whole, edges, weights)
        for l in range(lev):
            for i in range(tiles):
                at = PAD - 8 + 8 * i
                start = 8 * (tiles * l + i)
                value = total[start : start + 8] + (local[t, l, at - 1 : at + 7, :] + local[t, l, at + 1 : at + 9, :])
                there = pl.ds(base + at, 8)
                value = scaled[l, there, :] + coupling[l, there, :] * value
                if t < SWEEPS - 1 and i in (0, tiles - 1):
                    cross = side_cross[t + 1, 8 + l : 9 + l, :]
                    if i == 0:
                        at_end = rows - near + PAD - 8
                        value = jnp.where(north & (row8 == 7), cross, value)
                        value = jnp.where(last, stack[t + 1, l, at_end : at_end + 8, :], value)
                    else:
                        at_end = near + PAD
                        value = jnp.where(
                            last, jnp.where(row8 == 0, cross, value), stack[t + 1, l, at_end : at_end + 8, :]
                        )
                local[t + 1, l, at : at + 8, :] = value
        if t == SWEEPS - 1:
            break
        for l in range(lev):
            for j in range(5):
                at = 8 + 8 * j
                x = beside[l, at : at + 8, :]
                value = pltpu.roll(x, 1, 1) + pltpu.roll(x, width - 1, 1)
                value = value + (beside[l, at - 1 : at + 7, :] + beside[l, at + 1 : at + 9, :])
                x = side_scaled[l, at : at + 8, :] + side_coupling[l, at : at + 8, :] * value
                cross = side_cross[t + 1, l : l + 1, :]
                if j == 0:
                    x = jnp.where(north & (row8 == 3) & (lane < 16), cross, x)
                if j == 4:
                    x = jnp.where(last & (row8 == 4) & (lane >= width - 16), cross, x)
                side[t, l, at : at + 8, :] = x
    copy = pltpu.make_async_copy(
        local.at[SWEEPS, :, pl.ds(PAD, near), :], balanced.at[:, pl.ds(base, near), :], sems.at[2]
    )
    copy.start()
    for copy in (*copies, copy):
        copy.wait()


def solution(mesh):
    sectors, bands = mesh.shape["lon"], mesh.shape["lat"]

    def per_device(tracer, wind_east, wind_north, kappa, cutoff, partner):
        lev, rows, width = tracer.shape
        f32 = jnp.float32
        high = rows + 2 * PAD

        def array(*shape):
            return pltpu.VMEM(shape, f32)

        block, tall = array(lev, rows, width), array(lev, high, width)
        strips = array(sectors * DEEP, width)
        pair, four = array(2, lev * 8, width), array(4, lev * 8, width)
        narrow = array(lev, 56, width)
        vmem = pl.BlockSpec(memory_space=pltpu.VMEM)
        hbm = pl.BlockSpec(memory_space=pltpu.HBM)
        tw_cos, tw_sin, fwd, inv = tables(sectors, width)
        blank = np.zeros((16 - tw_cos.shape[0], width), np.float32)
        table = np.concatenate([tw_cos, blank, tw_sin, blank, fwd, inv[:, :width], inv[:, width:]], axis=0)
        small = (cutoff.reshape(1, -1), partner.reshape(sectors, width), table)
        dma = pltpu.SemaphoreType.DMA
        made = [(SWEEPS + 1, lev, high, width)] + [(lev, high, width)] * 2 + [(lev, 56, width)] * 3 + [(SWEEPS, 16, width)]
        limit = 24 * 1024 * 1024
        near = cutoff.shape[0] // 2 + 32
        held = pl.pallas_call(
            functools.partial(kernel, sectors, bands),
            out_shape=[jax.ShapeDtypeStruct(shape, f32) for shape in made],
            in_specs=[hbm] * 7,
            out_specs=[vmem] * len(made),
            scratch_shapes=[
                tall, block, block, tall,
                *[pltpu.VMEM(a.shape, a.dtype) for a in small],
                dma((7,)),
                strips, strips, array(16 * lev, width), array(16 * sectors, width), strips, strips,
                array(sectors, width),
                pair, pair, pair, pair, four, pair, pair, four, pair, tall, array(lev * 32, width), narrow, array(SWEEPS + 1, lev, 56, width), narrow,
                *[dma] * 12,
            ],
            compiler_params=pltpu.CompilerParams(collective_id=0, has_side_effects=True, vmem_limit_bytes=limit),
        )(
            *[pltpu.with_memory_space_constraint(jnp.asarray(a), pltpu.HBM) for a in (tracer, wind_east, wind_north, kappa, *small)]
        )
        return pl.pallas_call(
            functools.partial(relax, bands),
            out_shape=[jax.ShapeDtypeStruct(tracer.shape, f32)] * 2,
            in_specs=[vmem] * len(made),
            out_specs=[hbm] * 2,
            scratch_shapes=[array(SWEEPS + 1, lev, near + 2 * PAD, width), array(SWEEPS - 1, lev, 56, width), dma((3,))],
            compiler_params=pltpu.CompilerParams(vmem_limit_bytes=limit),
        )(*[pltpu.with_memory_space_constraint(a, pltpu.VMEM) for a in held])

    spec = P(None, "lat", "lon")
    return jax.shard_map(
        per_device, mesh=mesh, in_specs=(spec, spec, spec, spec, P(), P()), out_specs=(spec, spec),
        check_vma=False,
    )
```

```python
import functools
import math

import jax
import jax.numpy as jnp
import numpy as np
from jax import lax
from jax.experimental import pallas as pl
from jax.experimental.pallas import tpu as pltpu
from jax.sharding import PartitionSpec as P

KMAX = 512
SWEEPS = 4
COURANT = 0.4
HIGHEST = lax.Precision.HIGHEST


def tables(sectors, width):
    total = sectors * width
    half = sectors // 2
    m = np.arange(width)
    theta = 2.0 * np.pi * (np.outer(np.arange(half + 1), m) % total) / total
    kept = 2 * KMAX // sectors
    k2 = np.arange(kept) - kept // 2
    phase = 2.0 * np.pi * (np.outer(m, k2) % width) / width
    c, s = np.cos(phase), np.sin(phase)
    forward = np.block([[c, -s], [s, c]])
    inverse = np.block([[c.T, s.T], [-s.T, c.T]]) / total
    return [a.astype(np.float32) for a in (np.cos(theta), np.sin(theta), forward, inverse)]


def weighted(terms):
    total = None
    for factor, value in terms:
        if abs(factor) < 1e-12:
            continue
        part = value if abs(factor - 1.0) < 1e-12 else value * np.float32(factor)
        total = part if total is None else total + part
    return total


PAD = 16
DEEP = 24
MESH = pl.DeviceIdType.MESH


def taken(x, at_lane):
    return jnp.take_along_axis(x, at_lane, axis=1, mode="promise_in_bounds")


def parts(x):
    high = x.astype(jnp.bfloat16)
    return high, (x - high.astype(jnp.float32)).astype(jnp.bfloat16)


def shift_weights(width, east, west_lane, east_lane, lanes):
    one = lax.broadcasted_iota(jnp.int32, (width, width), 0)
    two = lax.broadcasted_iota(jnp.int32, (width, width), 1)
    shift = jnp.where(one - two == 1, east, 0.0) + jnp.where(two - one == 1, 1.0, 0.0)
    spot = one & (lanes - 1)
    edge = jnp.where((two == width - 1) & (spot == east_lane), east, 0.0)
    edge = edge + jnp.where((two == 0) & (spot == west_lane), 1.0, 0.0)
    shift, edge = shift.astype(jnp.bfloat16), edge.astype(jnp.bfloat16)
    return jnp.concatenate([shift, shift, edge, edge], axis=0)


def rim(h, at16):
    high, low = parts(jnp.where((at16 == 3) | (at16 == 12), h, 0.0))
    return high.astype(jnp.float32), low.astype(jnp.float32)


def masked(here, pair):
    return [jnp.where(here, x, 0.0) for x in pair]


def west_and_east(x, edges, weights):
    high, low = parts(x)
    rims = [jnp.concatenate(tiles, axis=0).astype(jnp.bfloat16) for tiles in zip(*edges)]
    return jnp.dot(jnp.concatenate([high, low, *rims], axis=1), weights, preferred_element_type=jnp.float32)


def refined(x, weights):
    high, low = parts(x)
    return jnp.dot(jnp.concatenate([high, low, high], axis=1), weights, preferred_element_type=jnp.float32)


def kernel(
    sectors, bands,
    tracer_h, wind_east_h, wind_north_h, kappa_h, cutoff_h, partner_h, table_h, fine_h,
    stack, scaled, coupling, side, side_scaled, side_coupling, side_cross,
    tr, we, wn, ka, cutoff, partner, table, fine, load_s,
    send_a, recv_a, pole_send, pole_recv, send_d, recv_d, beyond_fix,
    rim_send, rim_recv, kap_send, kap_recv, kap_diag, adv_send, adv_recv, adv_diag, corner, invert, side_tiles, side_invert, early, early_scaled,
    a_s, a_r, b_s, b_r, d_s, d_r, x_s, x_r, k_s, k_r, f_s, f_r,
):
    lev, rows, width = we.shape
    field = stack.at[0]
    pole = cutoff.shape[1] // 2
    share = lev * pole // sectors
    slices = sectors // lev
    half = sectors // 2
    groups = rows // 8
    lat = lax.axis_index("lat")
    lon = lax.axis_index("lon")
    last = lat == bands - 1
    north = lat == 0
    polar = north | last

    def sector(offset):
        return lax.rem(lon + (offset % sectors), sectors)

    def band(offset):
        return lax.rem(lat + (offset % bands), bands)

    body = pl.ds(PAD, rows)
    held = (tracer_h, wind_east_h, wind_north_h, kappa_h, partner_h, cutoff_h, table_h, fine_h)
    near = (tr.at[:, body, :], we, wn, ka.at[:, body, :], partner, cutoff, table, fine)
    loads = [pltpu.make_async_copy(h, v, load_s.at[i]) for i, (h, v) in enumerate(zip(held, near))]
    for load in loads[:3]:
        load.start()

    barrier = pltpu.get_barrier_semaphore()
    for t in range(1, sectors):
        pl.semaphore_signal(barrier, inc=1, device_id=(lat, sector(t)), device_id_type=MESH)
    beside = (1,) if bands == 2 else (1, -1)
    for t in beside:
        for i in (-1, 0, 1):
            pl.semaphore_signal(barrier, inc=1, device_id=(band(t), sector(i)), device_id_type=MESH)

    for load in loads[3:]:
        load.start()

    lane = lax.broadcasted_iota(jnp.int32, (8, width), 1)
    row8 = lax.broadcasted_iota(jnp.int32, (8, width), 0)
    zero = jnp.zeros((8, width), jnp.float32)

    def roll(x, by):
        by = by % width
        return x if by == 0 else pltpu.roll(x, by, 1)

    def swapped(v0, v1):
        low = lane < width // 2
        v0, v1 = jnp.where(low, v0, roll(v1, width // 2)), jnp.where(low, roll(v0, width // 2), v1)
        out = []
        for v in (v0, v1):
            for b in (2, 1, 0):
                step, hop = 1 << b, 8 << b
                upper = (lane & hop) != 0
                same = ((row8 >> b) & 1) == ((lane >> (3 + b)) & 1)
                v = jnp.where(
                    same, v,
                    jnp.where(upper, pltpu.roll(roll(v, hop), 8 - step, 0), pltpu.roll(roll(v, -hop), step, 0)),
                )
            out.append(v)
        return out

    base = pl.multiple_of(jnp.where(last, rows - pole, 0), 8)
    tip = jnp.where(last, rows - 1, 0)
    tip_tile = pl.multiple_of(jnp.where(last, rows - 8, 0), 8)
    tip_slice = jnp.where(last, slices - 1, 0)
    keeper = lax.rem(lon, slices) == tip_slice

    @pl.when(north)
    def _():
        for l in range(lev):
            tr[l, PAD - 8 : PAD, :] = zero

    @pl.when(last)
    def _():
        for l in range(lev):
            tr[l, PAD + rows : PAD + rows + 8, :] = zero

    for load in loads[:3]:
        load.wait()
    lane_p = lax.broadcasted_iota(jnp.int32, (pole, width), 1)
    row_p = lax.broadcasted_iota(jnp.int32, (pole, width), 0)
    before = jnp.where(last, rows - pole - 1, 0)
    after = jnp.where(last, rows - 1, pole)
    eight = lane & 7
    packs = [zero, zero]
    for l in range(lev):
        x = tr[l, pl.ds(base + PAD, pole), :]
        east_wind = we[l, pl.ds(base, pole), :]
        w = jnp.where(lane_p == 0, 0.0, pltpu.roll(x, 1, 1))
        e = jnp.where(lane_p == width - 1, 0.0, pltpu.roll(x, width - 1, 1))
        above = jnp.where(last, tr[l, pl.ds(PAD + before, 1), :], 0.0)
        below = jnp.where(last, 0.0, tr[l, pl.ds(PAD + after, 1), :])
        u = jnp.where(row_p == 0, above, pltpu.roll(x, 1, 0))
        d = jnp.where(row_p == pole - 1, below, pltpu.roll(x, pole - 1, 0))
        stage = x - COURANT * 0.5 * (east_wind * (e - w) + wn[l, pl.ds(base, pole), :] * (d - u))
        for q in range(slices):
            k = l * slices + q
            send_a[k * DEEP : k * DEEP + share, :] = stage[q * share : (q + 1) * share]
            for h in range(2):
                at = q * share + 8 * h
                t = jnp.where(
                    (eight == 3) | (eight == 4), roll(x[at : at + 8], 4 + 8 * k), roll(east_wind[at : at + 8], 6 + 8 * k)
                )
                packs[h] = jnp.where((lane >> 3) == k, t, packs[h])
    for h, v in enumerate(swapped(*packs)):
        send_a[pl.ds(8 * h * DEEP + share, 8, stride=DEEP), :] = v

    def across(src, dst, count, ss, rs):
        for t in range(1, sectors):
            there = sector(t)
            pltpu.make_async_remote_copy(
                src_ref=src.at[pl.ds(pl.multiple_of(there * DEEP, 8), count), :],
                dst_ref=dst.at[pl.ds(pl.multiple_of(lon * DEEP, 8), count), :],
                send_sem=ss, recv_sem=rs, device_id=(lat, there), device_id_type=MESH,
            ).start()

    def bulk(count, sem):
        whole = send_d.at[pl.ds(0, count), :]
        return pltpu.make_async_remote_copy(
            src_ref=whole, dst_ref=whole, send_sem=sem, recv_sem=sem, device_id=(lat, sector(1)), device_id_type=MESH
        )

    def split_wait(single, double, sem, send):
        for here, count in ((polar, single), (jnp.logical_not(polar), double)):
            @pl.when(here)
            def _(count=count):
                if send:
                    bulk(count, sem).wait_send()
                else:
                    bulk(count, sem).wait_recv()

    four = lane >> 2

    def packed(tiles):
        first, second = zero, zero
        for g, x in enumerate(tiles):
            z = roll(x, 4 * g + 4)
            first = jnp.where(four == g, z, first)
            second = jnp.where(four == (g + 1) % groups, z, second)
        return first, second

    def pack_rims(source, target):
        def one(l, carry):
            at = pl.multiple_of(8 * l, 8)
            first, second = packed([source[l, PAD + 8 * g : PAD + 8 * g + 8, :] for g in range(groups)])
            target[0, pl.ds(at, 8), :] = first
            target[1, pl.ds(at, 8), :] = second
            return carry

        lax.fori_loop(0, lev, one, 0)

    def sideways(src, dst, ss, rs):
        for j in range(2):
            pltpu.make_async_remote_copy(
                src_ref=src.at[j], dst_ref=dst.at[j], send_sem=ss, recv_sem=rs,
                device_id=(lat, sector(1 - 2 * j)), device_id_type=MESH,
            ).start()

    def poleward(ref, ss, rs, send=None, recv=None):
        for i, step in enumerate((1, -1)):
            plan = [
                (
                    ref.at[:, pl.ds(PAD + rows - 8 if step == 1 else PAD, 8), :],
                    ref.at[:, pl.ds(PAD - 8 if step == 1 else PAD + rows, 8), :], 0,
                )
            ]
            if send is not None:
                plan += [(send.at[j], recv.at[2 * i + j], 1 - 2 * j) for j in range(2)]

            @pl.when(lat < bands - 1 if step == 1 else lat > 0)
            def _(step=step, plan=plan):
                for src, dst, aside in plan:
                    pltpu.make_async_remote_copy(
                        src_ref=src, dst_ref=dst, send_sem=ss, recv_sem=rs,
                        device_id=(band(step), sector(aside)), device_id_type=MESH,
                    ).start()

    unit = 8 * lev
    pack_rims(tr, rim_send)
    pl.semaphore_wait(barrier, sectors - 1 + 3 * len(beside))
    sideways(rim_send, rim_recv, x_s, x_r)
    poleward(tr, x_s, x_r)
    across(send_a, recv_a, share + 1, a_s, a_r)

    loads[3].wait()
    for l in range(lev):
        pole_send[16 * l : 16 * l + 8, :] = ka[l, pl.ds(tip_tile + PAD, 8), :]
        pole_send[16 * l + 8 : 16 * l + 9, :] = tr[l, pl.ds(tip + PAD, 1), :]
        pole_send[16 * l + 9 : 16 * l + 10, :] = wn[l, pl.ds(tip, 1), :]

    def pole_copy(l):
        return pltpu.make_async_remote_copy(
            src_ref=pole_send.at[pl.ds(16 * l, 10), :], dst_ref=pole_recv.at[pl.ds(pl.multiple_of(16 * lon, 8), 10), :],
            send_sem=b_s, recv_sem=b_r,
            device_id=(lat, l * slices + tip_slice), device_id_type=MESH,
        )

    for l in range(lev):
        @pl.when(lon != l * slices + tip_slice)
        def _(l=l):
            pole_copy(l).start()

        @pl.when(lon == l * slices + tip_slice)
        def _(l=l):
            pole_recv[pl.ds(pl.multiple_of(16 * lon, 8), 8), :] = pole_send[16 * l : 16 * l + 8, :]
            pole_recv[pl.ds(pl.multiple_of(16 * lon, 8) + 8, 2), :] = pole_send[16 * l + 8 : 16 * l + 10, :]

    pack_rims(ka, kap_send)
    sideways(kap_send, kap_recv, k_s, k_r)
    poleward(ka, k_s, k_r, kap_send, kap_diag)
    for load in loads[4:]:
        load.wait()

    start = lax.broadcasted_iota(jnp.int32, (sectors, width), 0) + half
    reach = partner[...] - jnp.where(start >= sectors, start - sectors, start) * width
    reach = jnp.where(reach < 0, reach + sectors * width, reach)
    farther = reach >= width
    at_lane = jnp.where(farther, reach - width, reach)

    def crossed(points):
        return jnp.where(
            farther, taken(pltpu.roll(points, sectors - half - 1, 0), at_lane), taken(pltpu.roll(points, half, 0), at_lane)
        )


    change = shift_weights(width, -1.0, 3, 2, 4)
    split_wait(3 * unit, 4 * unit, x_r, False)
    for l in range(lev):
        edge = jnp.where((lane & 3) == 3, rim_recv[0, 8 * l : 8 * l + 8, :], roll(rim_recv[1, 8 * l : 8 * l + 8, :], -2))
        edge = [x.astype(jnp.float32) for x in parts(edge)]
        across_west = west_and_east(
            tr[l, PAD : PAD + rows, :], [masked(four == g, edge) for g in range(groups)], change
        )
        tiles = []
        for g in range(groups):
            at = PAD + 8 * g
            x = tr[l, at : at + 8, :]
            turn = wn[l, 8 * g : 8 * g + 8, :] * (tr[l, at + 1 : at + 9, :] - tr[l, at - 1 : at + 7, :])
            push = we[l, 8 * g : 8 * g + 8, :] * across_west[8 * g : 8 * g + 8]
            value = x + COURANT * 0.5 * (push - turn)
            field[l, at : at + 8, :] = value
            k = ka[l, at : at + 8, :]
            inverse = 1.0 / (1.0 + 4.0 * k)
            invert[l, at : at + 8, :] = inverse
            coupling[l, at : at + 8, :] = k * inverse
            scaled[l, at : at + 8, :] = value * inverse
            tiles.append(value)
        first, second = packed(tiles)
        adv_send[0, 8 * l : 8 * l + 8, :] = first
        adv_send[1, 8 * l : 8 * l + 8, :] = second

    def sided(send, recv, at, put):
        for kk in range(4):
            mine = (four & 3) == kk
            near_west = jnp.where(mine, recv[0, at : at + 8, :], send[1, at : at + 8, :])
            near_east = jnp.where(mine, send[0, at : at + 8, :], recv[1, at : at + 8, :])
            put(kk, jnp.where((lane & 15) < 8, roll(near_west, -4 * kk), roll(near_east, 8 - 4 * kk)))

    sideways(adv_send, adv_recv, f_s, f_r)
    poleward(field, f_s, f_r, adv_send, adv_diag)

    beyond_fix[...] = jnp.zeros_like(beyond_fix)

    @pl.when(keeper)
    def _():
        bulk(10 * (sectors - 1), b_r).wait_recv()
        tips = jnp.concatenate([pole_recv[16 * d + 8 : 16 * d + 9, :] for d in range(sectors)], axis=0)
        winds = jnp.concatenate([pole_recv[16 * d + 9 : 16 * d + 10, :] for d in range(sectors)], axis=0)
        turned = COURANT * 0.5 * winds * crossed(tips)
        beyond_fix[...] = jnp.where(last, -turned, turned)

    first = jnp.where(last, pole, 0) + lax.rem(lon, slices) * share
    spot = lax.broadcasted_iota(jnp.int32, (share, 2 * pole), 0) + first
    limit = jnp.sum(
        jnp.where(
            lax.broadcasted_iota(jnp.int32, (share, 2 * pole), 1) == spot,
            cutoff[...].astype(jnp.float32), 0.0,
        ),
        axis=1, keepdims=True,
    )
    kept = 2 * KMAX // sectors
    slot = lax.broadcasted_iota(jnp.int32, (share, 2 * kept), 1)
    wave = sectors * (jnp.where(slot < kept, slot, slot - kept) - kept // 2)
    own = pl.multiple_of(lon * DEEP, 8)
    recv_a[pl.ds(own, share), :] = send_a[pl.ds(own, share), :]
    recv_a[pl.ds(own + share, 1), :] = send_a[pl.ds(own + share, 1), :]
    bulk((share + 1) * (sectors - 1), a_r).wait_recv()
    tw_cos, tw_sin = table[0 : half + 1, :], table[16 : half + 17, :]
    fwd = fine[: 6 * width, :]
    inv = jnp.concatenate([fine[6 * width : 9 * width, :], fine[9 * width :, :]], axis=1)

    def rows_of(ref, at):
        return [ref[pl.ds(8 * h * DEEP + at, 8, stride=DEEP), :] for h in range(2)]

    fixes = []
    for v in swapped(*rows_of(recv_a, share)):
        fixes.append(COURANT * 0.5 * v * jnp.where(eight == 6, roll(v, 11), -roll(v, -7)))
    at_tip = [(row8 == 0) & north & keeper, (row8 == 7) & last & keeper]
    ends = (lane == 0) | (lane == width - 1)
    spread = []
    for d in range(sectors):
        halves = []
        for h in range(2):
            x = recv_a[d * DEEP + 8 * h : d * DEEP + 8 * h + 8, :]
            x = x + jnp.where(ends, roll(fixes[h], -(8 * d + 6)), 0.0)
            halves.append(x + jnp.where(at_tip[h], beyond_fix[d : d + 1, :], 0.0))
        spread.append(jnp.concatenate(halves, axis=0))

    def circle(d, k):
        angle = 2.0 * math.pi * ((d * k) % sectors) / sectors
        return math.cos(angle), math.sin(angle)

    even = [spread[0]] + [spread[d] + spread[sectors - d] for d in range(1, half)] + [spread[half]]
    odd = [None] + [spread[d] - spread[sectors - d] for d in range(1, half)]
    blocks = []
    for k in range(half + 1):
        c, s = tw_cos[k : k + 1, :], tw_sin[k : k + 1, :]
        re = weighted([(circle(d, k)[0], even[d]) for d in range(half + 1)])
        im = weighted([(-circle(d, k)[1], odd[d]) for d in range(1, half)])
        if im is None:
            blocks.append(jnp.concatenate([re * c, -(re * s)], axis=1))
        else:
            blocks.append(jnp.concatenate([re * c + im * s, im * c - re * s], axis=1))
    spectrum = refined(jnp.concatenate(blocks, axis=0), fwd)
    keep = jnp.concatenate(
        [jnp.where(jnp.abs(wave + k).astype(jnp.float32) <= limit, 1.0, 0.0) for k in range(half + 1)], axis=0
    )
    back = refined(jnp.where(keep > 0.0, spectrum, 0.0), inv)
    real, imag = [], []
    for k in range(half + 1):
        c, s = tw_cos[k : k + 1, :], tw_sin[k : k + 1, :]
        zr = back[k * share : (k + 1) * share, :width]
        zi = back[k * share : (k + 1) * share, width:]
        twice = 1.0 if k in (0, half) else 2.0
        real.append((zr * c - zi * s) * twice)
        imag.append((zr * s + zi * c) * twice)
    smooth = [None] * sectors
    for d in range(half + 1):
        p = weighted([(circle(d, k)[0], real[k]) for k in range(half + 1)])
        q = weighted([(circle(d, k)[1], imag[k]) for k in range(1, half)])
        if q is None:
            smooth[d] = p
        else:
            smooth[d], smooth[sectors - d] = p - q, p + q
    edges = [zero, zero]
    for d in range(sectors):
        send_d[d * DEEP : d * DEEP + share, :] = smooth[d]
        for h in range(2):
            edges[h] = jnp.where((lane >> 3) == d, roll(smooth[d][8 * h : 8 * h + 8], 8 * d + 4), edges[h])
    beyond = [jnp.where(eight < 4, roll(v, 8), roll(v, -8)) for v in edges]
    for i in range(2):
        west, east = (beyond, edges) if i == 0 else (edges, beyond)
        for h, v in enumerate(swapped(*[jnp.where(eight < 4, w, e) for w, e in zip(west, east)])):
            send_d[pl.ds(8 * h * DEEP + share + i, 8, stride=DEEP), :] = v

    extra = share + 2 + SWEEPS + 1

    def put_cross(t, rows16):
        for h in range(2):
            send_d[pl.ds(8 * h * DEEP + share + 2 + t, 8, stride=DEEP), :] = rows16[8 * h : 8 * h + 8]

    @pl.when(keeper)
    def _():
        now, inverse, pull = [], [], []
        for d in range(sectors):
            top, low = d * DEEP, d * DEEP + 8
            now.append(jnp.where(last, send_d[low : low + 8, :], send_d[top : top + 8, :]))
            k = pole_recv[16 * d : 16 * d + 8, :]
            inverse.append(1.0 / (1.0 + 4.0 * k))
            pull.append(k * inverse[d])
        source = [a * b for a, b in zip(now, inverse)]
        ends = jnp.zeros((sectors, width), jnp.float32)
        wide = lax.broadcasted_iota(jnp.int32, (sectors, width), 1)
        for t in range(SWEEPS):
            tips = jnp.concatenate([jnp.where(last, x[7:8], x[0:1]) for x in now], axis=0)
            over = crossed(tips)
            put_cross(t, over)
            z = roll(over, 8 * t + 4)
            z = jnp.where((wide & 7) < 4, pltpu.roll(z, 1, 0), pltpu.roll(z, sectors - 1, 0))
            ends = jnp.where((wide >> 3) == t, z, ends)
            if t < SWEEPS - 1:
                right, left = [roll(x, 1) for x in now], [roll(x, -1) for x in now]
                later = []
                for d in range(sectors):
                    w = jnp.where(lane == 0, right[d - 1], right[d])
                    e = jnp.where(lane == width - 1, left[(d + 1) % sectors], left[d])
                    u = jnp.where((row8 == 0) & jnp.logical_not(last), over[d : d + 1], pltpu.roll(now[d], 1, 0))
                    b = jnp.where((row8 == 7) & last, over[d : d + 1], pltpu.roll(now[d], 7, 0))
                    later.append(source[d] + pull[d] * (w + e + u + b))
                now = later
        put_cross(SWEEPS, ends)
        across(send_d, recv_d, extra, d_s, d_r)

    @pl.when(jnp.logical_not(keeper))
    def _():
        across(send_d, recv_d, share + 2, d_s, d_r)

    recv_d[pl.ds(own, share), :] = send_d[pl.ds(own, share), :]
    recv_d[pl.ds(own + share, 2), :] = send_d[pl.ds(own + share, 2), :]

    @pl.when(keeper)
    def _():
        recv_d[pl.ds(own + share + 2, SWEEPS + 1), :] = send_d[pl.ds(own + share + 2, SWEEPS + 1), :]

    split_wait(5 * unit, 8 * unit, k_r, False)

    def corners(ref, diag, l):
        top, bottom = ref[l, PAD - 8 : PAD, :], ref[l, PAD + rows : PAD + rows + 8, :]
        nw, ne, sw, se = [diag[i, 8 * l : 8 * l + 8, :] for i in range(4)]
        first = jnp.where(
            lane < 8, roll(jnp.where(lane >= width - 4, nw, top), 4), roll(jnp.where(lane < 4, ne, top), 12)
        )
        second = jnp.where(
            lane < width - 8,
            jnp.where(lane < width - 12, roll(sw, -16), roll(bottom, -12)),
            jnp.where(lane < width - 4, roll(bottom, -4), roll(se, -8)),
        )
        return first, second

    def capped(first_tile, last_tile, first, second):
        return jnp.where(lane < 16, first, roll(last_tile, 16)), jnp.where(lane >= width - 16, second, roll(first_tile, -16))

    for l in range(lev):
        tiles = []

        def put(kk, tile, l=l, tiles=tiles):
            side_invert[l, 12 + 8 * kk : 20 + 8 * kk, :] = tile
            tiles.append(tile)

        sided(kap_send, kap_recv, 8 * l, put)
        top, bottom = capped(tiles[0], tiles[3], *corners(ka, kap_diag, l))
        side_invert[l, 4:12, :] = top
        side_invert[l, 44:52, :] = bottom
        for j in range(5):
            at = 8 + 8 * j
            k = side_invert[l, at : at + 8, :]
            inverse = 1.0 / (1.0 + 4.0 * k)
            side_invert[l, at : at + 8, :] = inverse
            side_coupling[l, at : at + 8, :] = k * inverse
    split_wait(5 * unit, 8 * unit, f_r, False)
    for l in range(lev):
        for at in (PAD - 8, PAD + rows):
            k = ka[l, at : at + 8, :]
            inverse = 1.0 / (1.0 + 4.0 * k)
            coupling[l, at : at + 8, :] = k * inverse
            scaled[l, at : at + 8, :] = field[l, at : at + 8, :] * inverse

        def put(kk, tile, l=l):
            side_tiles[32 * l + 8 * kk : 32 * l + 8 * kk + 8, :] = tile

        sided(adv_send, adv_recv, 8 * l, put)
        corner[0, 8 * l : 8 * l + 8, :], corner[1, 8 * l : 8 * l + 8, :] = corners(field, adv_diag, l)
        at = 32 * l
        early[0, l, 12:44, :] = side_tiles[at : at + 32, :]
        early[0, l, 4:12, :], early[0, l, 44:52, :] = capped(
            side_tiles[at : at + 8, :], side_tiles[at + 24 : at + 32, :],
            corner[0, 8 * l : 8 * l + 8, :], corner[1, 8 * l : 8 * l + 8, :],
        )
        early_scaled[l, 8:48, :] = early[0, l, 8:48, :] * side_invert[l, 8:48, :]

    weights = shift_weights(width, 1.0, 3, 12, 16)
    order = [(0, -1)] + [(i // 4, i % 4) for i in range(groups)] + [(groups // 4 - 1, 4)]
    at16 = lane & 15

    def sweep_early(t, carry):
        for l in range(lev):
            ends = {kk: rim(early[t, l, 12 + 8 * kk : 20 + 8 * kk, :], at16) for kk in range(-1, 5)}
            total = west_and_east(
                stack[t, l, PAD - 8 : PAD + rows + 8, :],
                [masked((lane >> 4) == g, ends[kk]) for g, kk in order], weights,
            )
            for i in range(groups + 2):
                at = PAD - 8 + 8 * i
                value = total[8 * i : 8 * i + 8] + (stack[t, l, at - 1 : at + 7, :] + stack[t, l, at + 1 : at + 9, :])
                stack[t + 1, l, at : at + 8, :] = scaled[l, at : at + 8, :] + coupling[l, at : at + 8, :] * value
            for j in range(5):
                at = 8 + 8 * j
                x = early[t, l, at : at + 8, :]
                value = roll(x, 1) + roll(x, -1) + early[t, l, at - 1 : at + 7, :] + early[t, l, at + 1 : at + 9, :]
                early[t + 1, l, at : at + 8, :] = (
                    early_scaled[l, at : at + 8, :] + side_coupling[l, at : at + 8, :] * value
                )
        return carry

    lax.fori_loop(0, SWEEPS, sweep_early, 0)

    plain_rows, more = (share + 2) * (sectors - 1), SWEEPS + 1
    d_waits = ((keeper, plain_rows + more * (lev - 1)), (jnp.logical_not(keeper), plain_rows + more * lev))
    for here, count in d_waits:
        @pl.when(here)
        def _(count=count):
            bulk(count, d_r).wait_recv()

    def cross(l, t):
        return recv_d[pl.ds((l * slices + tip_slice) * DEEP + share + 2 + t, 1), :]

    @pl.when(polar)
    def _():
        for k in range(sectors):
            l, q = k // slices, k % slices
            x = recv_d[k * DEEP : k * DEEP + share, :]
            at = base + PAD + q * share
            field[l, pl.ds(at, share), :] = x
            scaled[l, pl.ds(at, share), :] = x * invert[l, pl.ds(at, share), :]

    @pl.when(north)
    def _():
        for l in range(lev):
            field[l, PAD - 1 : PAD, :] = cross(l, 0)

    @pl.when(last)
    def _():
        for l in range(lev):
            field[l, PAD + rows : PAD + rows + 1, :] = cross(l, 0)

    halo = jnp.concatenate([cross(l, SWEEPS) for l in range(lev)] * 2, axis=0)
    for t in range(SWEEPS):
        plain = jnp.concatenate([cross(l, t) for l in range(lev)] * 2, axis=0)
        z = jnp.where(
            lane < 8,
            jnp.where(lane < 4, roll(halo, -8 * t), roll(plain, 4)),
            jnp.where(lane < 12, roll(plain, 12), roll(halo, 8 - 8 * t)),
        )
        side_cross[t, :8, :] = jnp.where(last, roll(z, -16), z)
        side_cross[t, 8:, :] = plain

    strips = [
        [jnp.where(last, roll(v, -32), v) for v in swapped(*rows_of(recv_d, share + i))] for i in range(2)
    ]
    from_cap = jnp.where(last, lane - (width - 32), lane)
    inside_cap = polar & (from_cap >= 0) & (from_cap < 32)
    top_spot = north & (row8 == 7) & (lane < 16)
    bottom_spot = last & (row8 == 0) & (lane >= width - 16)
    for l in range(lev):
        tiles = []
        for kk in range(4):
            h, by = kk % 2, -32 * l - 8 * (kk // 2)
            z = jnp.where((lane & 15) < 8, roll(strips[0][h], by), roll(strips[1][h], by + 8))
            tile = jnp.where(inside_cap, z, side_tiles[32 * l + 8 * kk : 32 * l + 8 * kk + 8, :])
            side[l, 12 + 8 * kk : 20 + 8 * kk, :] = tile
            tiles.append(tile)
        at = 8 * l
        top, bottom = capped(tiles[0], tiles[3], corner[0, at : at + 8, :], corner[1, at : at + 8, :])
        side[l, 4:12, :] = jnp.where(top_spot, side_cross[0, l : l + 1, :], top)
        side[l, 44:52, :] = jnp.where(bottom_spot, side_cross[0, l : l + 1, :], bottom)
        for j in range(5):
            at = 8 + 8 * j
            side_scaled[l, at : at + 8, :] = side[l, at : at + 8, :] * side_invert[l, at : at + 8, :]

    bulk((share + 1) * (sectors - 1), a_s).wait_send()
    split_wait(3 * unit, 4 * unit, x_s, True)
    split_wait(5 * unit, 8 * unit, k_s, True)
    split_wait(5 * unit, 8 * unit, f_s, True)
    for here, pole_rows, rows_out in (
        (keeper, 10 * (lev - 1), extra * (sectors - 1)), (jnp.logical_not(keeper), 10 * lev, plain_rows)
    ):
        @pl.when(here)
        def _(pole_rows=pole_rows, rows_out=rows_out):
            bulk(pole_rows, b_s).wait_send()
            bulk(rows_out, d_s).wait_send()


def relax(
    bands, stack, scaled, coupling, side0, side_scaled, side_coupling, side_cross, filtered, balanced, local, side, sems
):
    lev, rows, width = filtered.shape
    near = local.shape[2] - 2 * PAD
    tiles = near // 8 + 1
    lat = lax.axis_index("lat")
    north, last = lat == 0, lat == bands - 1
    base = pl.multiple_of(jnp.where(last, rows - near, 0), 8)
    rest = pl.multiple_of(jnp.where(last, 0, near), 8)
    copies = [
        pltpu.make_async_copy(stack.at[0, :, pl.ds(PAD, rows), :], filtered, sems.at[0]),
        pltpu.make_async_copy(
            stack.at[SWEEPS, :, pl.ds(rest + PAD, rows - near), :], balanced.at[:, pl.ds(rest, rows - near), :], sems.at[1]
        ),
    ]
    for copy in copies:
        copy.start()
    lane = lax.broadcasted_iota(jnp.int32, (8, width), 1)
    row8 = lax.broadcasted_iota(jnp.int32, (8, width), 0)
    at16 = lane & 15
    group = (lane >> 4) - jnp.where(last, (rows - near) // 32, 0)
    weights = shift_weights(width, 1.0, 3, 12, 16)
    for l in range(lev):
        local[0, l, PAD - 8 : PAD + near + 8, :] = stack[0, l, pl.ds(base + PAD - 8, near + 16), :]
    for t in range(SWEEPS):
        beside = side0 if t == 0 else side.at[t - 1]
        edges = []
        for l in range(lev):
            ends = {kk: rim(beside[l, 12 + 8 * kk : 20 + 8 * kk, :], at16) for kk in range(-1, 4)}
            edges.append(masked(lane < 16, ends[-1]))
            for i in range(near // 8):
                edges.append(masked(group == i // 4, ends[i % 4]))
        whole = jnp.concatenate([local[t, l, PAD - 8 : PAD + near, :] for l in range(lev)], axis=0)
        total = west_and_east(whole, edges, weights)
        for l in range(lev):
            for i in range(tiles):
                at = PAD - 8 + 8 * i
                start = 8 * (tiles * l + i)
                value = total[start : start + 8] + (local[t, l, at - 1 : at + 7, :] + local[t, l, at + 1 : at + 9, :])
                there = pl.ds(base + at, 8)
                value = scaled[l, there, :] + coupling[l, there, :] * value
                if t < SWEEPS - 1 and i == 0:
                    cross = side_cross[t + 1, 8 + l : 9 + l, :]
                    at_end = rows - near + PAD - 8
                    value = jnp.where(north & (row8 == 7), cross, value)
                    value = jnp.where(last, stack[t + 1, l, at_end : at_end + 8, :], value)
                    at_end = near + PAD
                    local[t + 1, l, at_end : at_end + 8, :] = jnp.where(
                        last, jnp.broadcast_to(cross, (8, width)), stack[t + 1, l, at_end : at_end + 8, :]
                    )
                local[t + 1, l, at : at + 8, :] = value
        if t == SWEEPS - 1:
            break
        for l in range(lev):
            for j in range(5):
                at = 8 + 8 * j
                x = beside[l, at : at + 8, :]
                value = pltpu.roll(x, 1, 1) + pltpu.roll(x, width - 1, 1)
                value = value + (beside[l, at - 1 : at + 7, :] + beside[l, at + 1 : at + 9, :])
                x = side_scaled[l, at : at + 8, :] + side_coupling[l, at : at + 8, :] * value
                cross = side_cross[t + 1, l : l + 1, :]
                if j == 0:
                    x = jnp.where(north & (row8 == 3) & (lane < 16), cross, x)
                if j == 4:
                    x = jnp.where(last & (row8 == 4) & (lane >= width - 16), cross, x)
                side[t, l, at : at + 8, :] = x
    copy = pltpu.make_async_copy(
        local.at[SWEEPS, :, pl.ds(PAD, near), :], balanced.at[:, pl.ds(base, near), :], sems.at[2]
    )
    copy.start()
    for copy in (*copies, copy):
        copy.wait()


def solution(mesh):
    sectors, bands = mesh.shape["lon"], mesh.shape["lat"]

    def per_device(tracer, wind_east, wind_north, kappa, cutoff, partner):
        lev, rows, width = tracer.shape
        f32 = jnp.float32
        high = rows + 2 * PAD

        def array(*shape):
            return pltpu.VMEM(shape, f32)

        block, tall = array(lev, rows, width), array(lev, high, width)
        strips = array(sectors * DEEP, width)
        pair, four = array(2, lev * 8, width), array(4, lev * 8, width)
        narrow = array(lev, 56, width)
        vmem = pl.BlockSpec(memory_space=pltpu.VMEM)
        hbm = pl.BlockSpec(memory_space=pltpu.HBM)
        tw_cos, tw_sin, fwd, inv = tables(sectors, width)
        blank = np.zeros((16 - tw_cos.shape[0], width), np.float32)
        table = np.concatenate([tw_cos, blank, tw_sin, blank], axis=0)
        fine = []
        for whole in (fwd, inv[:, :width], inv[:, width:]):
            first = whole.astype(jnp.bfloat16)
            fine += [first, first, (whole - first.astype(np.float32)).astype(jnp.bfloat16)]
        fine = np.concatenate(fine, axis=0)
        small = (cutoff.reshape(1, -1), partner.reshape(sectors, width), table, fine)
        dma = pltpu.SemaphoreType.DMA
        made = [(SWEEPS + 1, lev, high, width)] + [(lev, high, width)] * 2 + [(lev, 56, width)] * 3 + [(SWEEPS, 16, width)]
        limit = 24 * 1024 * 1024
        near = cutoff.shape[0] // 2 + 32
        held = pl.pallas_call(
            functools.partial(kernel, sectors, bands),
            out_shape=[jax.ShapeDtypeStruct(shape, f32) for shape in made],
            in_specs=[hbm] * 8,
            out_specs=[vmem] * len(made),
            scratch_shapes=[
                tall, block, block, tall,
                *[pltpu.VMEM(a.shape, a.dtype) for a in small],
                dma((8,)),
                strips, strips, array(16 * lev, width), array(16 * sectors, width), strips, strips,
                array(sectors, width),
                pair, pair, pair, pair, four, pair, pair, four, pair, tall, array(lev * 32, width), narrow, array(SWEEPS + 1, lev, 56, width), narrow,
                *[dma] * 12,
            ],
            compiler_params=pltpu.CompilerParams(collective_id=0, has_side_effects=True, vmem_limit_bytes=limit),
        )(
            *[pltpu.with_memory_space_constraint(jnp.asarray(a), pltpu.HBM) for a in (tracer, wind_east, wind_north, kappa, *small)]
        )
        return pl.pallas_call(
            functools.partial(relax, bands),
            out_shape=[jax.ShapeDtypeStruct(tracer.shape, f32)] * 2,
            in_specs=[vmem] * len(made),
            out_specs=[hbm] * 2,
            scratch_shapes=[array(SWEEPS + 1, lev, near + 2 * PAD, width), array(SWEEPS - 1, lev, 56, width), dma((3,))],
            compiler_params=pltpu.CompilerParams(vmem_limit_bytes=limit),
        )(*[pltpu.with_memory_space_constraint(a, pltpu.VMEM) for a in held])

    spec = P(None, "lat", "lon")
    return jax.shard_map(
        per_device, mesh=mesh, in_specs=(spec, spec, spec, spec, P(), P()), out_specs=(spec, spec),
        check_vma=False,
    )
```

```python
import functools
import math

import jax
import jax.numpy as jnp
import numpy as np
from jax import lax
from jax.experimental import pallas as pl
from jax.experimental.pallas import tpu as pltpu
from jax.sharding import PartitionSpec as P

KMAX = 512
SWEEPS = 4
COURANT = 0.4
HIGHEST = lax.Precision.HIGHEST


def tables(sectors, width):
    total = sectors * width
    half = sectors // 2
    m = np.arange(width)
    theta = 2.0 * np.pi * (np.outer(np.arange(half + 1), m) % total) / total
    kept = 2 * KMAX // sectors
    k2 = np.arange(kept) - kept // 2
    phase = 2.0 * np.pi * (np.outer(m, k2) % width) / width
    c, s = np.cos(phase), np.sin(phase)
    forward = np.block([[c, -s], [s, c]])
    inverse = np.block([[c.T, s.T], [-s.T, c.T]]) / total
    return [a.astype(np.float32) for a in (np.cos(theta), np.sin(theta), forward, inverse)]


def weighted(terms):
    total = None
    for factor, value in terms:
        if abs(factor) < 1e-12:
            continue
        part = value if abs(factor - 1.0) < 1e-12 else value * np.float32(factor)
        total = part if total is None else total + part
    return total


PAD = 16
DEEP = 24
MESH = pl.DeviceIdType.MESH


def taken(x, at_lane):
    return jnp.take_along_axis(x, at_lane, axis=1, mode="promise_in_bounds")


def parts(x):
    high = x.astype(jnp.bfloat16)
    return high, (x - high.astype(jnp.float32)).astype(jnp.bfloat16)


def shift_weights(width, east, west_lane, east_lane, lanes):
    one = lax.broadcasted_iota(jnp.int32, (width, width), 0)
    two = lax.broadcasted_iota(jnp.int32, (width, width), 1)
    shift = jnp.where(one - two == 1, east, 0.0) + jnp.where(two - one == 1, 1.0, 0.0)
    spot = one & (lanes - 1)
    edge = jnp.where((two == width - 1) & (spot == east_lane), east, 0.0)
    edge = edge + jnp.where((two == 0) & (spot == west_lane), 1.0, 0.0)
    shift, edge = shift.astype(jnp.bfloat16), edge.astype(jnp.bfloat16)
    return jnp.concatenate([shift, shift, edge, edge], axis=0)


def rim(h, at16):
    high, low = parts(jnp.where((at16 == 3) | (at16 == 12), h, 0.0))
    return high.astype(jnp.float32), low.astype(jnp.float32)


def masked(here, pair):
    return [jnp.where(here, x, 0.0) for x in pair]


def west_and_east(x, edges, weights):
    high, low = parts(x)
    rims = [jnp.concatenate(tiles, axis=0).astype(jnp.bfloat16) for tiles in zip(*edges)]
    return jnp.dot(jnp.concatenate([high, low, *rims], axis=1), weights, preferred_element_type=jnp.float32)


def refined(x, weights):
    high, low = parts(x)
    return jnp.dot(jnp.concatenate([high, low, high], axis=1), weights, preferred_element_type=jnp.float32)


def kernel(
    sectors, bands,
    tracer_h, wind_east_h, wind_north_h, kappa_h, cutoff_h, partner_h, table_h, fine_h,
    stack, scaled, coupling, side, side_scaled, side_coupling, side_cross,
    tr, we, wn, ka, cutoff, partner, table, fine, load_s,
    send_a, recv_a, pole_send, pole_recv, send_d, recv_d, beyond_fix,
    rim_send, rim_recv, kap_send, kap_recv, kap_diag, adv_send, adv_recv, adv_diag, corner, invert, side_tiles, side_invert, early, early_scaled,
    a_s, a_r, b_s, b_r, d_s, d_r, x_s, x_r, k_s, k_r, f_s, f_r,
):
    lev, rows, width = we.shape
    field = stack.at[0]
    pole = cutoff.shape[1] // 2
    share = lev * pole // sectors
    slices = sectors // lev
    half = sectors // 2
    groups = rows // 8
    lat = lax.axis_index("lat")
    lon = lax.axis_index("lon")
    last = lat == bands - 1
    north = lat == 0
    polar = north | last

    def sector(offset):
        return lax.rem(lon + (offset % sectors), sectors)

    def band(offset):
        return lax.rem(lat + (offset % bands), bands)

    body = pl.ds(PAD, rows)
    held = (tracer_h, wind_east_h, wind_north_h, kappa_h, partner_h, cutoff_h, table_h, fine_h)
    near = (tr.at[:, body, :], we, wn, ka.at[:, body, :], partner, cutoff, table, fine)
    loads = [pltpu.make_async_copy(h, v, load_s.at[i]) for i, (h, v) in enumerate(zip(held, near))]
    for load in loads[:3]:
        load.start()

    barrier = pltpu.get_barrier_semaphore()
    for t in range(1, sectors):
        pl.semaphore_signal(barrier, inc=1, device_id=(lat, sector(t)), device_id_type=MESH)
    beside = (1,) if bands == 2 else (1, -1)
    for t in beside:
        for i in (-1, 0, 1):
            pl.semaphore_signal(barrier, inc=1, device_id=(band(t), sector(i)), device_id_type=MESH)

    for load in loads[3:]:
        load.start()

    lane = lax.broadcasted_iota(jnp.int32, (8, width), 1)
    row8 = lax.broadcasted_iota(jnp.int32, (8, width), 0)
    zero = jnp.zeros((8, width), jnp.float32)

    def roll(x, by):
        by = by % width
        return x if by == 0 else pltpu.roll(x, by, 1)

    def swapped(v0, v1):
        low = lane < width // 2
        v0, v1 = jnp.where(low, v0, roll(v1, width // 2)), jnp.where(low, roll(v0, width // 2), v1)
        out = []
        for v in (v0, v1):
            for b in (2, 1, 0):
                step, hop = 1 << b, 8 << b
                upper = (lane & hop) != 0
                same = ((row8 >> b) & 1) == ((lane >> (3 + b)) & 1)
                v = jnp.where(
                    same, v,
                    jnp.where(upper, pltpu.roll(roll(v, hop), 8 - step, 0), pltpu.roll(roll(v, -hop), step, 0)),
                )
            out.append(v)
        return out

    base = pl.multiple_of(jnp.where(last, rows - pole, 0), 8)
    tip = jnp.where(last, rows - 1, 0)
    tip_tile = pl.multiple_of(jnp.where(last, rows - 8, 0), 8)
    tip_slice = jnp.where(last, slices - 1, 0)
    keeper = lax.rem(lon, slices) == tip_slice

    @pl.when(north)
    def _():
        for l in range(lev):
            tr[l, PAD - 8 : PAD, :] = zero

    @pl.when(last)
    def _():
        for l in range(lev):
            tr[l, PAD + rows : PAD + rows + 8, :] = zero

    for load in loads[:3]:
        load.wait()
    lane_p = lax.broadcasted_iota(jnp.int32, (pole, width), 1)
    row_p = lax.broadcasted_iota(jnp.int32, (pole, width), 0)
    before = jnp.where(last, rows - pole - 1, 0)
    after = jnp.where(last, rows - 1, pole)
    eight = lane & 7
    packs = [zero, zero]
    for l in range(lev):
        x = tr[l, pl.ds(base + PAD, pole), :]
        east_wind = we[l, pl.ds(base, pole), :]
        w = jnp.where(lane_p == 0, 0.0, pltpu.roll(x, 1, 1))
        e = jnp.where(lane_p == width - 1, 0.0, pltpu.roll(x, width - 1, 1))
        above = jnp.where(last, tr[l, pl.ds(PAD + before, 1), :], 0.0)
        below = jnp.where(last, 0.0, tr[l, pl.ds(PAD + after, 1), :])
        u = jnp.where(row_p == 0, above, pltpu.roll(x, 1, 0))
        d = jnp.where(row_p == pole - 1, below, pltpu.roll(x, pole - 1, 0))
        stage = x - COURANT * 0.5 * (east_wind * (e - w) + wn[l, pl.ds(base, pole), :] * (d - u))
        for q in range(slices):
            k = l * slices + q
            send_a[k * DEEP : k * DEEP + share, :] = stage[q * share : (q + 1) * share]
            for h in range(2):
                at = q * share + 8 * h
                t = jnp.where(
                    (eight == 3) | (eight == 4), roll(x[at : at + 8], 4 + 8 * k), roll(east_wind[at : at + 8], 6 + 8 * k)
                )
                packs[h] = jnp.where((lane >> 3) == k, t, packs[h])
    for h, v in enumerate(swapped(*packs)):
        send_a[pl.ds(8 * h * DEEP + share, 8, stride=DEEP), :] = v

    def across(src, dst, count, ss, rs):
        for t in range(1, sectors):
            there = sector(t)
            pltpu.make_async_remote_copy(
                src_ref=src.at[pl.ds(pl.multiple_of(there * DEEP, 8), count), :],
                dst_ref=dst.at[pl.ds(pl.multiple_of(lon * DEEP, 8), count), :],
                send_sem=ss, recv_sem=rs, device_id=(lat, there), device_id_type=MESH,
            ).start()

    def bulk(count, sem):
        whole = send_d.at[pl.ds(0, count), :]
        return pltpu.make_async_remote_copy(
            src_ref=whole, dst_ref=whole, send_sem=sem, recv_sem=sem, device_id=(lat, sector(1)), device_id_type=MESH
        )

    def split_wait(single, double, sem, send):
        for here, count in ((polar, single), (jnp.logical_not(polar), double)):
            @pl.when(here)
            def _(count=count):
                if send:
                    bulk(count, sem).wait_send()
                else:
                    bulk(count, sem).wait_recv()

    four = lane >> 2

    def packed(tiles):
        first, second = zero, zero
        for g, x in enumerate(tiles):
            z = roll(x, 4 * g + 4)
            first = jnp.where(four == g, z, first)
            second = jnp.where(four == (g + 1) % groups, z, second)
        return first, second

    def pack_rims(source, target):
        def one(l, carry):
            at = pl.multiple_of(8 * l, 8)
            first, second = packed([source[l, PAD + 8 * g : PAD + 8 * g + 8, :] for g in range(groups)])
            target[0, pl.ds(at, 8), :] = first
            target[1, pl.ds(at, 8), :] = second
            return carry

        lax.fori_loop(0, lev, one, 0)

    def sideways(src, dst, ss, rs):
        for j in range(2):
            pltpu.make_async_remote_copy(
                src_ref=src.at[j], dst_ref=dst.at[j], send_sem=ss, recv_sem=rs,
                device_id=(lat, sector(1 - 2 * j)), device_id_type=MESH,
            ).start()

    def poleward(ref, ss, rs, send=None, recv=None):
        for i, step in enumerate((1, -1)):
            plan = [
                (
                    ref.at[:, pl.ds(PAD + rows - 8 if step == 1 else PAD, 8), :],
                    ref.at[:, pl.ds(PAD - 8 if step == 1 else PAD + rows, 8), :], 0,
                )
            ]
            if send is not None:
                plan += [(send.at[j], recv.at[2 * i + j], 1 - 2 * j) for j in range(2)]

            @pl.when(lat < bands - 1 if step == 1 else lat > 0)
            def _(step=step, plan=plan):
                for src, dst, aside in plan:
                    pltpu.make_async_remote_copy(
                        src_ref=src, dst_ref=dst, send_sem=ss, recv_sem=rs,
                        device_id=(band(step), sector(aside)), device_id_type=MESH,
                    ).start()

    unit = 8 * lev
    pack_rims(tr, rim_send)
    pl.semaphore_wait(barrier, sectors - 1 + 3 * len(beside))
    sideways(rim_send, rim_recv, x_s, x_r)
    poleward(tr, x_s, x_r)
    across(send_a, recv_a, share + 1, a_s, a_r)

    loads[3].wait()
    for l in range(lev):
        pole_send[16 * l : 16 * l + 8, :] = ka[l, pl.ds(tip_tile + PAD, 8), :]
        pole_send[16 * l + 8 : 16 * l + 9, :] = tr[l, pl.ds(tip + PAD, 1), :]
        pole_send[16 * l + 9 : 16 * l + 10, :] = wn[l, pl.ds(tip, 1), :]

    def pole_copy(l):
        return pltpu.make_async_remote_copy(
            src_ref=pole_send.at[pl.ds(16 * l, 10), :], dst_ref=pole_recv.at[pl.ds(pl.multiple_of(16 * lon, 8), 10), :],
            send_sem=b_s, recv_sem=b_r,
            device_id=(lat, l * slices + tip_slice), device_id_type=MESH,
        )

    for l in range(lev):
        @pl.when(lon != l * slices + tip_slice)
        def _(l=l):
            pole_copy(l).start()

        @pl.when(lon == l * slices + tip_slice)
        def _(l=l):
            pole_recv[pl.ds(pl.multiple_of(16 * lon, 8), 8), :] = pole_send[16 * l : 16 * l + 8, :]
            pole_recv[pl.ds(pl.multiple_of(16 * lon, 8) + 8, 2), :] = pole_send[16 * l + 8 : 16 * l + 10, :]

    pack_rims(ka, kap_send)
    sideways(kap_send, kap_recv, k_s, k_r)
    poleward(ka, k_s, k_r, kap_send, kap_diag)
    for load in loads[4:]:
        load.wait()

    start = lax.broadcasted_iota(jnp.int32, (sectors, width), 0) + half
    reach = partner[...] - jnp.where(start >= sectors, start - sectors, start) * width
    reach = jnp.where(reach < 0, reach + sectors * width, reach)
    farther = reach >= width
    at_lane = jnp.where(farther, reach - width, reach)

    def crossed(points):
        return jnp.where(
            farther, taken(pltpu.roll(points, sectors - half - 1, 0), at_lane), taken(pltpu.roll(points, half, 0), at_lane)
        )


    change = shift_weights(width, -1.0, 3, 2, 4)
    split_wait(3 * unit, 4 * unit, x_r, False)
    for l in range(lev):
        edge = jnp.where((lane & 3) == 3, rim_recv[0, 8 * l : 8 * l + 8, :], roll(rim_recv[1, 8 * l : 8 * l + 8, :], -2))
        edge = [x.astype(jnp.float32) for x in parts(edge)]
        across_west = west_and_east(
            tr[l, PAD : PAD + rows, :], [masked(four == g, edge) for g in range(groups)], change
        )
        tiles = []
        for g in range(groups):
            at = PAD + 8 * g
            x = tr[l, at : at + 8, :]
            turn = wn[l, 8 * g : 8 * g + 8, :] * (tr[l, at + 1 : at + 9, :] - tr[l, at - 1 : at + 7, :])
            push = we[l, 8 * g : 8 * g + 8, :] * across_west[8 * g : 8 * g + 8]
            value = x + COURANT * 0.5 * (push - turn)
            field[l, at : at + 8, :] = value
            k = ka[l, at : at + 8, :]
            inverse = 1.0 / (1.0 + 4.0 * k)
            invert[l, at : at + 8, :] = inverse
            coupling[l, at : at + 8, :] = k * inverse
            scaled[l, at : at + 8, :] = value * inverse
            tiles.append(value)
        first, second = packed(tiles)
        adv_send[0, 8 * l : 8 * l + 8, :] = first
        adv_send[1, 8 * l : 8 * l + 8, :] = second

    def sided(send, recv, at, put):
        for kk in range(4):
            mine = (four & 3) == kk
            near_west = jnp.where(mine, recv[0, at : at + 8, :], send[1, at : at + 8, :])
            near_east = jnp.where(mine, send[0, at : at + 8, :], recv[1, at : at + 8, :])
            put(kk, jnp.where((lane & 15) < 8, roll(near_west, -4 * kk), roll(near_east, 8 - 4 * kk)))

    sideways(adv_send, adv_recv, f_s, f_r)
    poleward(field, f_s, f_r, adv_send, adv_diag)

    beyond_fix[...] = jnp.zeros_like(beyond_fix)

    @pl.when(keeper)
    def _():
        bulk(10 * (sectors - 1), b_r).wait_recv()
        tips = jnp.concatenate([pole_recv[16 * d + 8 : 16 * d + 9, :] for d in range(sectors)], axis=0)
        winds = jnp.concatenate([pole_recv[16 * d + 9 : 16 * d + 10, :] for d in range(sectors)], axis=0)
        turned = COURANT * 0.5 * winds * crossed(tips)
        beyond_fix[...] = jnp.where(last, -turned, turned)

    first = jnp.where(last, pole, 0) + lax.rem(lon, slices) * share
    spot = lax.broadcasted_iota(jnp.int32, (share, 2 * pole), 0) + first
    limit = jnp.sum(
        jnp.where(
            lax.broadcasted_iota(jnp.int32, (share, 2 * pole), 1) == spot,
            cutoff[...].astype(jnp.float32), 0.0,
        ),
        axis=1, keepdims=True,
    )
    kept = 2 * KMAX // sectors
    slot = lax.broadcasted_iota(jnp.int32, (share, 2 * kept), 1)
    wave = sectors * (jnp.where(slot < kept, slot, slot - kept) - kept // 2)
    own = pl.multiple_of(lon * DEEP, 8)
    recv_a[pl.ds(own, share), :] = send_a[pl.ds(own, share), :]
    recv_a[pl.ds(own + share, 1), :] = send_a[pl.ds(own + share, 1), :]
    bulk((share + 1) * (sectors - 1), a_r).wait_recv()
    tw_cos, tw_sin = table[0 : half + 1, :], table[16 : half + 17, :]
    fwd = fine[: 6 * width, :]
    inv = jnp.concatenate([fine[6 * width : 9 * width, :], fine[9 * width :, :]], axis=1)

    def rows_of(ref, at):
        return [ref[pl.ds(8 * h * DEEP + at, 8, stride=DEEP), :] for h in range(2)]

    fixes = []
    for v in swapped(*rows_of(recv_a, share)):
        fixes.append(COURANT * 0.5 * v * jnp.where(eight == 6, roll(v, 11), -roll(v, -7)))
    at_tip = [(row8 == 0) & north & keeper, (row8 == 7) & last & keeper]
    ends = (lane == 0) | (lane == width - 1)
    spread = []
    for d in range(sectors):
        halves = []
        for h in range(2):
            x = recv_a[d * DEEP + 8 * h : d * DEEP + 8 * h + 8, :]
            x = x + jnp.where(ends, roll(fixes[h], -(8 * d + 6)), 0.0)
            halves.append(x + jnp.where(at_tip[h], beyond_fix[d : d + 1, :], 0.0))
        spread.append(jnp.concatenate(halves, axis=0))

    def circle(d, k):
        angle = 2.0 * math.pi * ((d * k) % sectors) / sectors
        return math.cos(angle), math.sin(angle)

    def folded(x, lowest):
        middle = half // 2
        pairs = range(lowest, middle)
        return (
            {d: x[d] + x[half - d] for d in pairs} | {middle: x[middle]},
            {d: x[d] - x[half - d] for d in pairs},
        )

    def cosine_sums(x):
        plus, minus = folded(x, 0)
        return [weighted([(circle(d, k)[0], v) for d, v in (minus if k % 2 else plus).items()]) for k in range(half + 1)]

    def sine_sums(x):
        plus, minus = folded(x, 1)
        return [None] + [
            weighted([(circle(d, k)[1], v) for d, v in (plus if k % 2 else minus).items()]) for k in range(1, half)
        ] + [None]

    even = [spread[0]] + [spread[d] + spread[sectors - d] for d in range(1, half)] + [spread[half]]
    odd = [None] + [spread[d] - spread[sectors - d] for d in range(1, half)]
    blocks = []
    for k, (re, im) in enumerate(zip(cosine_sums(even), sine_sums(odd))):
        c, s = tw_cos[k : k + 1, :], tw_sin[k : k + 1, :]
        if im is None:
            blocks.append(jnp.concatenate([re * c, -(re * s)], axis=1))
        else:
            blocks.append(jnp.concatenate([re * c - im * s, -(im * c) - re * s], axis=1))
    spectrum = refined(jnp.concatenate(blocks, axis=0), fwd)
    keep = jnp.concatenate(
        [jnp.where(jnp.abs(wave + k).astype(jnp.float32) <= limit, 1.0, 0.0) for k in range(half + 1)], axis=0
    )
    back = refined(jnp.where(keep > 0.0, spectrum, 0.0), inv)
    real, imag = [], []
    for k in range(half + 1):
        c, s = tw_cos[k : k + 1, :], tw_sin[k : k + 1, :]
        zr = back[k * share : (k + 1) * share, :width]
        zi = back[k * share : (k + 1) * share, width:]
        twice = 1.0 if k in (0, half) else 2.0
        real.append((zr * c - zi * s) * twice)
        imag.append((zr * s + zi * c) * twice)
    smooth = [None] * sectors
    for d, (p, q) in enumerate(zip(cosine_sums(real), sine_sums(imag))):
        if q is None:
            smooth[d] = p
        else:
            smooth[d], smooth[sectors - d] = p - q, p + q
    edges = [zero, zero]
    for d in range(sectors):
        send_d[d * DEEP : d * DEEP + share, :] = smooth[d]
        for h in range(2):
            edges[h] = jnp.where((lane >> 3) == d, roll(smooth[d][8 * h : 8 * h + 8], 8 * d + 4), edges[h])
    beyond = [jnp.where(eight < 4, roll(v, 8), roll(v, -8)) for v in edges]
    for i in range(2):
        west, east = (beyond, edges) if i == 0 else (edges, beyond)
        for h, v in enumerate(swapped(*[jnp.where(eight < 4, w, e) for w, e in zip(west, east)])):
            send_d[pl.ds(8 * h * DEEP + share + i, 8, stride=DEEP), :] = v

    extra = share + 2 + SWEEPS + 1

    def put_cross(t, rows16):
        for h in range(2):
            send_d[pl.ds(8 * h * DEEP + share + 2 + t, 8, stride=DEEP), :] = rows16[8 * h : 8 * h + 8]

    @pl.when(keeper)
    def _():
        now, inverse, pull = [], [], []
        for d in range(sectors):
            top, low = d * DEEP, d * DEEP + 8
            now.append(jnp.where(last, send_d[low : low + 8, :], send_d[top : top + 8, :]))
            k = pole_recv[16 * d : 16 * d + 8, :]
            inverse.append(1.0 / (1.0 + 4.0 * k))
            pull.append(k * inverse[d])
        source = [a * b for a, b in zip(now, inverse)]
        ends = jnp.zeros((sectors, width), jnp.float32)
        wide = lax.broadcasted_iota(jnp.int32, (sectors, width), 1)
        for t in range(SWEEPS):
            tips = jnp.concatenate([jnp.where(last, x[7:8], x[0:1]) for x in now], axis=0)
            over = crossed(tips)
            put_cross(t, over)
            z = roll(over, 8 * t + 4)
            z = jnp.where((wide & 7) < 4, pltpu.roll(z, 1, 0), pltpu.roll(z, sectors - 1, 0))
            ends = jnp.where((wide >> 3) == t, z, ends)
            if t < SWEEPS - 1:
                right, left = [roll(x, 1) for x in now], [roll(x, -1) for x in now]
                later = []
                for d in range(sectors):
                    w = jnp.where(lane == 0, right[d - 1], right[d])
                    e = jnp.where(lane == width - 1, left[(d + 1) % sectors], left[d])
                    u = jnp.where((row8 == 0) & jnp.logical_not(last), over[d : d + 1], pltpu.roll(now[d], 1, 0))
                    b = jnp.where((row8 == 7) & last, over[d : d + 1], pltpu.roll(now[d], 7, 0))
                    later.append(source[d] + pull[d] * (w + e + u + b))
                now = later
        put_cross(SWEEPS, ends)
        across(send_d, recv_d, extra, d_s, d_r)

    @pl.when(jnp.logical_not(keeper))
    def _():
        across(send_d, recv_d, share + 2, d_s, d_r)

    recv_d[pl.ds(own, share), :] = send_d[pl.ds(own, share), :]
    recv_d[pl.ds(own + share, 2), :] = send_d[pl.ds(own + share, 2), :]

    @pl.when(keeper)
    def _():
        recv_d[pl.ds(own + share + 2, SWEEPS + 1), :] = send_d[pl.ds(own + share + 2, SWEEPS + 1), :]

    split_wait(5 * unit, 8 * unit, k_r, False)

    def corners(ref, diag, l):
        top, bottom = ref[l, PAD - 8 : PAD, :], ref[l, PAD + rows : PAD + rows + 8, :]
        nw, ne, sw, se = [diag[i, 8 * l : 8 * l + 8, :] for i in range(4)]
        first = jnp.where(
            lane < 8, roll(jnp.where(lane >= width - 4, nw, top), 4), roll(jnp.where(lane < 4, ne, top), 12)
        )
        second = jnp.where(
            lane < width - 8,
            jnp.where(lane < width - 12, roll(sw, -16), roll(bottom, -12)),
            jnp.where(lane < width - 4, roll(bottom, -4), roll(se, -8)),
        )
        return first, second

    def capped(first_tile, last_tile, first, second):
        return jnp.where(lane < 16, first, roll(last_tile, 16)), jnp.where(lane >= width - 16, second, roll(first_tile, -16))

    for l in range(lev):
        tiles = []

        def put(kk, tile, l=l, tiles=tiles):
            side_invert[l, 12 + 8 * kk : 20 + 8 * kk, :] = tile
            tiles.append(tile)

        sided(kap_send, kap_recv, 8 * l, put)
        top, bottom = capped(tiles[0], tiles[3], *corners(ka, kap_diag, l))
        side_invert[l, 4:12, :] = top
        side_invert[l, 44:52, :] = bottom
        for j in range(5):
            at = 8 + 8 * j
            k = side_invert[l, at : at + 8, :]
            inverse = 1.0 / (1.0 + 4.0 * k)
            side_invert[l, at : at + 8, :] = inverse
            side_coupling[l, at : at + 8, :] = k * inverse
    split_wait(5 * unit, 8 * unit, f_r, False)
    for l in range(lev):
        for at in (PAD - 8, PAD + rows):
            k = ka[l, at : at + 8, :]
            inverse = 1.0 / (1.0 + 4.0 * k)
            coupling[l, at : at + 8, :] = k * inverse
            scaled[l, at : at + 8, :] = field[l, at : at + 8, :] * inverse

        def put(kk, tile, l=l):
            side_tiles[32 * l + 8 * kk : 32 * l + 8 * kk + 8, :] = tile

        sided(adv_send, adv_recv, 8 * l, put)
        corner[0, 8 * l : 8 * l + 8, :], corner[1, 8 * l : 8 * l + 8, :] = corners(field, adv_diag, l)
        at = 32 * l
        early[0, l, 12:44, :] = side_tiles[at : at + 32, :]
        early[0, l, 4:12, :], early[0, l, 44:52, :] = capped(
            side_tiles[at : at + 8, :], side_tiles[at + 24 : at + 32, :],
            corner[0, 8 * l : 8 * l + 8, :], corner[1, 8 * l : 8 * l + 8, :],
        )
        early_scaled[l, 8:48, :] = early[0, l, 8:48, :] * side_invert[l, 8:48, :]

    weights = shift_weights(width, 1.0, 3, 12, 16)
    order = [(0, -1)] + [(i // 4, i % 4) for i in range(groups)] + [(groups // 4 - 1, 4)]
    at16 = lane & 15

    def sweep_early(t, carry):
        for l in range(lev):
            ends = {kk: rim(early[t, l, 12 + 8 * kk : 20 + 8 * kk, :], at16) for kk in range(-1, 5)}
            total = west_and_east(
                stack[t, l, PAD - 8 : PAD + rows + 8, :],
                [masked((lane >> 4) == g, ends[kk]) for g, kk in order], weights,
            )
            for i in range(groups + 2):
                at = PAD - 8 + 8 * i
                value = total[8 * i : 8 * i + 8] + (stack[t, l, at - 1 : at + 7, :] + stack[t, l, at + 1 : at + 9, :])
                stack[t + 1, l, at : at + 8, :] = scaled[l, at : at + 8, :] + coupling[l, at : at + 8, :] * value
            for j in range(5):
                at = 8 + 8 * j
                x = early[t, l, at : at + 8, :]
                value = roll(x, 1) + roll(x, -1) + early[t, l, at - 1 : at + 7, :] + early[t, l, at + 1 : at + 9, :]
                early[t + 1, l, at : at + 8, :] = (
                    early_scaled[l, at : at + 8, :] + side_coupling[l, at : at + 8, :] * value
                )
        return carry

    lax.fori_loop(0, SWEEPS, sweep_early, 0)

    plain_rows, more = (share + 2) * (sectors - 1), SWEEPS + 1
    bulk((share + 1) * (sectors - 1), a_s).wait_send()
    split_wait(3 * unit, 4 * unit, x_s, True)
    split_wait(5 * unit, 8 * unit, k_s, True)
    split_wait(5 * unit, 8 * unit, f_s, True)
    for here, pole_rows in ((keeper, 10 * (lev - 1)), (jnp.logical_not(keeper), 10 * lev)):
        @pl.when(here)
        def _(pole_rows=pole_rows):
            bulk(pole_rows, b_s).wait_send()

    d_waits = ((keeper, plain_rows + more * (lev - 1)), (jnp.logical_not(keeper), plain_rows + more * lev))
    for here, count in d_waits:
        @pl.when(here)
        def _(count=count):
            bulk(count, d_r).wait_recv()

    def cross(l, t):
        return recv_d[pl.ds((l * slices + tip_slice) * DEEP + share + 2 + t, 1), :]

    for k in range(sectors):
        l, q = k // slices, k % slices
        at = pl.ds(base + PAD + q * share, share)
        x = jnp.where(polar, recv_d[k * DEEP : k * DEEP + share, :], field[l, at, :])
        field[l, at, :] = x
        scaled[l, at, :] = x * invert[l, at, :]
    for l in range(lev):
        for here, at in ((north, PAD - 1), (last, PAD + rows)):
            field[l, at : at + 1, :] = jnp.where(here, cross(l, 0), field[l, at : at + 1, :])

    halo = jnp.concatenate([cross(l, SWEEPS) for l in range(lev)] * 2, axis=0)
    for t in range(SWEEPS):
        plain = jnp.concatenate([cross(l, t) for l in range(lev)] * 2, axis=0)
        z = jnp.where(
            lane < 8,
            jnp.where(lane < 4, roll(halo, -8 * t), roll(plain, 4)),
            jnp.where(lane < 12, roll(plain, 12), roll(halo, 8 - 8 * t)),
        )
        side_cross[t, :8, :] = jnp.where(last, roll(z, -16), z)
        side_cross[t, 8:, :] = plain

    strips = [
        [jnp.where(last, roll(v, -32), v) for v in swapped(*rows_of(recv_d, share + i))] for i in range(2)
    ]
    from_cap = jnp.where(last, lane - (width - 32), lane)
    inside_cap = polar & (from_cap >= 0) & (from_cap < 32)
    top_spot = north & (row8 == 7) & (lane < 16)
    bottom_spot = last & (row8 == 0) & (lane >= width - 16)
    for l in range(lev):
        tiles = []
        for kk in range(4):
            h, by = kk % 2, -32 * l - 8 * (kk // 2)
            z = jnp.where((lane & 15) < 8, roll(strips[0][h], by), roll(strips[1][h], by + 8))
            tile = jnp.where(inside_cap, z, side_tiles[32 * l + 8 * kk : 32 * l + 8 * kk + 8, :])
            side[l, 12 + 8 * kk : 20 + 8 * kk, :] = tile
            tiles.append(tile)
        at = 8 * l
        top, bottom = capped(tiles[0], tiles[3], corner[0, at : at + 8, :], corner[1, at : at + 8, :])
        side[l, 4:12, :] = jnp.where(top_spot, side_cross[0, l : l + 1, :], top)
        side[l, 44:52, :] = jnp.where(bottom_spot, side_cross[0, l : l + 1, :], bottom)
        for j in range(5):
            at = 8 + 8 * j
            side_scaled[l, at : at + 8, :] = side[l, at : at + 8, :] * side_invert[l, at : at + 8, :]

    for here, rows_out in ((keeper, extra * (sectors - 1)), (jnp.logical_not(keeper), plain_rows)):
        @pl.when(here)
        def _(rows_out=rows_out):
            bulk(rows_out, d_s).wait_send()


def relax(
    bands, stack, scaled, coupling, side0, side_scaled, side_coupling, side_cross, filtered, balanced, local, side, sems
):
    lev, rows, width = filtered.shape
    near = local.shape[2] - 2 * PAD
    tiles = near // 8 + 1
    lat = lax.axis_index("lat")
    north, last = lat == 0, lat == bands - 1
    base = pl.multiple_of(jnp.where(last, rows - near, 0), 8)
    rest = pl.multiple_of(jnp.where(last, 0, near), 8)
    copies = [
        pltpu.make_async_copy(stack.at[0, :, pl.ds(PAD, rows), :], filtered, sems.at[0]),
        pltpu.make_async_copy(
            stack.at[SWEEPS, :, pl.ds(rest + PAD, rows - near), :], balanced.at[:, pl.ds(rest, rows - near), :], sems.at[1]
        ),
    ]
    for copy in copies:
        copy.start()
    lane = lax.broadcasted_iota(jnp.int32, (8, width), 1)
    row8 = lax.broadcasted_iota(jnp.int32, (8, width), 0)
    at16 = lane & 15
    group = (lane >> 4) - jnp.where(last, (rows - near) // 32, 0)
    weights = shift_weights(width, 1.0, 3, 12, 16)
    for l in range(lev):
        local[0, l, PAD - 8 : PAD + near + 8, :] = stack[0, l, pl.ds(base + PAD - 8, near + 16), :]
    for t in range(SWEEPS):
        beside = side0 if t == 0 else side.at[t - 1]
        edges = []
        for l in range(lev):
            ends = {kk: rim(beside[l, 12 + 8 * kk : 20 + 8 * kk, :], at16) for kk in range(-1, 4)}
            edges.append(masked(lane < 16, ends[-1]))
            for i in range(near // 8):
                edges.append(masked(group == i // 4, ends[i % 4]))
        whole = jnp.concatenate([local[t, l, PAD - 8 : PAD + near, :] for l in range(lev)], axis=0)
        total = west_and_east(whole, edges, weights)
        for l in range(lev):
            for i in range(tiles):
                at = PAD - 8 + 8 * i
                start = 8 * (tiles * l + i)
                value = total[start : start + 8] + (local[t, l, at - 1 : at + 7, :] + local[t, l, at + 1 : at + 9, :])
                there = pl.ds(base + at, 8)
                value = scaled[l, there, :] + coupling[l, there, :] * value
                if t < SWEEPS - 1 and i == 0:
                    cross = side_cross[t + 1, 8 + l : 9 + l, :]
                    at_end = rows - near + PAD - 8
                    value = jnp.where(north & (row8 == 7), cross, value)
                    value = jnp.where(last, stack[t + 1, l, at_end : at_end + 8, :], value)
                    at_end = near + PAD
                    local[t + 1, l, at_end : at_end + 8, :] = jnp.where(
                        last, jnp.broadcast_to(cross, (8, width)), stack[t + 1, l, at_end : at_end + 8, :]
                    )
                local[t + 1, l, at : at + 8, :] = value
        if t == SWEEPS - 1:
            break
        for l in range(lev):
            for j in range(5):
                at = 8 + 8 * j
                x = beside[l, at : at + 8, :]
                value = pltpu.roll(x, 1, 1) + pltpu.roll(x, width - 1, 1)
                value = value + (beside[l, at - 1 : at + 7, :] + beside[l, at + 1 : at + 9, :])
                x = side_scaled[l, at : at + 8, :] + side_coupling[l, at : at + 8, :] * value
                cross = side_cross[t + 1, l : l + 1, :]
                if j == 0:
                    x = jnp.where(north & (row8 == 3) & (lane < 16), cross, x)
                if j == 4:
                    x = jnp.where(last & (row8 == 4) & (lane >= width - 16), cross, x)
                side[t, l, at : at + 8, :] = x
    copy = pltpu.make_async_copy(
        local.at[SWEEPS, :, pl.ds(PAD, near), :], balanced.at[:, pl.ds(base, near), :], sems.at[2]
    )
    copy.start()
    for copy in (*copies, copy):
        copy.wait()


def solution(mesh):
    sectors, bands = mesh.shape["lon"], mesh.shape["lat"]

    def per_device(tracer, wind_east, wind_north, kappa, cutoff, partner):
        lev, rows, width = tracer.shape
        f32 = jnp.float32
        high = rows + 2 * PAD

        def array(*shape):
            return pltpu.VMEM(shape, f32)

        block, tall = array(lev, rows, width), array(lev, high, width)
        strips = array(sectors * DEEP, width)
        pair, four = array(2, lev * 8, width), array(4, lev * 8, width)
        narrow = array(lev, 56, width)
        vmem = pl.BlockSpec(memory_space=pltpu.VMEM)
        hbm = pl.BlockSpec(memory_space=pltpu.HBM)
        tw_cos, tw_sin, fwd, inv = tables(sectors, width)
        blank = np.zeros((16 - tw_cos.shape[0], width), np.float32)
        table = np.concatenate([tw_cos, blank, tw_sin, blank], axis=0)
        fine = []
        for whole in (fwd, inv[:, :width], inv[:, width:]):
            first = whole.astype(jnp.bfloat16)
            fine += [first, first, (whole - first.astype(np.float32)).astype(jnp.bfloat16)]
        fine = np.concatenate(fine, axis=0)
        small = (cutoff.reshape(1, -1), partner.reshape(sectors, width), table, fine)
        dma = pltpu.SemaphoreType.DMA
        made = [(SWEEPS + 1, lev, high, width)] + [(lev, high, width)] * 2 + [(lev, 56, width)] * 3 + [(SWEEPS, 16, width)]
        limit = 24 * 1024 * 1024
        near = cutoff.shape[0] // 2 + 32
        held = pl.pallas_call(
            functools.partial(kernel, sectors, bands),
            out_shape=[jax.ShapeDtypeStruct(shape, f32) for shape in made],
            in_specs=[hbm] * 8,
            out_specs=[vmem] * len(made),
            scratch_shapes=[
                tall, block, block, tall,
                *[pltpu.VMEM(a.shape, a.dtype) for a in small],
                dma((8,)),
                strips, strips, array(16 * lev, width), array(16 * sectors, width), strips, strips,
                array(sectors, width),
                pair, pair, pair, pair, four, pair, pair, four, pair, tall, array(lev * 32, width), narrow, array(SWEEPS + 1, lev, 56, width), narrow,
                *[dma] * 12,
            ],
            compiler_params=pltpu.CompilerParams(collective_id=0, has_side_effects=True, vmem_limit_bytes=limit),
        )(
            *[pltpu.with_memory_space_constraint(jnp.asarray(a), pltpu.HBM) for a in (tracer, wind_east, wind_north, kappa, *small)]
        )
        return pl.pallas_call(
            functools.partial(relax, bands),
            out_shape=[jax.ShapeDtypeStruct(tracer.shape, f32)] * 2,
            in_specs=[vmem] * len(made),
            out_specs=[hbm] * 2,
            scratch_shapes=[array(SWEEPS + 1, lev, near + 2 * PAD, width), array(SWEEPS - 1, lev, 56, width), dma((3,))],
            compiler_params=pltpu.CompilerParams(vmem_limit_bytes=limit),
        )(*[pltpu.with_memory_space_constraint(a, pltpu.VMEM) for a in held])

    spec = P(None, "lat", "lon")
    return jax.shard_map(
        per_device, mesh=mesh, in_specs=(spec, spec, spec, spec, P(), P()), out_specs=(spec, spec),
        check_vma=False,
    )
```

```python
import functools
import math

import jax
import jax.numpy as jnp
import numpy as np
from jax import lax
from jax.experimental import pallas as pl
from jax.experimental.pallas import tpu as pltpu
from jax.sharding import PartitionSpec as P

KMAX = 512
SWEEPS = 4
COURANT = 0.4
HIGHEST = lax.Precision.HIGHEST


def tables(sectors, width):
    total = sectors * width
    half = sectors // 2
    m = np.arange(width)
    theta = 2.0 * np.pi * (np.outer(np.arange(half + 1), m) % total) / total
    kept = 2 * KMAX // sectors
    k2 = np.arange(kept) - kept // 2
    phase = 2.0 * np.pi * (np.outer(m, k2) % width) / width
    c, s = np.cos(phase), np.sin(phase)
    forward = np.block([[c, -s], [s, c]])
    inverse = np.block([[c.T, s.T], [-s.T, c.T]]) / total
    return [a.astype(np.float32) for a in (np.cos(theta), np.sin(theta), forward, inverse)]


def weighted(terms):
    total = None
    for factor, value in terms:
        if abs(factor) < 1e-12:
            continue
        part = value if abs(factor - 1.0) < 1e-12 else value * np.float32(factor)
        total = part if total is None else total + part
    return total


PAD = 16
DEEP = 24
MESH = pl.DeviceIdType.MESH


def taken(x, at_lane):
    return jnp.take_along_axis(x, at_lane, axis=1, mode="promise_in_bounds")


def parts(x):
    high = x.astype(jnp.bfloat16)
    return high, (x - high.astype(jnp.float32)).astype(jnp.bfloat16)


def shift_weights(width, east, west_lane, east_lane, lanes):
    one = lax.broadcasted_iota(jnp.int32, (width, width), 0)
    two = lax.broadcasted_iota(jnp.int32, (width, width), 1)
    shift = jnp.where(one - two == 1, east, 0.0) + jnp.where(two - one == 1, 1.0, 0.0)
    spot = one & (lanes - 1)
    edge = jnp.where((two == width - 1) & (spot == east_lane), east, 0.0)
    edge = edge + jnp.where((two == 0) & (spot == west_lane), 1.0, 0.0)
    shift, edge = shift.astype(jnp.bfloat16), edge.astype(jnp.bfloat16)
    return jnp.concatenate([shift, shift, edge, edge], axis=0)


def rim(h, at16):
    high, low = parts(jnp.where((at16 == 3) | (at16 == 12), h, 0.0))
    return high.astype(jnp.float32), low.astype(jnp.float32)


def masked(here, pair):
    return [jnp.where(here, x, 0.0) for x in pair]


def west_and_east(x, edges, weights):
    high, low = parts(x)
    rims = [jnp.concatenate(tiles, axis=0).astype(jnp.bfloat16) for tiles in zip(*edges)]
    return jnp.dot(jnp.concatenate([high, low, *rims], axis=1), weights, preferred_element_type=jnp.float32)


def refined(x, weights):
    high, low = parts(x)
    return jnp.dot(jnp.concatenate([high, low, high], axis=1), weights, preferred_element_type=jnp.float32)


def kernel(
    sectors, bands,
    tracer_h, wind_east_h, wind_north_h, kappa_h, cutoff_h, partner_h, table_h, fine_h,
    stack, scaled, coupling, side, side_scaled, side_coupling, side_cross,
    tr, we, wn, ka, cutoff, partner, table, fine, load_s,
    send_a, recv_a, pole_send, pole_recv, send_d, recv_d, beyond_fix,
    rim_send, rim_recv, kap_send, kap_recv, kap_diag, adv_send, adv_recv, adv_diag, corner, invert, side_tiles, side_invert, early, early_scaled,
    a_s, a_r, b_s, b_r, d_s, d_r, x_s, x_r, k_s, k_r, f_s, f_r,
):
    lev, rows, width = we.shape
    field = stack.at[0]
    pole = cutoff.shape[1] // 2
    share = lev * pole // sectors
    slices = sectors // lev
    half = sectors // 2
    groups = rows // 8
    lat = lax.axis_index("lat")
    lon = lax.axis_index("lon")
    last = lat == bands - 1
    north = lat == 0
    polar = north | last

    def sector(offset):
        return lax.rem(lon + (offset % sectors), sectors)

    def band(offset):
        return lax.rem(lat + (offset % bands), bands)

    body = pl.ds(PAD, rows)
    held = (tracer_h, wind_east_h, wind_north_h, kappa_h, partner_h, cutoff_h, table_h, fine_h)
    near = (tr.at[:, body, :], we, wn, ka.at[:, body, :], partner, cutoff, table, fine)
    loads = [pltpu.make_async_copy(h, v, load_s.at[i]) for i, (h, v) in enumerate(zip(held, near))]
    for load in loads[:3]:
        load.start()

    barrier = pltpu.get_barrier_semaphore()
    for t in range(1, sectors):
        pl.semaphore_signal(barrier, inc=1, device_id=(lat, sector(t)), device_id_type=MESH)
    beside = (1,) if bands == 2 else (1, -1)
    for t in beside:
        for i in (-1, 0, 1):
            pl.semaphore_signal(barrier, inc=1, device_id=(band(t), sector(i)), device_id_type=MESH)

    for load in loads[3:]:
        load.start()

    lane = lax.broadcasted_iota(jnp.int32, (8, width), 1)
    row8 = lax.broadcasted_iota(jnp.int32, (8, width), 0)
    zero = jnp.zeros((8, width), jnp.float32)

    def roll(x, by):
        by = by % width
        return x if by == 0 else pltpu.roll(x, by, 1)

    def swapped(v0, v1):
        low = lane < width // 2
        v0, v1 = jnp.where(low, v0, roll(v1, width // 2)), jnp.where(low, roll(v0, width // 2), v1)
        out = []
        for v in (v0, v1):
            for b in (2, 1, 0):
                step, hop = 1 << b, 8 << b
                upper = (lane & hop) != 0
                same = ((row8 >> b) & 1) == ((lane >> (3 + b)) & 1)
                v = jnp.where(
                    same, v,
                    jnp.where(upper, pltpu.roll(roll(v, hop), 8 - step, 0), pltpu.roll(roll(v, -hop), step, 0)),
                )
            out.append(v)
        return out

    base = pl.multiple_of(jnp.where(last, rows - pole, 0), 8)
    tip = jnp.where(last, rows - 1, 0)
    tip_tile = pl.multiple_of(jnp.where(last, rows - 8, 0), 8)
    tip_slice = jnp.where(last, slices - 1, 0)
    keeper = lax.rem(lon, slices) == tip_slice

    @pl.when(north)
    def _():
        for l in range(lev):
            tr[l, PAD - 8 : PAD, :] = zero

    @pl.when(last)
    def _():
        for l in range(lev):
            tr[l, PAD + rows : PAD + rows + 8, :] = zero

    for load in loads[:3]:
        load.wait()
    lane_p = lax.broadcasted_iota(jnp.int32, (pole, width), 1)
    row_p = lax.broadcasted_iota(jnp.int32, (pole, width), 0)
    before = jnp.where(last, rows - pole - 1, 0)
    after = jnp.where(last, rows - 1, pole)
    eight = lane & 7
    packs = [zero, zero]
    for l in range(lev):
        x = tr[l, pl.ds(base + PAD, pole), :]
        east_wind = we[l, pl.ds(base, pole), :]
        w = jnp.where(lane_p == 0, 0.0, pltpu.roll(x, 1, 1))
        e = jnp.where(lane_p == width - 1, 0.0, pltpu.roll(x, width - 1, 1))
        above = jnp.where(last, tr[l, pl.ds(PAD + before, 1), :], 0.0)
        below = jnp.where(last, 0.0, tr[l, pl.ds(PAD + after, 1), :])
        u = jnp.where(row_p == 0, above, pltpu.roll(x, 1, 0))
        d = jnp.where(row_p == pole - 1, below, pltpu.roll(x, pole - 1, 0))
        stage = x - COURANT * 0.5 * (east_wind * (e - w) + wn[l, pl.ds(base, pole), :] * (d - u))
        for q in range(slices):
            k = l * slices + q
            send_a[k * DEEP : k * DEEP + share, :] = stage[q * share : (q + 1) * share]
            for h in range(2):
                at = q * share + 8 * h
                t = jnp.where(
                    (eight == 3) | (eight == 4), roll(x[at : at + 8], 4 + 8 * k), roll(east_wind[at : at + 8], 6 + 8 * k)
                )
                packs[h] = jnp.where((lane >> 3) == k, t, packs[h])
    for h, v in enumerate(swapped(*packs)):
        send_a[pl.ds(8 * h * DEEP + share, 8, stride=DEEP), :] = v

    def across(src, dst, count, ss, rs):
        for t in range(1, sectors):
            there = sector(t)
            pltpu.make_async_remote_copy(
                src_ref=src.at[pl.ds(pl.multiple_of(there * DEEP, 8), count), :],
                dst_ref=dst.at[pl.ds(pl.multiple_of(lon * DEEP, 8), count), :],
                send_sem=ss, recv_sem=rs, device_id=(lat, there), device_id_type=MESH,
            ).start()

    def bulk(count, sem):
        whole = send_d.at[pl.ds(0, count), :]
        return pltpu.make_async_remote_copy(
            src_ref=whole, dst_ref=whole, send_sem=sem, recv_sem=sem, device_id=(lat, sector(1)), device_id_type=MESH
        )

    def split_wait(single, double, sem, send):
        for here, count in ((polar, single), (jnp.logical_not(polar), double)):
            @pl.when(here)
            def _(count=count):
                if send:
                    bulk(count, sem).wait_send()
                else:
                    bulk(count, sem).wait_recv()

    four = lane >> 2

    def packed(tiles):
        first, second = zero, zero
        for g, x in enumerate(tiles):
            z = roll(x, 4 * g + 4)
            first = jnp.where(four == g, z, first)
            second = jnp.where(four == (g + 1) % groups, z, second)
        return first, second

    def pack_rims(source, target):
        def one(l, carry):
            at = pl.multiple_of(8 * l, 8)
            first, second = packed([source[l, PAD + 8 * g : PAD + 8 * g + 8, :] for g in range(groups)])
            target[0, pl.ds(at, 8), :] = first
            target[1, pl.ds(at, 8), :] = second
            return carry

        lax.fori_loop(0, lev, one, 0)

    def sideways(src, dst, ss, rs):
        for j in range(2):
            pltpu.make_async_remote_copy(
                src_ref=src.at[j], dst_ref=dst.at[j], send_sem=ss, recv_sem=rs,
                device_id=(lat, sector(1 - 2 * j)), device_id_type=MESH,
            ).start()

    def poleward(ref, ss, rs, send=None, recv=None):
        for i, step in enumerate((1, -1)):
            plan = [
                (
                    ref.at[:, pl.ds(PAD + rows - 8 if step == 1 else PAD, 8), :],
                    ref.at[:, pl.ds(PAD - 8 if step == 1 else PAD + rows, 8), :], 0,
                )
            ]
            if send is not None:
                plan += [(send.at[j], recv.at[2 * i + j], 1 - 2 * j) for j in range(2)]

            @pl.when(lat < bands - 1 if step == 1 else lat > 0)
            def _(step=step, plan=plan):
                for src, dst, aside in plan:
                    pltpu.make_async_remote_copy(
                        src_ref=src, dst_ref=dst, send_sem=ss, recv_sem=rs,
                        device_id=(band(step), sector(aside)), device_id_type=MESH,
                    ).start()

    unit = 8 * lev
    pack_rims(tr, rim_send)
    pl.semaphore_wait(barrier, sectors - 1 + 3 * len(beside))
    sideways(rim_send, rim_recv, x_s, x_r)
    poleward(tr, x_s, x_r)
    across(send_a, recv_a, share + 1, a_s, a_r)

    loads[3].wait()
    for l in range(lev):
        pole_send[16 * l : 16 * l + 8, :] = ka[l, pl.ds(tip_tile + PAD, 8), :]
        pole_send[16 * l + 8 : 16 * l + 9, :] = tr[l, pl.ds(tip + PAD, 1), :]
        pole_send[16 * l + 9 : 16 * l + 10, :] = wn[l, pl.ds(tip, 1), :]

    def pole_copy(l):
        return pltpu.make_async_remote_copy(
            src_ref=pole_send.at[pl.ds(16 * l, 10), :], dst_ref=pole_recv.at[pl.ds(pl.multiple_of(16 * lon, 8), 10), :],
            send_sem=b_s, recv_sem=b_r,
            device_id=(lat, l * slices + tip_slice), device_id_type=MESH,
        )

    for l in range(lev):
        @pl.when(lon != l * slices + tip_slice)
        def _(l=l):
            pole_copy(l).start()

        @pl.when(lon == l * slices + tip_slice)
        def _(l=l):
            pole_recv[pl.ds(pl.multiple_of(16 * lon, 8), 8), :] = pole_send[16 * l : 16 * l + 8, :]
            pole_recv[pl.ds(pl.multiple_of(16 * lon, 8) + 8, 2), :] = pole_send[16 * l + 8 : 16 * l + 10, :]

    pack_rims(ka, kap_send)
    sideways(kap_send, kap_recv, k_s, k_r)
    poleward(ka, k_s, k_r, kap_send, kap_diag)
    for load in loads[4:]:
        load.wait()

    start = lax.broadcasted_iota(jnp.int32, (sectors, width), 0) + half
    reach = partner[...] - jnp.where(start >= sectors, start - sectors, start) * width
    reach = jnp.where(reach < 0, reach + sectors * width, reach)
    farther = reach >= width
    at_lane = jnp.where(farther, reach - width, reach)

    def crossed(points):
        return jnp.where(
            farther, taken(pltpu.roll(points, sectors - half - 1, 0), at_lane), taken(pltpu.roll(points, half, 0), at_lane)
        )


    change = shift_weights(width, -1.0, 3, 2, 4)
    split_wait(3 * unit, 4 * unit, x_r, False)
    for l in range(lev):
        edge = jnp.where((lane & 3) == 3, rim_recv[0, 8 * l : 8 * l + 8, :], roll(rim_recv[1, 8 * l : 8 * l + 8, :], -2))
        edge = [x.astype(jnp.float32) for x in parts(edge)]
        across_west = west_and_east(
            tr[l, PAD : PAD + rows, :], [masked(four == g, edge) for g in range(groups)], change
        )
        tiles = []
        for g in range(groups):
            at = PAD + 8 * g
            x = tr[l, at : at + 8, :]
            turn = wn[l, 8 * g : 8 * g + 8, :] * (tr[l, at + 1 : at + 9, :] - tr[l, at - 1 : at + 7, :])
            push = we[l, 8 * g : 8 * g + 8, :] * across_west[8 * g : 8 * g + 8]
            value = x + COURANT * 0.5 * (push - turn)
            field[l, at : at + 8, :] = value
            k = ka[l, at : at + 8, :]
            inverse = 1.0 / (1.0 + 4.0 * k)
            invert[l, at : at + 8, :] = inverse
            coupling[l, at : at + 8, :] = k * inverse
            scaled[l, at : at + 8, :] = value * inverse
            tiles.append(value)
        first, second = packed(tiles)
        adv_send[0, 8 * l : 8 * l + 8, :] = first
        adv_send[1, 8 * l : 8 * l + 8, :] = second

    def sided(send, recv, at, put):
        for kk in range(4):
            mine = (four & 3) == kk
            near_west = jnp.where(mine, recv[0, at : at + 8, :], send[1, at : at + 8, :])
            near_east = jnp.where(mine, send[0, at : at + 8, :], recv[1, at : at + 8, :])
            put(kk, jnp.where((lane & 15) < 8, roll(near_west, -4 * kk), roll(near_east, 8 - 4 * kk)))

    sideways(adv_send, adv_recv, f_s, f_r)
    poleward(field, f_s, f_r, adv_send, adv_diag)

    beyond_fix[...] = jnp.zeros_like(beyond_fix)

    @pl.when(keeper)
    def _():
        bulk(10 * (sectors - 1), b_r).wait_recv()
        tips = jnp.concatenate([pole_recv[16 * d + 8 : 16 * d + 9, :] for d in range(sectors)], axis=0)
        winds = jnp.concatenate([pole_recv[16 * d + 9 : 16 * d + 10, :] for d in range(sectors)], axis=0)
        turned = COURANT * 0.5 * winds * crossed(tips)
        beyond_fix[...] = jnp.where(last, -turned, turned)

    first = jnp.where(last, pole, 0) + lax.rem(lon, slices) * share
    spot = lax.broadcasted_iota(jnp.int32, (share, 2 * pole), 0) + first
    limit = jnp.sum(
        jnp.where(
            lax.broadcasted_iota(jnp.int32, (share, 2 * pole), 1) == spot,
            cutoff[...].astype(jnp.float32), 0.0,
        ),
        axis=1, keepdims=True,
    )
    kept = 2 * KMAX // sectors
    slot = lax.broadcasted_iota(jnp.int32, (share, 2 * kept), 1)
    wave = sectors * (jnp.where(slot < kept, slot, slot - kept) - kept // 2)
    own = pl.multiple_of(lon * DEEP, 8)
    recv_a[pl.ds(own, share), :] = send_a[pl.ds(own, share), :]
    recv_a[pl.ds(own + share, 1), :] = send_a[pl.ds(own + share, 1), :]
    bulk((share + 1) * (sectors - 1), a_r).wait_recv()
    tw_cos, tw_sin = table[0 : half + 1, :], table[16 : half + 17, :]
    fwd = fine[: 6 * width, :]
    inv = jnp.concatenate([fine[6 * width : 9 * width, :], fine[9 * width :, :]], axis=1)

    def rows_of(ref, at):
        return [ref[pl.ds(8 * h * DEEP + at, 8, stride=DEEP), :] for h in range(2)]

    fixes = []
    for v in swapped(*rows_of(recv_a, share)):
        fixes.append(COURANT * 0.5 * v * jnp.where(eight == 6, roll(v, 11), -roll(v, -7)))
    at_tip = [(row8 == 0) & north & keeper, (row8 == 7) & last & keeper]
    ends = (lane == 0) | (lane == width - 1)
    spread = []
    for d in range(sectors):
        halves = []
        for h in range(2):
            x = recv_a[d * DEEP + 8 * h : d * DEEP + 8 * h + 8, :]
            x = x + jnp.where(ends, roll(fixes[h], -(8 * d + 6)), 0.0)
            halves.append(x + jnp.where(at_tip[h], beyond_fix[d : d + 1, :], 0.0))
        spread.append(jnp.concatenate(halves, axis=0))

    def circle(d, k):
        angle = 2.0 * math.pi * ((d * k) % sectors) / sectors
        return math.cos(angle), math.sin(angle)

    even = [spread[0]] + [spread[d] + spread[sectors - d] for d in range(1, half)] + [spread[half]]
    odd = [None] + [spread[d] - spread[sectors - d] for d in range(1, half)]
    blocks = []
    for k in range(half + 1):
        c, s = tw_cos[k : k + 1, :], tw_sin[k : k + 1, :]
        re = weighted([(circle(d, k)[0], even[d]) for d in range(half + 1)])
        im = weighted([(-circle(d, k)[1], odd[d]) for d in range(1, half)])
        if im is None:
            blocks.append(jnp.concatenate([re * c, -(re * s)], axis=1))
        else:
            blocks.append(jnp.concatenate([re * c + im * s, im * c - re * s], axis=1))
    spectrum = refined(jnp.concatenate(blocks, axis=0), fwd)
    keep = jnp.concatenate(
        [jnp.where(jnp.abs(wave + k).astype(jnp.float32) <= limit, 1.0, 0.0) for k in range(half + 1)], axis=0
    )
    back = refined(jnp.where(keep > 0.0, spectrum, 0.0), inv)
    real, imag = [], []
    for k in range(half + 1):
        c, s = tw_cos[k : k + 1, :], tw_sin[k : k + 1, :]
        zr = back[k * share : (k + 1) * share, :width]
        zi = back[k * share : (k + 1) * share, width:]
        twice = 1.0 if k in (0, half) else 2.0
        real.append((zr * c - zi * s) * twice)
        imag.append((zr * s + zi * c) * twice)
    smooth = [None] * sectors
    for d in range(half + 1):
        p = weighted([(circle(d, k)[0], real[k]) for k in range(half + 1)])
        q = weighted([(circle(d, k)[1], imag[k]) for k in range(1, half)])
        if q is None:
            smooth[d] = p
        else:
            smooth[d], smooth[sectors - d] = p - q, p + q
    edges = [zero, zero]
    for d in range(sectors):
        send_d[d * DEEP : d * DEEP + share, :] = smooth[d]
        for h in range(2):
            edges[h] = jnp.where((lane >> 3) == d, roll(smooth[d][8 * h : 8 * h + 8], 8 * d + 4), edges[h])
    beyond = [jnp.where(eight < 4, roll(v, 8), roll(v, -8)) for v in edges]
    for i in range(2):
        west, east = (beyond, edges) if i == 0 else (edges, beyond)
        for h, v in enumerate(swapped(*[jnp.where(eight < 4, w, e) for w, e in zip(west, east)])):
            send_d[pl.ds(8 * h * DEEP + share + i, 8, stride=DEEP), :] = v

    extra = share + 2 + SWEEPS + 1

    def put_cross(t, rows16):
        for h in range(2):
            send_d[pl.ds(8 * h * DEEP + share + 2 + t, 8, stride=DEEP), :] = rows16[8 * h : 8 * h + 8]

    @pl.when(keeper)
    def _():
        now, inverse, pull = [], [], []
        for d in range(sectors):
            top, low = d * DEEP, d * DEEP + 8
            now.append(jnp.where(last, send_d[low : low + 8, :], send_d[top : top + 8, :]))
            k = pole_recv[16 * d : 16 * d + 8, :]
            inverse.append(1.0 / (1.0 + 4.0 * k))
            pull.append(k * inverse[d])
        source = [a * b for a, b in zip(now, inverse)]
        ends = jnp.zeros((sectors, width), jnp.float32)
        wide = lax.broadcasted_iota(jnp.int32, (sectors, width), 1)
        for t in range(SWEEPS):
            tips = jnp.concatenate([jnp.where(last, x[7:8], x[0:1]) for x in now], axis=0)
            over = crossed(tips)
            put_cross(t, over)
            z = roll(over, 8 * t + 4)
            z = jnp.where((wide & 7) < 4, pltpu.roll(z, 1, 0), pltpu.roll(z, sectors - 1, 0))
            ends = jnp.where((wide >> 3) == t, z, ends)
            if t < SWEEPS - 1:
                right, left = [roll(x, 1) for x in now], [roll(x, -1) for x in now]
                later = []
                for d in range(sectors):
                    w = jnp.where(lane == 0, right[d - 1], right[d])
                    e = jnp.where(lane == width - 1, left[(d + 1) % sectors], left[d])
                    u = jnp.where((row8 == 0) & jnp.logical_not(last), over[d : d + 1], pltpu.roll(now[d], 1, 0))
                    b = jnp.where((row8 == 7) & last, over[d : d + 1], pltpu.roll(now[d], 7, 0))
                    later.append(source[d] + pull[d] * (w + e + u + b))
                now = later
        put_cross(SWEEPS, ends)
        across(send_d, recv_d, extra, d_s, d_r)

    @pl.when(jnp.logical_not(keeper))
    def _():
        across(send_d, recv_d, share + 2, d_s, d_r)

    recv_d[pl.ds(own, share), :] = send_d[pl.ds(own, share), :]
    recv_d[pl.ds(own + share, 2), :] = send_d[pl.ds(own + share, 2), :]

    @pl.when(keeper)
    def _():
        recv_d[pl.ds(own + share + 2, SWEEPS + 1), :] = send_d[pl.ds(own + share + 2, SWEEPS + 1), :]

    split_wait(5 * unit, 8 * unit, k_r, False)

    def corners(ref, diag, l):
        top, bottom = ref[l, PAD - 8 : PAD, :], ref[l, PAD + rows : PAD + rows + 8, :]
        nw, ne, sw, se = [diag[i, 8 * l : 8 * l + 8, :] for i in range(4)]
        first = jnp.where(
            lane < 8, roll(jnp.where(lane >= width - 4, nw, top), 4), roll(jnp.where(lane < 4, ne, top), 12)
        )
        second = jnp.where(
            lane < width - 8,
            jnp.where(lane < width - 12, roll(sw, -16), roll(bottom, -12)),
            jnp.where(lane < width - 4, roll(bottom, -4), roll(se, -8)),
        )
        return first, second

    def capped(first_tile, last_tile, first, second):
        return jnp.where(lane < 16, first, roll(last_tile, 16)), jnp.where(lane >= width - 16, second, roll(first_tile, -16))

    for l in range(lev):
        tiles = []

        def put(kk, tile, l=l, tiles=tiles):
            side_invert[l, 12 + 8 * kk : 20 + 8 * kk, :] = tile
            tiles.append(tile)

        sided(kap_send, kap_recv, 8 * l, put)
        top, bottom = capped(tiles[0], tiles[3], *corners(ka, kap_diag, l))
        side_invert[l, 4:12, :] = top
        side_invert[l, 44:52, :] = bottom
        for j in range(5):
            at = 8 + 8 * j
            k = side_invert[l, at : at + 8, :]
            inverse = 1.0 / (1.0 + 4.0 * k)
            side_invert[l, at : at + 8, :] = inverse
            side_coupling[l, at : at + 8, :] = k * inverse
    split_wait(5 * unit, 8 * unit, f_r, False)
    for l in range(lev):
        for at in (PAD - 8, PAD + rows):
            k = ka[l, at : at + 8, :]
            inverse = 1.0 / (1.0 + 4.0 * k)
            coupling[l, at : at + 8, :] = k * inverse
            scaled[l, at : at + 8, :] = field[l, at : at + 8, :] * inverse

        def put(kk, tile, l=l):
            side_tiles[32 * l + 8 * kk : 32 * l + 8 * kk + 8, :] = tile

        sided(adv_send, adv_recv, 8 * l, put)
        corner[0, 8 * l : 8 * l + 8, :], corner[1, 8 * l : 8 * l + 8, :] = corners(field, adv_diag, l)
        at = 32 * l
        early[0, l, 12:44, :] = side_tiles[at : at + 32, :]
        early[0, l, 4:12, :], early[0, l, 44:52, :] = capped(
            side_tiles[at : at + 8, :], side_tiles[at + 24 : at + 32, :],
            corner[0, 8 * l : 8 * l + 8, :], corner[1, 8 * l : 8 * l + 8, :],
        )
        early_scaled[l, 8:48, :] = early[0, l, 8:48, :] * side_invert[l, 8:48, :]

    weights = shift_weights(width, 1.0, 3, 12, 16)
    order = [(0, -1)] + [(i // 4, i % 4) for i in range(groups)] + [(groups // 4 - 1, 4)]
    at16 = lane & 15

    def sweep_early(t, carry):
        for l in range(lev):
            ends = {kk: rim(early[t, l, 12 + 8 * kk : 20 + 8 * kk, :], at16) for kk in range(-1, 5)}
            total = west_and_east(
                stack[t, l, PAD - 8 : PAD + rows + 8, :],
                [masked((lane >> 4) == g, ends[kk]) for g, kk in order], weights,
            )
            for i in range(groups + 2):
                at = PAD - 8 + 8 * i
                value = total[8 * i : 8 * i + 8] + (stack[t, l, at - 1 : at + 7, :] + stack[t, l, at + 1 : at + 9, :])
                stack[t + 1, l, at : at + 8, :] = scaled[l, at : at + 8, :] + coupling[l, at : at + 8, :] * value
            for j in range(5):
                at = 8 + 8 * j
                x = early[t, l, at : at + 8, :]
                value = roll(x, 1) + roll(x, -1) + early[t, l, at - 1 : at + 7, :] + early[t, l, at + 1 : at + 9, :]
                early[t + 1, l, at : at + 8, :] = (
                    early_scaled[l, at : at + 8, :] + side_coupling[l, at : at + 8, :] * value
                )
        return carry

    lax.fori_loop(0, SWEEPS, sweep_early, 0)

    plain_rows, more = (share + 2) * (sectors - 1), SWEEPS + 1
    d_waits = ((keeper, plain_rows + more * (lev - 1)), (jnp.logical_not(keeper), plain_rows + more * lev))
    for here, count in d_waits:
        @pl.when(here)
        def _(count=count):
            bulk(count, d_r).wait_recv()

    def cross(l, t):
        return recv_d[pl.ds((l * slices + tip_slice) * DEEP + share + 2 + t, 1), :]

    @pl.when(polar)
    def _():
        for k in range(sectors):
            l, q = k // slices, k % slices
            x = recv_d[k * DEEP : k * DEEP + share, :]
            at = base + PAD + q * share
            field[l, pl.ds(at, share), :] = x
            scaled[l, pl.ds(at, share), :] = x * invert[l, pl.ds(at, share), :]

    @pl.when(north)
    def _():
        for l in range(lev):
            field[l, PAD - 1 : PAD, :] = cross(l, 0)

    @pl.when(last)
    def _():
        for l in range(lev):
            field[l, PAD + rows : PAD + rows + 1, :] = cross(l, 0)

    halo = jnp.concatenate([cross(l, SWEEPS) for l in range(lev)] * 2, axis=0)
    for t in range(SWEEPS):
        plain = jnp.concatenate([cross(l, t) for l in range(lev)] * 2, axis=0)
        z = jnp.where(
            lane < 8,
            jnp.where(lane < 4, roll(halo, -8 * t), roll(plain, 4)),
            jnp.where(lane < 12, roll(plain, 12), roll(halo, 8 - 8 * t)),
        )
        side_cross[t, :8, :] = jnp.where(last, roll(z, -16), z)
        side_cross[t, 8:, :] = plain

    strips = [
        [jnp.where(last, roll(v, -32), v) for v in swapped(*rows_of(recv_d, share + i))] for i in range(2)
    ]
    from_cap = jnp.where(last, lane - (width - 32), lane)
    inside_cap = polar & (from_cap >= 0) & (from_cap < 32)
    top_spot = north & (row8 == 7) & (lane < 16)
    bottom_spot = last & (row8 == 0) & (lane >= width - 16)
    for l in range(lev):
        tiles = []
        for kk in range(4):
            h, by = kk % 2, -32 * l - 8 * (kk // 2)
            z = jnp.where((lane & 15) < 8, roll(strips[0][h], by), roll(strips[1][h], by + 8))
            tile = jnp.where(inside_cap, z, side_tiles[32 * l + 8 * kk : 32 * l + 8 * kk + 8, :])
            side[l, 12 + 8 * kk : 20 + 8 * kk, :] = tile
            tiles.append(tile)
        at = 8 * l
        top, bottom = capped(tiles[0], tiles[3], corner[0, at : at + 8, :], corner[1, at : at + 8, :])
        side[l, 4:12, :] = jnp.where(top_spot, side_cross[0, l : l + 1, :], top)
        side[l, 44:52, :] = jnp.where(bottom_spot, side_cross[0, l : l + 1, :], bottom)
        for j in range(5):
            at = 8 + 8 * j
            side_scaled[l, at : at + 8, :] = side[l, at : at + 8, :] * side_invert[l, at : at + 8, :]

    bulk((share + 1) * (sectors - 1), a_s).wait_send()
    split_wait(3 * unit, 4 * unit, x_s, True)
    split_wait(5 * unit, 8 * unit, k_s, True)
    split_wait(5 * unit, 8 * unit, f_s, True)
    for here, pole_rows, rows_out in (
        (keeper, 10 * (lev - 1), extra * (sectors - 1)), (jnp.logical_not(keeper), 10 * lev, plain_rows)
    ):
        @pl.when(here)
        def _(pole_rows=pole_rows, rows_out=rows_out):
            bulk(pole_rows, b_s).wait_send()
            bulk(rows_out, d_s).wait_send()


def relax(
    bands, stack, scaled, coupling, side0, side_scaled, side_coupling, side_cross, filtered, balanced, local, side, sems
):
    lev, rows, width = filtered.shape
    near = local.shape[2] - 2 * PAD
    tiles = near // 8 + 1
    lat = lax.axis_index("lat")
    north, last = lat == 0, lat == bands - 1
    base = pl.multiple_of(jnp.where(last, rows - near, 0), 8)
    rest = pl.multiple_of(jnp.where(last, 0, near), 8)
    copies = [
        pltpu.make_async_copy(stack.at[0, :, pl.ds(PAD, rows), :], filtered, sems.at[0]),
        pltpu.make_async_copy(
            stack.at[SWEEPS, :, pl.ds(rest + PAD, rows - near), :], balanced.at[:, pl.ds(rest, rows - near), :], sems.at[1]
        ),
    ]
    for copy in copies:
        copy.start()
    lane = lax.broadcasted_iota(jnp.int32, (8, width), 1)
    row8 = lax.broadcasted_iota(jnp.int32, (8, width), 0)
    at16 = lane & 15
    group = (lane >> 4) - jnp.where(last, (rows - near) // 32, 0)
    weights = shift_weights(width, 1.0, 3, 12, 16)
    for l in range(lev):
        local[0, l, PAD - 8 : PAD + near + 8, :] = stack[0, l, pl.ds(base + PAD - 8, near + 16), :]
    for t in range(SWEEPS):
        beside = side0 if t == 0 else side.at[t - 1]
        edges = []
        for l in range(lev):
            ends = {kk: rim(beside[l, 12 + 8 * kk : 20 + 8 * kk, :], at16) for kk in range(-1, 4)}
            edges.append(masked(lane < 16, ends[-1]))
            for i in range(near // 8):
                edges.append(masked(group == i // 4, ends[i % 4]))
        whole = jnp.concatenate([local[t, l, PAD - 8 : PAD + near, :] for l in range(lev)], axis=0)
        total = west_and_east(whole, edges, weights)
        for l in range(lev):
            for i in range(tiles):
                at = PAD - 8 + 8 * i
                start = 8 * (tiles * l + i)
                value = total[start : start + 8] + (local[t, l, at - 1 : at + 7, :] + local[t, l, at + 1 : at + 9, :])
                there = pl.ds(base + at, 8)
                value = scaled[l, there, :] + coupling[l, there, :] * value
                if t < SWEEPS - 1 and i == 0:
                    cross = side_cross[t + 1, 8 + l : 9 + l, :]
                    at_end = rows - near + PAD - 8
                    value = jnp.where(north & (row8 == 7), cross, value)
                    value = jnp.where(last, stack[t + 1, l, at_end : at_end + 8, :], value)
                    at_end = near + PAD
                    local[t + 1, l, at_end : at_end + 8, :] = jnp.where(
                        last, jnp.broadcast_to(cross, (8, width)), stack[t + 1, l, at_end : at_end + 8, :]
                    )
                local[t + 1, l, at : at + 8, :] = value
        if t == SWEEPS - 1:
            break
        for l in range(lev):
            for j in range(5):
                at = 8 + 8 * j
                x = beside[l, at : at + 8, :]
                value = pltpu.roll(x, 1, 1) + pltpu.roll(x, width - 1, 1)
                value = value + (beside[l, at - 1 : at + 7, :] + beside[l, at + 1 : at + 9, :])
                x = side_scaled[l, at : at + 8, :] + side_coupling[l, at : at + 8, :] * value
                cross = side_cross[t + 1, l : l + 1, :]
                if j == 0:
                    x = jnp.where(north & (row8 == 3) & (lane < 16), cross, x)
                if j == 4:
                    x = jnp.where(last & (row8 == 4) & (lane >= width - 16), cross, x)
                side[t, l, at : at + 8, :] = x
    copy = pltpu.make_async_copy(
        local.at[SWEEPS, :, pl.ds(PAD, near), :], balanced.at[:, pl.ds(base, near), :], sems.at[2]
    )
    copy.start()
    for copy in (*copies, copy):
        copy.wait()


def solution(mesh):
    sectors, bands = mesh.shape["lon"], mesh.shape["lat"]

    def per_device(tracer, wind_east, wind_north, kappa, cutoff, partner):
        lev, rows, width = tracer.shape
        f32 = jnp.float32
        high = rows + 2 * PAD

        def array(*shape):
            return pltpu.VMEM(shape, f32)

        block, tall = array(lev, rows, width), array(lev, high, width)
        strips = array((sectors + 1) * DEEP, width)
        pair, four = array(2, lev * 8, width), array(4, lev * 8, width)
        narrow = array(lev, 56, width)
        vmem = pl.BlockSpec(memory_space=pltpu.VMEM)
        hbm = pl.BlockSpec(memory_space=pltpu.HBM)
        tw_cos, tw_sin, fwd, inv = tables(sectors, width)
        blank = np.zeros((16 - tw_cos.shape[0], width), np.float32)
        table = np.concatenate([tw_cos, blank, tw_sin, blank], axis=0)
        fine = []
        for whole in (fwd, inv[:, :width], inv[:, width:]):
            first = whole.astype(jnp.bfloat16)
            fine += [first, first, (whole - first.astype(np.float32)).astype(jnp.bfloat16)]
        fine = np.concatenate(fine, axis=0)
        small = (cutoff.reshape(1, -1), partner.reshape(sectors, width), table, fine)
        dma = pltpu.SemaphoreType.DMA
        made = [(SWEEPS + 1, lev, high, width)] + [(lev, high, width)] * 2 + [(lev, 56, width)] * 3 + [(SWEEPS, 16, width)]
        limit = 24 * 1024 * 1024
        near = cutoff.shape[0] // 2 + 32
        held = pl.pallas_call(
            functools.partial(kernel, sectors, bands),
            out_shape=[jax.ShapeDtypeStruct(shape, f32) for shape in made],
            in_specs=[hbm] * 8,
            out_specs=[vmem] * len(made),
            scratch_shapes=[
                tall, block, block, tall,
                *[pltpu.VMEM(a.shape, a.dtype) for a in small],
                dma((8,)),
                strips, strips, array(16 * lev, width), array(16 * sectors, width), strips, strips,
                array(sectors, width),
                pair, pair, pair, pair, four, pair, pair, four, pair, tall, array(lev * 32, width), narrow, array(SWEEPS + 1, lev, 56, width), narrow,
                *[dma] * 12,
            ],
            compiler_params=pltpu.CompilerParams(collective_id=0, has_side_effects=True, vmem_limit_bytes=limit),
        )(
            *[pltpu.with_memory_space_constraint(jnp.asarray(a), pltpu.HBM) for a in (tracer, wind_east, wind_north, kappa, *small)]
        )
        return pl.pallas_call(
            functools.partial(relax, bands),
            out_shape=[jax.ShapeDtypeStruct(tracer.shape, f32)] * 2,
            in_specs=[vmem] * len(made),
            out_specs=[hbm] * 2,
            scratch_shapes=[array(SWEEPS + 1, lev, near + 2 * PAD, width), array(SWEEPS - 1, lev, 56, width), dma((3,))],
            compiler_params=pltpu.CompilerParams(vmem_limit_bytes=limit),
        )(*[pltpu.with_memory_space_constraint(a, pltpu.VMEM) for a in held])

    spec = P(None, "lat", "lon")
    return jax.shard_map(
        per_device, mesh=mesh, in_specs=(spec, spec, spec, spec, P(), P()), out_specs=(spec, spec),
        check_vma=False,
    )
```

```python
import functools
import math

import jax
import jax.numpy as jnp
import numpy as np
from jax import lax
from jax.experimental import pallas as pl
from jax.experimental.pallas import tpu as pltpu
from jax.sharding import PartitionSpec as P

KMAX = 512
SWEEPS = 4
COURANT = 0.4
HIGHEST = lax.Precision.HIGHEST


def tables(sectors, width):
    total = sectors * width
    half = sectors // 2
    m = np.arange(width)
    theta = 2.0 * np.pi * (np.outer(np.arange(half + 1), m) % total) / total
    kept = 2 * KMAX // sectors
    k2 = np.arange(kept) - kept // 2
    phase = 2.0 * np.pi * (np.outer(m, k2) % width) / width
    c, s = np.cos(phase), np.sin(phase)
    forward = np.block([[c, -s], [s, c]])
    inverse = np.block([[c.T, s.T], [-s.T, c.T]]) / total
    return [a.astype(np.float32) for a in (np.cos(theta), np.sin(theta), forward, inverse)]


def weighted(terms):
    total = None
    for factor, value in terms:
        if abs(factor) < 1e-12:
            continue
        part = value if abs(factor - 1.0) < 1e-12 else value * np.float32(factor)
        total = part if total is None else total + part
    return total


PAD = 16
DEEP = 24
MESH = pl.DeviceIdType.MESH


def taken(x, at_lane):
    return jnp.take_along_axis(x, at_lane, axis=1, mode="promise_in_bounds")


def parts(x):
    high = x.astype(jnp.bfloat16)
    return high, (x - high.astype(jnp.float32)).astype(jnp.bfloat16)


def shift_weights(width, east, west_lane, east_lane, lanes):
    one = lax.broadcasted_iota(jnp.int32, (width, width), 0)
    two = lax.broadcasted_iota(jnp.int32, (width, width), 1)
    shift = jnp.where(one - two == 1, east, 0.0) + jnp.where(two - one == 1, 1.0, 0.0)
    spot = one & (lanes - 1)
    edge = jnp.where((two == width - 1) & (spot == east_lane), east, 0.0)
    edge = edge + jnp.where((two == 0) & (spot == west_lane), 1.0, 0.0)
    shift, edge = shift.astype(jnp.bfloat16), edge.astype(jnp.bfloat16)
    return jnp.concatenate([shift, shift, edge, edge], axis=0)


def rim(h, at16):
    high, low = parts(jnp.where((at16 == 3) | (at16 == 12), h, 0.0))
    return high.astype(jnp.float32), low.astype(jnp.float32)


def masked(here, pair):
    return [jnp.where(here, x, 0.0) for x in pair]


def west_and_east(x, edges, weights):
    high, low = parts(x)
    rims = [jnp.concatenate(tiles, axis=0).astype(jnp.bfloat16) for tiles in zip(*edges)]
    return jnp.dot(jnp.concatenate([high, low, *rims], axis=1), weights, preferred_element_type=jnp.float32)


def refined(x, weights):
    high, low = parts(x)
    return jnp.dot(jnp.concatenate([high, low, high], axis=1), weights, preferred_element_type=jnp.float32)


def kernel(
    sectors, bands,
    tracer_h, wind_east_h, wind_north_h, kappa_h, cutoff_h, partner_h, table_h, fine_h,
    stack, scaled, coupling, side, side_scaled, side_coupling, side_cross,
    tr, we, wn, ka, cutoff, partner, table, fine, load_s,
    send_a, recv_a, pole_send, pole_recv, send_d, recv_d, beyond_fix,
    rim_send, rim_recv, kap_send, kap_recv, kap_diag, adv_send, adv_recv, adv_diag, corner, invert, side_tiles, side_invert, early, early_scaled,
    a_s, a_r, b_s, b_r, d_s, d_r, x_s, x_r, k_s, k_r, f_s, f_r,
):
    lev, rows, width = we.shape
    field = stack.at[0]
    pole = cutoff.shape[1] // 2
    share = lev * pole // sectors
    slices = sectors // lev
    half = sectors // 2
    groups = rows // 8
    lat = lax.axis_index("lat")
    lon = lax.axis_index("lon")
    last = lat == bands - 1
    north = lat == 0
    polar = north | last

    def sector(offset):
        return lax.rem(lon + (offset % sectors), sectors)

    def band(offset):
        return lax.rem(lat + (offset % bands), bands)

    body = pl.ds(PAD, rows)
    held = (tracer_h, wind_east_h, wind_north_h, kappa_h, partner_h, cutoff_h, table_h, fine_h)
    near = (tr.at[:, body, :], we, wn, ka.at[:, body, :], partner, cutoff, table, fine)
    loads = [pltpu.make_async_copy(h, v, load_s.at[i]) for i, (h, v) in enumerate(zip(held, near))]
    barrier = pltpu.get_barrier_semaphore()
    for t in range(1, sectors):
        pl.semaphore_signal(barrier, inc=1, device_id=(lat, sector(t)), device_id_type=MESH)
    beside = (1,) if bands == 2 else (1, -1)
    for t in beside:
        for i in (-1, 0, 1):
            pl.semaphore_signal(barrier, inc=1, device_id=(band(t), sector(i)), device_id_type=MESH)

    for load in loads:
        load.start()

    lane = lax.broadcasted_iota(jnp.int32, (8, width), 1)
    row8 = lax.broadcasted_iota(jnp.int32, (8, width), 0)
    zero = jnp.zeros((8, width), jnp.float32)

    def roll(x, by):
        by = by % width
        return x if by == 0 else pltpu.roll(x, by, 1)

    def swapped(v0, v1):
        low = lane < width // 2
        v0, v1 = jnp.where(low, v0, roll(v1, width // 2)), jnp.where(low, roll(v0, width // 2), v1)
        out = []
        for v in (v0, v1):
            for b in (2, 1, 0):
                step, hop = 1 << b, 8 << b
                upper = (lane & hop) != 0
                same = ((row8 >> b) & 1) == ((lane >> (3 + b)) & 1)
                v = jnp.where(
                    same, v,
                    jnp.where(upper, pltpu.roll(roll(v, hop), 8 - step, 0), pltpu.roll(roll(v, -hop), step, 0)),
                )
            out.append(v)
        return out

    base = pl.multiple_of(jnp.where(last, rows - pole, 0), 8)
    tip = jnp.where(last, rows - 1, 0)
    tip_tile = pl.multiple_of(jnp.where(last, rows - 8, 0), 8)
    tip_slice = jnp.where(last, slices - 1, 0)
    keeper = lax.rem(lon, slices) == tip_slice

    @pl.when(north)
    def _():
        for l in range(lev):
            tr[l, PAD - 8 : PAD, :] = zero

    @pl.when(last)
    def _():
        for l in range(lev):
            tr[l, PAD + rows : PAD + rows + 8, :] = zero

    for load in loads[:3]:
        load.wait()
    lane_p = lax.broadcasted_iota(jnp.int32, (pole, width), 1)
    row_p = lax.broadcasted_iota(jnp.int32, (pole, width), 0)
    before = jnp.where(last, rows - pole - 1, 0)
    after = jnp.where(last, rows - 1, pole)
    eight = lane & 7
    packs = [zero, zero]
    for l in range(lev):
        x = tr[l, pl.ds(base + PAD, pole), :]
        east_wind = we[l, pl.ds(base, pole), :]
        w = jnp.where(lane_p == 0, 0.0, pltpu.roll(x, 1, 1))
        e = jnp.where(lane_p == width - 1, 0.0, pltpu.roll(x, width - 1, 1))
        above = jnp.where(last, tr[l, pl.ds(PAD + before, 1), :], 0.0)
        below = jnp.where(last, 0.0, tr[l, pl.ds(PAD + after, 1), :])
        u = jnp.where(row_p == 0, above, pltpu.roll(x, 1, 0))
        d = jnp.where(row_p == pole - 1, below, pltpu.roll(x, pole - 1, 0))
        stage = x - COURANT * 0.5 * (east_wind * (e - w) + wn[l, pl.ds(base, pole), :] * (d - u))
        for q in range(slices):
            k = l * slices + q
            send_a[k * DEEP : k * DEEP + share, :] = stage[q * share : (q + 1) * share]
            for h in range(2):
                at = q * share + 8 * h
                t = jnp.where(
                    (eight == 3) | (eight == 4), roll(x[at : at + 8], 4 + 8 * k), roll(east_wind[at : at + 8], 6 + 8 * k)
                )
                packs[h] = jnp.where((lane >> 3) == k, t, packs[h])
    for h, v in enumerate(swapped(*packs)):
        send_a[pl.ds(8 * h * DEEP + share, 8, stride=DEEP), :] = v

    def across(src, dst, count, ss, rs):
        for t in range(1, sectors):
            there = sector(t)
            pltpu.make_async_remote_copy(
                src_ref=src.at[pl.ds(pl.multiple_of(there * DEEP, 8), count), :],
                dst_ref=dst.at[pl.ds(pl.multiple_of(lon * DEEP, 8), count), :],
                send_sem=ss, recv_sem=rs, device_id=(lat, there), device_id_type=MESH,
            ).start()

    def bulk(count, sem):
        whole = send_d.at[pl.ds(0, count), :]
        return pltpu.make_async_remote_copy(
            src_ref=whole, dst_ref=whole, send_sem=sem, recv_sem=sem, device_id=(lat, sector(1)), device_id_type=MESH
        )

    def split_wait(single, double, sem, send):
        for here, count in ((polar, single), (jnp.logical_not(polar), double)):
            @pl.when(here)
            def _(count=count):
                if send:
                    bulk(count, sem).wait_send()
                else:
                    bulk(count, sem).wait_recv()

    four = lane >> 2

    def packed(tiles):
        first, second = zero, zero
        for g, x in enumerate(tiles):
            z = roll(x, 4 * g + 4)
            first = jnp.where(four == g, z, first)
            second = jnp.where(four == (g + 1) % groups, z, second)
        return first, second

    def pack_rims(source, target):
        def one(l, carry):
            at = pl.multiple_of(8 * l, 8)
            first, second = packed([source[l, PAD + 8 * g : PAD + 8 * g + 8, :] for g in range(groups)])
            target[0, pl.ds(at, 8), :] = first
            target[1, pl.ds(at, 8), :] = second
            return carry

        lax.fori_loop(0, lev, one, 0)

    def sideways(src, dst, ss, rs):
        for j in range(2):
            pltpu.make_async_remote_copy(
                src_ref=src.at[j], dst_ref=dst.at[j], send_sem=ss, recv_sem=rs,
                device_id=(lat, sector(1 - 2 * j)), device_id_type=MESH,
            ).start()

    def poleward(ref, ss, rs, send=None, recv=None):
        for i, step in enumerate((1, -1)):
            plan = [
                (
                    ref.at[:, pl.ds(PAD + rows - 8 if step == 1 else PAD, 8), :],
                    ref.at[:, pl.ds(PAD - 8 if step == 1 else PAD + rows, 8), :], 0,
                )
            ]
            if send is not None:
                plan += [(send.at[j], recv.at[2 * i + j], 1 - 2 * j) for j in range(2)]

            @pl.when(lat < bands - 1 if step == 1 else lat > 0)
            def _(step=step, plan=plan):
                for src, dst, aside in plan:
                    pltpu.make_async_remote_copy(
                        src_ref=src, dst_ref=dst, send_sem=ss, recv_sem=rs,
                        device_id=(band(step), sector(aside)), device_id_type=MESH,
                    ).start()

    unit = 8 * lev
    pack_rims(tr, rim_send)
    pl.semaphore_wait(barrier, sectors - 1 + 3 * len(beside))
    sideways(rim_send, rim_recv, x_s, x_r)
    poleward(tr, x_s, x_r)
    across(send_a, recv_a, share + 1, a_s, a_r)

    loads[3].wait()
    for l in range(lev):
        pole_send[16 * l : 16 * l + 8, :] = ka[l, pl.ds(tip_tile + PAD, 8), :]
        pole_send[16 * l + 8 : 16 * l + 9, :] = tr[l, pl.ds(tip + PAD, 1), :]
        pole_send[16 * l + 9 : 16 * l + 10, :] = wn[l, pl.ds(tip, 1), :]

    def pole_copy(l):
        return pltpu.make_async_remote_copy(
            src_ref=pole_send.at[pl.ds(16 * l, 10), :], dst_ref=pole_recv.at[pl.ds(pl.multiple_of(16 * lon, 8), 10), :],
            send_sem=b_s, recv_sem=b_r,
            device_id=(lat, l * slices + tip_slice), device_id_type=MESH,
        )

    for l in range(lev):
        @pl.when(lon != l * slices + tip_slice)
        def _(l=l):
            pole_copy(l).start()

        @pl.when(lon == l * slices + tip_slice)
        def _(l=l):
            pole_recv[pl.ds(pl.multiple_of(16 * lon, 8), 8), :] = pole_send[16 * l : 16 * l + 8, :]
            pole_recv[pl.ds(pl.multiple_of(16 * lon, 8) + 8, 2), :] = pole_send[16 * l + 8 : 16 * l + 10, :]

    pack_rims(ka, kap_send)
    sideways(kap_send, kap_recv, k_s, k_r)
    poleward(ka, k_s, k_r, kap_send, kap_diag)
    for load in loads[4:]:
        load.wait()

    start = lax.broadcasted_iota(jnp.int32, (sectors, width), 0) + half
    reach = partner[...] - jnp.where(start >= sectors, start - sectors, start) * width
    reach = jnp.where(reach < 0, reach + sectors * width, reach)
    farther = reach >= width
    at_lane = jnp.where(farther, reach - width, reach)

    def crossed(points):
        return jnp.where(
            farther, taken(pltpu.roll(points, sectors - half - 1, 0), at_lane), taken(pltpu.roll(points, half, 0), at_lane)
        )


    change = shift_weights(width, -1.0, 3, 2, 4)
    split_wait(3 * unit, 4 * unit, x_r, False)
    for l in range(lev):
        edge = jnp.where((lane & 3) == 3, rim_recv[0, 8 * l : 8 * l + 8, :], roll(rim_recv[1, 8 * l : 8 * l + 8, :], -2))
        edge = [x.astype(jnp.float32) for x in parts(edge)]
        across_west = west_and_east(
            tr[l, PAD : PAD + rows, :], [masked(four == g, edge) for g in range(groups)], change
        )
        tiles = []
        for g in range(groups):
            at = PAD + 8 * g
            x = tr[l, at : at + 8, :]
            turn = wn[l, 8 * g : 8 * g + 8, :] * (tr[l, at + 1 : at + 9, :] - tr[l, at - 1 : at + 7, :])
            push = we[l, 8 * g : 8 * g + 8, :] * across_west[8 * g : 8 * g + 8]
            value = x + COURANT * 0.5 * (push - turn)
            field[l, at : at + 8, :] = value
            k = ka[l, at : at + 8, :]
            inverse = 1.0 / (1.0 + 4.0 * k)
            invert[l, at : at + 8, :] = inverse
            coupling[l, at : at + 8, :] = k * inverse
            scaled[l, at : at + 8, :] = value * inverse
            tiles.append(value)
        first, second = packed(tiles)
        adv_send[0, 8 * l : 8 * l + 8, :] = first
        adv_send[1, 8 * l : 8 * l + 8, :] = second

    def sided(send, recv, at, put):
        for kk in range(4):
            mine = (four & 3) == kk
            near_west = jnp.where(mine, recv[0, at : at + 8, :], send[1, at : at + 8, :])
            near_east = jnp.where(mine, send[0, at : at + 8, :], recv[1, at : at + 8, :])
            put(kk, jnp.where((lane & 15) < 8, roll(near_west, -4 * kk), roll(near_east, 8 - 4 * kk)))

    sideways(adv_send, adv_recv, f_s, f_r)
    poleward(field, f_s, f_r, adv_send, adv_diag)

    beyond_fix[...] = jnp.zeros_like(beyond_fix)

    @pl.when(keeper)
    def _():
        bulk(10 * (sectors - 1), b_r).wait_recv()
        tips = jnp.concatenate([pole_recv[16 * d + 8 : 16 * d + 9, :] for d in range(sectors)], axis=0)
        winds = jnp.concatenate([pole_recv[16 * d + 9 : 16 * d + 10, :] for d in range(sectors)], axis=0)
        turned = COURANT * 0.5 * winds * crossed(tips)
        beyond_fix[...] = jnp.where(last, -turned, turned)

    first = jnp.where(last, pole, 0) + lax.rem(lon, slices) * share
    spot = lax.broadcasted_iota(jnp.int32, (share, 2 * pole), 0) + first
    limit = jnp.sum(
        jnp.where(
            lax.broadcasted_iota(jnp.int32, (share, 2 * pole), 1) == spot,
            cutoff[...].astype(jnp.float32), 0.0,
        ),
        axis=1, keepdims=True,
    )
    kept = 2 * KMAX // sectors
    slot = lax.broadcasted_iota(jnp.int32, (share, 2 * kept), 1)
    wave = sectors * (jnp.where(slot < kept, slot, slot - kept) - kept // 2)
    own = pl.multiple_of(lon * DEEP, 8)
    recv_a[pl.ds(own, share), :] = send_a[pl.ds(own, share), :]
    recv_a[pl.ds(own + share, 1), :] = send_a[pl.ds(own + share, 1), :]
    bulk((share + 1) * (sectors - 1), a_r).wait_recv()
    tw_cos, tw_sin = table[0 : half + 1, :], table[16 : half + 17, :]
    fwd = fine[: 6 * width, :]
    inv = jnp.concatenate([fine[6 * width : 9 * width, :], fine[9 * width :, :]], axis=1)

    def rows_of(ref, at):
        return [ref[pl.ds(8 * h * DEEP + at, 8, stride=DEEP), :] for h in range(2)]

    fixes = []
    for v in swapped(*rows_of(recv_a, share)):
        fixes.append(COURANT * 0.5 * v * jnp.where(eight == 6, roll(v, 11), -roll(v, -7)))
    at_tip = [(row8 == 0) & north & keeper, (row8 == 7) & last & keeper]
    ends = (lane == 0) | (lane == width - 1)
    spread = []
    for d in range(sectors):
        halves = []
        for h in range(2):
            x = recv_a[d * DEEP + 8 * h : d * DEEP + 8 * h + 8, :]
            x = x + jnp.where(ends, roll(fixes[h], -(8 * d + 6)), 0.0)
            halves.append(x + jnp.where(at_tip[h], beyond_fix[d : d + 1, :], 0.0))
        spread.append(jnp.concatenate(halves, axis=0))

    def circle(d, k):
        angle = 2.0 * math.pi * ((d * k) % sectors) / sectors
        return math.cos(angle), math.sin(angle)

    even = [spread[0]] + [spread[d] + spread[sectors - d] for d in range(1, half)] + [spread[half]]
    odd = [None] + [spread[d] - spread[sectors - d] for d in range(1, half)]
    blocks = []
    for k in range(half + 1):
        c, s = tw_cos[k : k + 1, :], tw_sin[k : k + 1, :]
        re = weighted([(circle(d, k)[0], even[d]) for d in range(half + 1)])
        im = weighted([(-circle(d, k)[1], odd[d]) for d in range(1, half)])
        if im is None:
            blocks.append(jnp.concatenate([re * c, -(re * s)], axis=1))
        else:
            blocks.append(jnp.concatenate([re * c + im * s, im * c - re * s], axis=1))
    spectrum = refined(jnp.concatenate(blocks, axis=0), fwd)
    keep = jnp.concatenate(
        [jnp.where(jnp.abs(wave + k).astype(jnp.float32) <= limit, 1.0, 0.0) for k in range(half + 1)], axis=0
    )
    back = refined(jnp.where(keep > 0.0, spectrum, 0.0), inv)
    real, imag = [], []
    for k in range(half + 1):
        c, s = tw_cos[k : k + 1, :], tw_sin[k : k + 1, :]
        zr = back[k * share : (k + 1) * share, :width]
        zi = back[k * share : (k + 1) * share, width:]
        twice = 1.0 if k in (0, half) else 2.0
        real.append((zr * c - zi * s) * twice)
        imag.append((zr * s + zi * c) * twice)
    smooth = [None] * sectors
    for d in range(half + 1):
        p = weighted([(circle(d, k)[0], real[k]) for k in range(half + 1)])
        q = weighted([(circle(d, k)[1], imag[k]) for k in range(1, half)])
        if q is None:
            smooth[d] = p
        else:
            smooth[d], smooth[sectors - d] = p - q, p + q
    edges = [zero, zero]
    for d in range(sectors):
        send_d[d * DEEP : d * DEEP + share, :] = smooth[d]
        for h in range(2):
            edges[h] = jnp.where((lane >> 3) == d, roll(smooth[d][8 * h : 8 * h + 8], 8 * d + 4), edges[h])
    beyond = [jnp.where(eight < 4, roll(v, 8), roll(v, -8)) for v in edges]
    for i in range(2):
        west, east = (beyond, edges) if i == 0 else (edges, beyond)
        for h, v in enumerate(swapped(*[jnp.where(eight < 4, w, e) for w, e in zip(west, east)])):
            send_d[pl.ds(8 * h * DEEP + share + i, 8, stride=DEEP), :] = v

    extra = share + 2 + SWEEPS + 1

    def put_cross(t, rows16):
        for h in range(2):
            send_d[pl.ds(8 * h * DEEP + share + 2 + t, 8, stride=DEEP), :] = rows16[8 * h : 8 * h + 8]

    @pl.when(keeper)
    def _():
        now, inverse, pull = [], [], []
        for d in range(sectors):
            top, low = d * DEEP, d * DEEP + 8
            now.append(jnp.where(last, send_d[low : low + 8, :], send_d[top : top + 8, :]))
            k = pole_recv[16 * d : 16 * d + 8, :]
            inverse.append(1.0 / (1.0 + 4.0 * k))
            pull.append(k * inverse[d])
        source = [a * b for a, b in zip(now, inverse)]
        ends = jnp.zeros((sectors, width), jnp.float32)
        wide = lax.broadcasted_iota(jnp.int32, (sectors, width), 1)
        for t in range(SWEEPS):
            tips = jnp.concatenate([jnp.where(last, x[7:8], x[0:1]) for x in now], axis=0)
            over = crossed(tips)
            put_cross(t, over)
            z = roll(over, 8 * t + 4)
            z = jnp.where((wide & 7) < 4, pltpu.roll(z, 1, 0), pltpu.roll(z, sectors - 1, 0))
            ends = jnp.where((wide >> 3) == t, z, ends)
            if t < SWEEPS - 1:
                right, left = [roll(x, 1) for x in now], [roll(x, -1) for x in now]
                later = []
                for d in range(sectors):
                    w = jnp.where(lane == 0, right[d - 1], right[d])
                    e = jnp.where(lane == width - 1, left[(d + 1) % sectors], left[d])
                    u = jnp.where((row8 == 0) & jnp.logical_not(last), over[d : d + 1], pltpu.roll(now[d], 1, 0))
                    b = jnp.where((row8 == 7) & last, over[d : d + 1], pltpu.roll(now[d], 7, 0))
                    later.append(source[d] + pull[d] * (w + e + u + b))
                now = later
        put_cross(SWEEPS, ends)
        across(send_d, recv_d, extra, d_s, d_r)

    @pl.when(jnp.logical_not(keeper))
    def _():
        across(send_d, recv_d, share + 2, d_s, d_r)

    recv_d[pl.ds(own, share), :] = send_d[pl.ds(own, share), :]
    recv_d[pl.ds(own + share, 2), :] = send_d[pl.ds(own + share, 2), :]

    @pl.when(keeper)
    def _():
        recv_d[pl.ds(own + share + 2, SWEEPS + 1), :] = send_d[pl.ds(own + share + 2, SWEEPS + 1), :]

    split_wait(5 * unit, 8 * unit, k_r, False)

    def corners(ref, diag, l):
        top, bottom = ref[l, PAD - 8 : PAD, :], ref[l, PAD + rows : PAD + rows + 8, :]
        nw, ne, sw, se = [diag[i, 8 * l : 8 * l + 8, :] for i in range(4)]
        first = jnp.where(
            lane < 8, roll(jnp.where(lane >= width - 4, nw, top), 4), roll(jnp.where(lane < 4, ne, top), 12)
        )
        second = jnp.where(
            lane < width - 8,
            jnp.where(lane < width - 12, roll(sw, -16), roll(bottom, -12)),
            jnp.where(lane < width - 4, roll(bottom, -4), roll(se, -8)),
        )
        return first, second

    def capped(first_tile, last_tile, first, second):
        return jnp.where(lane < 16, first, roll(last_tile, 16)), jnp.where(lane >= width - 16, second, roll(first_tile, -16))

    for l in range(lev):
        tiles = []

        def put(kk, tile, l=l, tiles=tiles):
            side_invert[l, 12 + 8 * kk : 20 + 8 * kk, :] = tile
            tiles.append(tile)

        sided(kap_send, kap_recv, 8 * l, put)
        top, bottom = capped(tiles[0], tiles[3], *corners(ka, kap_diag, l))
        side_invert[l, 4:12, :] = top
        side_invert[l, 44:52, :] = bottom
        for j in range(5):
            at = 8 + 8 * j
            k = side_invert[l, at : at + 8, :]
            inverse = 1.0 / (1.0 + 4.0 * k)
            side_invert[l, at : at + 8, :] = inverse
            side_coupling[l, at : at + 8, :] = k * inverse
    split_wait(5 * unit, 8 * unit, f_r, False)
    for l in range(lev):
        for at in (PAD - 8, PAD + rows):
            k = ka[l, at : at + 8, :]
            inverse = 1.0 / (1.0 + 4.0 * k)
            coupling[l, at : at + 8, :] = k * inverse
            scaled[l, at : at + 8, :] = field[l, at : at + 8, :] * inverse

        def put(kk, tile, l=l):
            side_tiles[32 * l + 8 * kk : 32 * l + 8 * kk + 8, :] = tile

        sided(adv_send, adv_recv, 8 * l, put)
        corner[0, 8 * l : 8 * l + 8, :], corner[1, 8 * l : 8 * l + 8, :] = corners(field, adv_diag, l)
        at = 32 * l
        early[0, l, 12:44, :] = side_tiles[at : at + 32, :]
        early[0, l, 4:12, :], early[0, l, 44:52, :] = capped(
            side_tiles[at : at + 8, :], side_tiles[at + 24 : at + 32, :],
            corner[0, 8 * l : 8 * l + 8, :], corner[1, 8 * l : 8 * l + 8, :],
        )
        early_scaled[l, 8:48, :] = early[0, l, 8:48, :] * side_invert[l, 8:48, :]

    weights = shift_weights(width, 1.0, 3, 12, 16)
    order = [(0, -1)] + [(i // 4, i % 4) for i in range(groups)] + [(groups // 4 - 1, 4)]
    at16 = lane & 15

    def sweep_early(t, carry):
        for l in range(lev):
            ends = {kk: rim(early[t, l, 12 + 8 * kk : 20 + 8 * kk, :], at16) for kk in range(-1, 5)}
            total = west_and_east(
                stack[t, l, PAD - 8 : PAD + rows + 8, :],
                [masked((lane >> 4) == g, ends[kk]) for g, kk in order], weights,
            )
            for i in range(groups + 2):
                at = PAD - 8 + 8 * i
                value = total[8 * i : 8 * i + 8] + (stack[t, l, at - 1 : at + 7, :] + stack[t, l, at + 1 : at + 9, :])
                stack[t + 1, l, at : at + 8, :] = scaled[l, at : at + 8, :] + coupling[l, at : at + 8, :] * value
            for j in range(5):
                at = 8 + 8 * j
                x = early[t, l, at : at + 8, :]
                value = roll(x, 1) + roll(x, -1) + early[t, l, at - 1 : at + 7, :] + early[t, l, at + 1 : at + 9, :]
                early[t + 1, l, at : at + 8, :] = (
                    early_scaled[l, at : at + 8, :] + side_coupling[l, at : at + 8, :] * value
                )
        return carry

    lax.fori_loop(0, SWEEPS, sweep_early, 0)

    plain_rows, more = (share + 2) * (sectors - 1), SWEEPS + 1
    d_waits = ((keeper, plain_rows + more * (lev - 1)), (jnp.logical_not(keeper), plain_rows + more * lev))
    for here, count in d_waits:
        @pl.when(here)
        def _(count=count):
            bulk(count, d_r).wait_recv()

    def cross(l, t):
        return recv_d[pl.ds((l * slices + tip_slice) * DEEP + share + 2 + t, 1), :]

    @pl.when(polar)
    def _():
        for k in range(sectors):
            l, q = k // slices, k % slices
            x = recv_d[k * DEEP : k * DEEP + share, :]
            at = base + PAD + q * share
            field[l, pl.ds(at, share), :] = x
            scaled[l, pl.ds(at, share), :] = x * invert[l, pl.ds(at, share), :]

    @pl.when(north)
    def _():
        for l in range(lev):
            field[l, PAD - 1 : PAD, :] = cross(l, 0)

    @pl.when(last)
    def _():
        for l in range(lev):
            field[l, PAD + rows : PAD + rows + 1, :] = cross(l, 0)

    halo = jnp.concatenate([cross(l, SWEEPS) for l in range(lev)] * 2, axis=0)
    for t in range(SWEEPS):
        plain = jnp.concatenate([cross(l, t) for l in range(lev)] * 2, axis=0)
        z = jnp.where(
            lane < 8,
            jnp.where(lane < 4, roll(halo, -8 * t), roll(plain, 4)),
            jnp.where(lane < 12, roll(plain, 12), roll(halo, 8 - 8 * t)),
        )
        side_cross[t, :8, :] = jnp.where(last, roll(z, -16), z)
        side_cross[t, 8:, :] = plain

    strips = [
        [jnp.where(last, roll(v, -32), v) for v in swapped(*rows_of(recv_d, share + i))] for i in range(2)
    ]
    from_cap = jnp.where(last, lane - (width - 32), lane)
    inside_cap = polar & (from_cap >= 0) & (from_cap < 32)
    top_spot = north & (row8 == 7) & (lane < 16)
    bottom_spot = last & (row8 == 0) & (lane >= width - 16)
    for l in range(lev):
        tiles = []
        for kk in range(4):
            h, by = kk % 2, -32 * l - 8 * (kk // 2)
            z = jnp.where((lane & 15) < 8, roll(strips[0][h], by), roll(strips[1][h], by + 8))
            tile = jnp.where(inside_cap, z, side_tiles[32 * l + 8 * kk : 32 * l + 8 * kk + 8, :])
            side[l, 12 + 8 * kk : 20 + 8 * kk, :] = tile
            tiles.append(tile)
        at = 8 * l
        top, bottom = capped(tiles[0], tiles[3], corner[0, at : at + 8, :], corner[1, at : at + 8, :])
        side[l, 4:12, :] = jnp.where(top_spot, side_cross[0, l : l + 1, :], top)
        side[l, 44:52, :] = jnp.where(bottom_spot, side_cross[0, l : l + 1, :], bottom)
        for j in range(5):
            at = 8 + 8 * j
            side_scaled[l, at : at + 8, :] = side[l, at : at + 8, :] * side_invert[l, at : at + 8, :]

    bulk((share + 1) * (sectors - 1), a_s).wait_send()
    split_wait(3 * unit, 4 * unit, x_s, True)
    split_wait(5 * unit, 8 * unit, k_s, True)
    split_wait(5 * unit, 8 * unit, f_s, True)
    for here, pole_rows, rows_out in (
        (keeper, 10 * (lev - 1), extra * (sectors - 1)), (jnp.logical_not(keeper), 10 * lev, plain_rows)
    ):
        @pl.when(here)
        def _(pole_rows=pole_rows, rows_out=rows_out):
            bulk(pole_rows, b_s).wait_send()
            bulk(rows_out, d_s).wait_send()


def relax(
    bands, stack, scaled, coupling, side0, side_scaled, side_coupling, side_cross, filtered, balanced, local, side, sems
):
    lev, rows, width = filtered.shape
    near = local.shape[2] - 2 * PAD
    tiles = near // 8 + 1
    lat = lax.axis_index("lat")
    north, last = lat == 0, lat == bands - 1
    base = pl.multiple_of(jnp.where(last, rows - near, 0), 8)
    rest = pl.multiple_of(jnp.where(last, 0, near), 8)
    copies = [
        pltpu.make_async_copy(stack.at[0, :, pl.ds(PAD, rows), :], filtered, sems.at[0]),
        pltpu.make_async_copy(
            stack.at[SWEEPS, :, pl.ds(rest + PAD, rows - near), :], balanced.at[:, pl.ds(rest, rows - near), :], sems.at[1]
        ),
    ]
    for copy in copies:
        copy.start()
    lane = lax.broadcasted_iota(jnp.int32, (8, width), 1)
    row8 = lax.broadcasted_iota(jnp.int32, (8, width), 0)
    at16 = lane & 15
    group = (lane >> 4) - jnp.where(last, (rows - near) // 32, 0)
    weights = shift_weights(width, 1.0, 3, 12, 16)
    for l in range(lev):
        local[0, l, PAD - 8 : PAD + near + 8, :] = stack[0, l, pl.ds(base + PAD - 8, near + 16), :]
    for t in range(SWEEPS):
        beside = side0 if t == 0 else side.at[t - 1]
        edges = []
        for l in range(lev):
            ends = {kk: rim(beside[l, 12 + 8 * kk : 20 + 8 * kk, :], at16) for kk in range(-1, 4)}
            edges.append(masked(lane < 16, ends[-1]))
            for i in range(near // 8):
                edges.append(masked(group == i // 4, ends[i % 4]))
        whole = jnp.concatenate([local[t, l, PAD - 8 : PAD + near, :] for l in range(lev)], axis=0)
        total = west_and_east(whole, edges, weights)
        for l in range(lev):
            for i in range(tiles):
                at = PAD - 8 + 8 * i
                start = 8 * (tiles * l + i)
                value = total[start : start + 8] + (local[t, l, at - 1 : at + 7, :] + local[t, l, at + 1 : at + 9, :])
                there = pl.ds(base + at, 8)
                value = scaled[l, there, :] + coupling[l, there, :] * value
                if t < SWEEPS - 1 and i == 0:
                    cross = side_cross[t + 1, 8 + l : 9 + l, :]
                    at_end = rows - near + PAD - 8
                    value = jnp.where(north & (row8 == 7), cross, value)
                    value = jnp.where(last, stack[t + 1, l, at_end : at_end + 8, :], value)
                    at_end = near + PAD
                    local[t + 1, l, at_end : at_end + 8, :] = jnp.where(
                        last, jnp.broadcast_to(cross, (8, width)), stack[t + 1, l, at_end : at_end + 8, :]
                    )
                local[t + 1, l, at : at + 8, :] = value
        if t == SWEEPS - 1:
            break
        for l in range(lev):
            for j in range(5):
                at = 8 + 8 * j
                x = beside[l, at : at + 8, :]
                value = pltpu.roll(x, 1, 1) + pltpu.roll(x, width - 1, 1)
                value = value + (beside[l, at - 1 : at + 7, :] + beside[l, at + 1 : at + 9, :])
                x = side_scaled[l, at : at + 8, :] + side_coupling[l, at : at + 8, :] * value
                cross = side_cross[t + 1, l : l + 1, :]
                if j == 0:
                    x = jnp.where(north & (row8 == 3) & (lane < 16), cross, x)
                if j == 4:
                    x = jnp.where(last & (row8 == 4) & (lane >= width - 16), cross, x)
                side[t, l, at : at + 8, :] = x
    copy = pltpu.make_async_copy(
        local.at[SWEEPS, :, pl.ds(PAD, near), :], balanced.at[:, pl.ds(base, near), :], sems.at[2]
    )
    copy.start()
    for copy in (*copies, copy):
        copy.wait()


def solution(mesh):
    sectors, bands = mesh.shape["lon"], mesh.shape["lat"]

    def per_device(tracer, wind_east, wind_north, kappa, cutoff, partner):
        lev, rows, width = tracer.shape
        f32 = jnp.float32
        high = rows + 2 * PAD

        def array(*shape):
            return pltpu.VMEM(shape, f32)

        block, tall = array(lev, rows, width), array(lev, high, width)
        strips = array(sectors * DEEP, width)
        pair, four = array(2, lev * 8, width), array(4, lev * 8, width)
        narrow = array(lev, 56, width)
        vmem = pl.BlockSpec(memory_space=pltpu.VMEM)
        hbm = pl.BlockSpec(memory_space=pltpu.HBM)
        tw_cos, tw_sin, fwd, inv = tables(sectors, width)
        blank = np.zeros((16 - tw_cos.shape[0], width), np.float32)
        table = np.concatenate([tw_cos, blank, tw_sin, blank], axis=0)
        fine = []
        for whole in (fwd, inv[:, :width], inv[:, width:]):
            first = whole.astype(jnp.bfloat16)
            fine += [first, first, (whole - first.astype(np.float32)).astype(jnp.bfloat16)]
        fine = np.concatenate(fine, axis=0)
        small = (cutoff.reshape(1, -1), partner.reshape(sectors, width), table, fine)
        dma = pltpu.SemaphoreType.DMA
        made = [(SWEEPS + 1, lev, high, width)] + [(lev, high, width)] * 2 + [(lev, 56, width)] * 3 + [(SWEEPS, 16, width)]
        limit = 24 * 1024 * 1024
        near = cutoff.shape[0] // 2 + 32
        held = pl.pallas_call(
            functools.partial(kernel, sectors, bands),
            out_shape=[jax.ShapeDtypeStruct(shape, f32) for shape in made],
            in_specs=[hbm] * 8,
            out_specs=[vmem] * len(made),
            scratch_shapes=[
                tall, block, block, tall,
                *[pltpu.VMEM(a.shape, a.dtype) for a in small],
                dma((8,)),
                strips, strips, array(16 * lev, width), array(16 * sectors, width), strips, strips,
                array(sectors, width),
                pair, pair, pair, pair, four, pair, pair, four, pair, tall, array(lev * 32, width), narrow, array(SWEEPS + 1, lev, 56, width), narrow,
                *[dma] * 12,
            ],
            compiler_params=pltpu.CompilerParams(collective_id=0, has_side_effects=True, vmem_limit_bytes=limit),
        )(
            *[pltpu.with_memory_space_constraint(jnp.asarray(a), pltpu.HBM) for a in (tracer, wind_east, wind_north, kappa, *small)]
        )
        return pl.pallas_call(
            functools.partial(relax, bands),
            out_shape=[jax.ShapeDtypeStruct(tracer.shape, f32)] * 2,
            in_specs=[vmem] * len(made),
            out_specs=[hbm] * 2,
            scratch_shapes=[array(SWEEPS + 1, lev, near + 2 * PAD, width), array(SWEEPS - 1, lev, 56, width), dma((3,))],
            compiler_params=pltpu.CompilerParams(vmem_limit_bytes=limit),
        )(*[pltpu.with_memory_space_constraint(a, pltpu.VMEM) for a in held])

    spec = P(None, "lat", "lon")
    return jax.shard_map(
        per_device, mesh=mesh, in_specs=(spec, spec, spec, spec, P(), P()), out_specs=(spec, spec),
        check_vma=False,
    )
```
